128 devices in a mesh: seq: 32 (over y, z, core), ch: 4 (over x).
Axes of the slice: x: 4, y: 4, z: 4, core: 2. Of those that a mesh axis runs over, the one named last changes fastest.
Arguments:
- block_input: bfloat16 [16384, 1024], P('seq', 'ch'), may hold values from -36 to 36
- segment_ids: int32 [16384], P('seq'), may hold values from 0 to 1, as said below
- norm1_gain: float32 [1024], replicated, may hold values from 0.25 to 1.75
- in_weight: bfloat16 [1024, 3, 1024], P(None, None, 'ch'), may hold values from -0.1875 to 0.1875
- conv_weight: float32 [3, 1024], P(None, 'ch'), may hold values from -3 to 3
- out_weight: bfloat16 [1024, 1024], P(None, 'ch'), may hold values from -0.1875 to 0.1875
- norm2_gain: float32 [1024], replicated, may hold values from 0.25 to 1.75
- ffn_in_weight: bfloat16 [1024, 2, 4608], P(None, None, 'ch'), may hold values from -0.1875 to 0.1875
- ffn_out_weight: bfloat16 [1024, 4608], P(None, 'ch'), may hold values from -0.125 to 0.125
- out_grad: bfloat16 [16384, 1024], P('seq', 'ch'), may hold values from -6 to 6
Outputs:
- block_output: bfloat16 [16384, 1024], P('seq', 'ch')
- input_grad: bfloat16 [16384, 1024], P('seq', 'ch')
- grad_norm1_gain: float32 [1024], P('ch')
- grad_in_weight: float32 [1024, 3, 1024], P('seq', None, 'ch')
- grad_conv_weight: float32 [3, 1024], P(None, 'ch')
- grad_out_weight: float32 [1024, 1024], P('seq', 'ch')
- grad_norm2_gain: float32 [1024], P('ch')
- grad_ffn_in_weight: float32 [1024, 2, 4608], P('seq', None, 'ch')
- grad_ffn_out_weight: float32 [1024, 4608], P('seq', 'ch')
The draws below stay inside these ranges and needn't reach their ends.
Inputs may be any that keep to these rules, and one draw needn't show every extreme that they name: `segment_ids`: two sequences: ids are 0 before a position b and 1 from b on, with 1024 <= b <= 15360 and b % 512 >= 3.
All inputs are finite; a program needn't handle non-finite values.
Results may differ from the reference program's by a relative error of at most 0.0099.
Values may be sent and summed in bfloat16 or wider, within the bound.
No kernel may reach another device: no remote copies, remote signals or barrier semaphores. Data moves between devices by JAX's collectives and lax.ppermute only.
A program may use at most 128 MiB of HBM per device.

```python
import math
import jax
import jax.numpy as jnp
from jax import lax

D = 1024
FF = 4608
MINLEN = 1024
ROWS = 512
TOKENS = 16384


def draw_block_input(key, part):
    key = jax.random.fold_in(key, 5)
    noise_key, row_key = jax.random.split(key)
    column = jnp.arange(D, dtype=jnp.float32) / (D - 1)
    row_scale = jnp.exp(jax.random.uniform(row_key, (TOKENS, 1), jnp.float32, math.log(0.3), math.log(3.0)))
    noise_draw = jnp.clip(jax.random.normal(noise_key, (TOKENS, D), jnp.float32), -4.0, 4.0)
    column_scale = 0.3 * jnp.power(10.0, column)
    return (noise_draw * column_scale[None, :] * row_scale).astype(jnp.bfloat16)


def draw_segment_ids(key, part):
    key = jax.random.fold_in(key, 11)
    boundary = jax.random.randint(key, (), MINLEN + 3, TOKENS - MINLEN - 2, dtype=jnp.int32)
    boundary = jnp.where(boundary % ROWS < 3, boundary + 3, boundary)
    position = jnp.arange(TOKENS, dtype=jnp.int32)
    return (position >= boundary).astype(jnp.int32)


def level_of(key, extent, cuts, low, top_value):
    gain = 1.0
    for dim, blocks in cuts:
        heights = jax.random.uniform(jax.random.fold_in(jax.random.fold_in(key, 6), dim), (blocks,), jnp.float32, low / len(cuts), top_value / len(cuts))
        gain = gain * jnp.repeat(jnp.exp(heights), extent[dim] // blocks).reshape((-1,) + (1,) * (len(extent) - 1 - dim))
    return gain


def bell_draw(rng, extent, deviation, limit, shards=(), kind=jnp.bfloat16):
    entries = deviation * jax.random.normal(rng, extent, jnp.float32)
    if shards:
        entries = entries * level_of(rng, extent, shards, -0.22, 0.18)
    return jnp.clip(entries, -limit, limit).astype(kind)


def setup_inputs(seed: int = 0) -> dict:
    key_list = jax.random.split(jax.random.key(seed), 11)
    return {
        "block_input": draw_block_input(jax.random.fold_in(key_list[10], 71), 0),
        "segment_ids": draw_segment_ids(jax.random.fold_in(key_list[10], 71), 0),
        "norm1_gain": jnp.clip(1.0 + 0.15 * jax.random.normal(key_list[2], (D,), jnp.float32), 0.25, 1.75),
        "in_weight": bell_draw(key_list[3], (D, 3, D), D ** -0.5, 0.1875, ((2, 4),)),
        "conv_weight": bell_draw(key_list[4], (3, D), 0.6, 3.0, ((1, 4),), jnp.float32),
        "out_weight": bell_draw(key_list[5], (D, D), D ** -0.5, 0.1875, ((1, 4),)),
        "norm2_gain": jnp.clip(1.0 + 0.15 * jax.random.normal(key_list[6], (D,), jnp.float32), 0.25, 1.75),
        "ffn_in_weight": bell_draw(key_list[7], (D, 2, FF), D ** -0.5, 0.1875, ((2, 4),)),
        "ffn_out_weight": bell_draw(key_list[8], (D, FF), (FF // 2) ** -0.5, 0.125, ((1, 4),)),
        "out_grad": bell_draw(key_list[9], (TOKENS, D), 1.0, 6.0, ((0, 32), (1, 4))),
    }


EPS = 1e-05
HIGH = lax.Precision.HIGHEST

@jax.custom_vjp
def low(v):
    return lax.optimization_barrier(v.astype(jnp.bfloat16)).astype(jnp.float32)

@jax.custom_vjp
def low_back(v):
    return v

def low_keep(v):
    return (low(v), None)

def low_pass(kept, grad):
    return (grad,)

def back_keep(v):
    return (v, None)

def back_low(kept, grad):
    return (low(grad),)
low.defvjp(low_keep, low_pass)
low_back.defvjp(back_keep, back_low)

def shifted(values, steps):
    padding = jnp.zeros((steps, values.shape[1]), jnp.float32)
    return jnp.concatenate([padding, values[:-steps]], axis=0)

def forward(input_rows, gain_one, in_proj, conv_taps, out_proj, gain_two, ffn_in, ffn_out, same_one, same_two):
    r_one = lax.rsqrt(lax.optimization_barrier(jnp.mean(input_rows * input_rows, axis=1, keepdims=True)) + EPS)
    normed_one = low(input_rows * r_one * gain_one)
    projected = low_back(jnp.einsum('td,dkc->tkc', normed_one, in_proj, precision=HIGH))
    gated_rows = low(projected[:, 0] * projected[:, 2])
    conv_out = conv_taps[0] * gated_rows + conv_taps[1] * same_one * shifted(gated_rows, 1) + conv_taps[2] * same_two * shifted(gated_rows, 2)
    mixed_rows = low(projected[:, 1] * conv_out)
    branch = low_back(jnp.dot(mixed_rows, out_proj.T, precision=HIGH, preferred_element_type=jnp.float32))
    hidden = input_rows + branch
    r_two = lax.rsqrt(lax.optimization_barrier(jnp.mean(hidden * hidden, axis=1, keepdims=True)) + EPS)
    normed_two = low(hidden * r_two * gain_two)
    gate_up = low_back(jnp.einsum('td,dkf->tkf', normed_two, ffn_in, precision=HIGH))
    act_rows = low(jax.nn.silu(gate_up[:, 0]) * gate_up[:, 1])
    down = low_back(jnp.dot(act_rows, ffn_out.T, precision=HIGH, preferred_element_type=jnp.float32))
    return hidden + down

def reference(block_input, segment_ids, norm1_gain, in_weight, conv_weight, out_weight, norm2_gain, ffn_in_weight, ffn_out_weight, out_grad):
    position = jnp.arange(TOKENS, dtype=jnp.int32)
    prev_one = jnp.concatenate([segment_ids[:1], segment_ids[:-1]])
    prev_two = jnp.concatenate([segment_ids[:2], segment_ids[:-2]])
    same_one = ((segment_ids == prev_one) & (position >= 1)).astype(jnp.float32)[:, None]
    same_two = ((segment_ids == prev_two) & (position >= 2)).astype(jnp.float32)[:, None]

    def run(input_rows, gain_one, in_proj, conv_taps, out_proj, gain_two, ffn_in, ffn_out):
        return forward(input_rows, gain_one, in_proj, conv_taps, out_proj, gain_two, ffn_in, ffn_out, same_one, same_two)
    result, pullback = jax.vjp(run, block_input.astype(jnp.float32), norm1_gain, in_weight.astype(jnp.float32), conv_weight, out_weight.astype(jnp.float32), norm2_gain, ffn_in_weight.astype(jnp.float32), ffn_out_weight.astype(jnp.float32))
    grads = pullback(out_grad.astype(jnp.float32))
    return (result.astype(jnp.bfloat16), grads[0].astype(jnp.bfloat16), grads[1], grads[2], grads[3], grads[4], grads[5], grads[6], grads[7])
```

```python
import jax
import jax.numpy as jnp
from jax import lax
from jax.sharding import PartitionSpec as P

EPS = 1e-05
F32 = jnp.float32
BF16 = jnp.bfloat16
CH = 4


def seq_index(y, z, core):
    return ((y % 4) * 4 + z % 4) * 2 + core


def seq_pairs(dy, dz, dcore):
    return [
        (seq_index(y, z, core), seq_index(y + dy, z + dz, core ^ dcore))
        for y in range(4)
        for z in range(4)
        for core in range(2)
    ]


def ch_pairs(step):
    return [(i, (i + step) % CH) for i in range(CH)]


def gather_ch(block):
    return [block] + [lax.ppermute(block, "ch", ch_pairs(-j)) for j in range(1, CH)]


def scatter_ch(chunks):
    total = chunks[0]
    for j in range(1, CH):
        total = total + lax.ppermute(chunks[j].astype(BF16), "ch", ch_pairs(j)).astype(F32)
    return total


def sum_ch(vector):
    total = vector
    for j in range(1, CH):
        total = total + lax.ppermute(vector, "ch", ch_pairs(j))
    return total


def pick(array, index, axis):
    return lax.dynamic_index_in_dim(array, index, axis, keepdims=False)


def from_behind(array, axis, by):
    size = lax.axis_size(axis)
    pairs = [(i, i + by) for i in range(size) if 0 <= i + by < size]
    return lax.ppermute(array, axis, pairs)


def tap_masks(segment_ids):
    padded = jnp.concatenate([segment_ids[:1], segment_ids[:1], segment_ids])
    same_one = (padded[2:] == padded[1:-1]).astype(F32)[:, None]
    same_two = (padded[2:] == padded[:-2]).astype(F32)[:, None]
    return (same_one, same_two)


def core_reduce(grads, rolled, x, core):
    def parity(grad, roll, which):
        blocks = grad.reshape(4, 4, 2, 32, grad.shape[1])
        if not roll:
            return pick(blocks, which, 2)
        return jnp.stack([pick(pick(blocks, (y - x) % 4, 0), which, 1) for y in range(4)], axis=0)

    give = jnp.concatenate([parity(g, r, 1 - core) for g, r in zip(grads, rolled)], axis=-1)
    got = lax.ppermute(give, "seq", seq_pairs(0, 0, 1))
    keep = jnp.concatenate([parity(g, r, core) for g, r in zip(grads, rolled)], axis=-1)
    return keep, got


def reduce_axis(array, axis, me, along_y):
    total = pick(array, me, axis).astype(F32)
    for step in (1, 3, 2):
        pairs = seq_pairs(step, 0, 0) if along_y else seq_pairs(0, step, 0)
        total = total + lax.ppermute(pick(array, (me + step) % 4, axis), "seq", pairs).astype(F32)
    return total


def shards(
    block_input,
    segment_ids,
    norm1_gain,
    in_weight,
    conv_weight,
    out_weight,
    norm2_gain,
    ffn_in_weight,
    ffn_out_weight,
    out_grad,
):
    x = lax.axis_index("ch")
    seq = lax.axis_index("seq")
    core, z, y = seq % 2, (seq // 2) % 4, seq // 8
    features = norm1_gain.shape[0]
    width = block_input.shape[1]
    hidden_units = ffn_out_weight.shape[1]

    def rolled(array):
        blocks = array.reshape((CH, width) + array.shape[1:])
        return jnp.concatenate([pick(blocks, (x + j) % CH, 0) for j in range(CH)], axis=0)

    gain_one = rolled(norm1_gain)
    gain_two = rolled(norm2_gain)
    own_one, own_two = gain_one[:width], gain_two[:width]

    pieces = gather_ch(block_input)
    half_rows = out_weight.shape[0] // 2
    half = lax.dynamic_slice_in_dim(out_weight, core * half_rows, half_rows, 0)
    half_full = jnp.concatenate(gather_ch(half), axis=1)
    other_half = lax.ppermute(half_full, "seq", seq_pairs(0, 0, 1))
    out_full = jnp.stack([half_full, other_half], axis=0)
    out_full = jnp.concatenate([pick(out_full, core, 0), pick(out_full, 1 - core, 0)], axis=0)
    out_full = lax.optimization_barrier(rolled(out_full))
    in_rolled = lax.optimization_barrier(rolled(in_weight))
    ffn_rolled = rolled(ffn_in_weight)
    ffn_cat = lax.optimization_barrier(
        jnp.concatenate([ffn_rolled[:, 0], ffn_rolled[:, 1]], axis=1)
    )

    full_rows = jnp.concatenate(pieces, axis=1).astype(F32)
    own_rows = block_input.astype(F32)
    r_one = lax.rsqrt(jnp.mean(full_rows * full_rows, axis=1, keepdims=True) + EPS)
    normed_one = (full_rows * r_one * gain_one).astype(BF16)
    projected = jnp.einsum("td,dkc->tkc", normed_one, in_rolled, preferred_element_type=F32)
    b_gate, c_gate, value_rows = projected[:, 0], projected[:, 1], projected[:, 2]
    gated_rows = (b_gate * value_rows).astype(BF16)
    carried = from_behind(gated_rows[-2:], "seq", 1)
    grad_full = lax.all_gather(out_grad, "ch", axis=1, tiled=True)
    extended = jnp.concatenate([carried, gated_rows], axis=0).astype(F32)
    same_one, same_two = tap_masks(segment_ids)
    current = extended[2:]
    prior_one = extended[1:-1] * same_one
    prior_two = extended[:-2] * same_two
    conv_out = conv_weight[0] * current + conv_weight[1] * prior_one + conv_weight[2] * prior_two
    mixed_rows = (c_gate * conv_out).astype(BF16)

    mixed_full = jnp.concatenate(gather_ch(mixed_rows), axis=1)
    hidden = full_rows + jnp.einsum(
        "tc,ec->te", mixed_full, out_full, preferred_element_type=F32
    )
    r_two = lax.rsqrt(jnp.mean(hidden * hidden, axis=1, keepdims=True) + EPS)
    normed_two = (hidden * r_two * gain_two).astype(BF16)
    gate_up = jnp.dot(normed_two, ffn_cat, preferred_element_type=F32)
    gate_rows, up_rows = gate_up[:, :hidden_units], gate_up[:, hidden_units:]
    sigma = jax.nn.sigmoid(gate_rows)
    swish = gate_rows * sigma
    act_rows = (swish * up_rows).astype(BF16)
    d_act = jnp.einsum("te,ef->tf", grad_full, ffn_out_weight, preferred_element_type=F32)
    d_gate = d_act * up_rows * sigma * (1.0 + gate_rows * (1.0 - sigma))
    d_up = d_act * swish
    d_gate_up = jnp.concatenate([d_gate, d_up], axis=1).astype(BF16)
    d_normed_two = jnp.einsum("tf,df->td", d_gate_up, ffn_cat, preferred_element_type=F32)
    chunks = [d_normed_two[:, j * width : (j + 1) * width] for j in range(CH)]
    d_normed_own = scatter_ch(chunks)
    inner_two = sum_ch(jnp.sum(gain_two * d_normed_two * hidden, axis=1))[:, None]

    down_terms = jnp.einsum(
        "tf,ef->te", act_rows, ffn_out_weight, preferred_element_type=F32
    ).astype(BF16)
    down = lax.psum_scatter(down_terms, "ch", scatter_dimension=1, tiled=True)
    hidden_own = hidden[:, :width]
    block_output = (hidden_own + down.astype(F32)).astype(BF16)

    grad_ffn_out = jnp.einsum(
        "te,tf->ef", grad_full, act_rows, preferred_element_type=F32
    ).astype(BF16)
    grad_ffn_in = jnp.einsum(
        "td,tf->df", normed_two, d_gate_up, preferred_element_type=F32
    ).astype(BF16)
    keep, got = core_reduce([grad_ffn_in, grad_ffn_out], [True, False], x, core)
    ffn_sum = (keep.astype(F32) + got.astype(F32)).astype(BF16)
    cut = hidden_units * 2 + 640
    part_p = jnp.concatenate(
        [ffn_sum[..., :hidden_units], ffn_sum[..., 2 * hidden_units : cut]], axis=-1
    )
    part_q = jnp.concatenate(
        [ffn_sum[..., hidden_units : 2 * hidden_units], ffn_sum[..., cut:]], axis=-1
    )
    part_p = reduce_axis(part_p, 1, z, False).astype(BF16)
    part_q = reduce_axis(part_q, 0, y, True).astype(BF16)
    part_p = reduce_axis(part_p, 0, y, True)
    part_q = reduce_axis(part_q, 0, z, False)
    grad_ffn_in = jnp.stack([part_p[:, :hidden_units], part_q[:, :hidden_units]], axis=1)
    grad_ffn_out = jnp.concatenate([part_p[:, hidden_units:], part_q[:, hidden_units:]], axis=1)

    grad_gain_two = jnp.sum(d_normed_own * hidden_own * r_two, axis=0)
    d_hidden = (
        out_grad.astype(F32)
        + r_two * own_two * d_normed_own
        - hidden_own * (r_two * r_two * r_two) / features * inner_two
    )
    d_branch = jnp.concatenate(gather_ch(d_hidden.astype(BF16)), axis=1)
    d_mixed = jnp.dot(d_branch, out_full[:, :width], preferred_element_type=F32)
    grad_out = jnp.einsum("te,tc->ec", d_branch, mixed_rows, preferred_element_type=F32)
    d_cgate = d_mixed * conv_out
    d_conv = d_mixed * c_gate
    following = from_behind(d_conv[:2], "seq", -1)
    edge_one = d_conv * same_one
    edge_two = d_conv * same_two
    after_one = jnp.concatenate([edge_one[1:], following[:1]], axis=0)
    after_two = jnp.concatenate([edge_two[2:], following], axis=0)
    d_gated = conv_weight[0] * d_conv + conv_weight[1] * after_one + conv_weight[2] * after_two
    d_proj = jnp.stack([d_gated * value_rows, d_cgate, d_gated * b_gate], axis=1).astype(BF16)
    d_normed_one = jnp.einsum("tkc,dkc->td", d_proj, in_rolled, preferred_element_type=F32)
    chunks = [d_normed_one[:, j * width : (j + 1) * width] for j in range(CH)]
    d_own_one = scatter_ch(chunks)
    inner_one = sum_ch(jnp.sum(gain_one * d_normed_one * full_rows, axis=1))[:, None]

    grad_in = jnp.einsum("td,tkc->dkc", normed_one, d_proj, preferred_element_type=F32)
    keep, got = core_reduce(
        [grad_in[:, 0].astype(BF16), grad_in[:, 1].astype(BF16), grad_in[:, 2].astype(BF16), grad_out.astype(BF16)],
        [True] * 4,
        x,
        core,
    )
    mix_sum = (keep.astype(F32) + got.astype(F32)).astype(BF16)
    mix_sum = reduce_axis(mix_sum, 1, z, False).astype(BF16)
    mix_sum = reduce_axis(mix_sum, 0, y, True)
    grad_in = mix_sum[:, : 3 * width].reshape(-1, 3, width)
    grad_out = mix_sum[:, 3 * width :]

    grad_conv = jnp.stack(
        [
            jnp.sum(d_conv * current, axis=0),
            jnp.sum(d_conv * prior_one, axis=0),
            jnp.sum(d_conv * prior_two, axis=0),
        ],
        axis=0,
    )
    grad_gain_one = jnp.sum(d_own_one * own_rows * r_one, axis=0)
    input_grad = (
        d_hidden
        + r_one * own_one * d_own_one
        - own_rows * (r_one * r_one * r_one) / features * inner_one
    ).astype(BF16)

    small = jnp.concatenate([grad_conv, grad_gain_one[None], grad_gain_two[None]], axis=0)
    small = small + lax.ppermute(small, "seq", seq_pairs(0, 0, 1))
    for along in (0, 1):
        steps = [(0, 1), (0, 2), (0, 3)] if along == 0 else [(1, 0), (2, 0), (3, 0)]
        small = small + sum(lax.ppermute(small, "seq", seq_pairs(dy, dz, 0)) for dy, dz in steps)
    return (
        block_output,
        input_grad,
        small[3],
        grad_in,
        small[:3],
        grad_out,
        small[4],
        grad_ffn_in,
        grad_ffn_out,
    )


def solution(mesh):
    return jax.shard_map(
        shards,
        mesh=mesh,
        in_specs=(
            P("seq", "ch"),
            P("seq"),
            P(),
            P(None, None, "ch"),
            P(None, "ch"),
            P(None, "ch"),
            P(),
            P(None, None, "ch"),
            P(None, "ch"),
            P("seq", "ch"),
        ),
        out_specs=(
            P("seq", "ch"),
            P("seq", "ch"),
            P("ch"),
            P("seq", None, "ch"),
            P(None, "ch"),
            P("seq", "ch"),
            P("ch"),
            P("seq", None, "ch"),
            P("seq", "ch"),
        ),
        check_vma=False,
    )
```

```python
import jax
import jax.numpy as jnp
from jax import lax
from jax.experimental import pallas as pl
from jax.experimental.pallas import tpu as pltpu
from jax.sharding import PartitionSpec as P

EPS = 1e-05
F32 = jnp.float32
BF16 = jnp.bfloat16
CH = 4


def seq_index(y, z, core):
    return ((y % 4) * 4 + z % 4) * 2 + core


def seq_pairs(dy, dz, dcore):
    return [
        (seq_index(y, z, core), seq_index(y + dy, z + dz, core ^ dcore))
        for y in range(4)
        for z in range(4)
        for core in range(2)
    ]


def ch_pairs(step):
    return [(i, (i + step) % CH) for i in range(CH)]


def gather_ch(block):
    return [block] + [lax.ppermute(block, "ch", ch_pairs(-j)) for j in range(1, CH)]


def scatter_ch(chunks):
    total = chunks[0]
    for j in range(1, CH):
        total = total + lax.ppermute(chunks[j], "ch", ch_pairs(j)).astype(F32)
    return total


def sum_ch(vector):
    total = vector
    for j in range(1, CH):
        total = total + lax.ppermute(vector, "ch", ch_pairs(j))
    return total


def pick(array, index, axis):
    return lax.dynamic_index_in_dim(array, index, axis, keepdims=False)


def from_behind(array, axis, by):
    size = lax.axis_size(axis)
    pairs = [(i, i + by) for i in range(size) if 0 <= i + by < size]
    return lax.ppermute(array, axis, pairs)


def tap_masks(segment_ids):
    padded = jnp.concatenate([segment_ids[:1], segment_ids[:1], segment_ids])
    same_one = (padded[2:] == padded[1:-1]).astype(F32)[:, None]
    same_two = (padded[2:] == padded[:-2]).astype(F32)[:, None]
    return (same_one, same_two)


def tie(*arrays):
    return lax.optimization_barrier(arrays)


def reduce_axis(array, axis, me, along_y):
    total = pick(array, me, axis).astype(F32)
    for step in (1, 3, 2):
        pairs = seq_pairs(step, 0, 0) if along_y else seq_pairs(0, step, 0)
        total = total + lax.ppermute(pick(array, (me + step) % 4, axis), "seq", pairs).astype(F32)
    return total


def dot_nt(a, b):
    return lax.dot_general(a, b, (((1,), (1,)), ((), ())), preferred_element_type=F32)


def dot_tn(a, b):
    return lax.dot_general(a, b, (((0,), (0,)), ((), ())), preferred_element_type=F32)


def dot_nn(a, b):
    return lax.dot_general(a, b, (((1,), (0,)), ((), ())), preferred_element_type=F32)


def rel_rows(x, j, width):
    return pl.ds(pl.multiple_of(lax.rem(x + j, CH) * width, width), width)


def vmem():
    return pl.BlockSpec(memory_space=pltpu.VMEM)


def smem():
    return pl.BlockSpec(memory_space=pltpu.SMEM)


def anywhere():
    return pl.BlockSpec(memory_space=pl.ANY)


def shape(dims, dtype):
    return jax.ShapeDtypeStruct(dims, dtype)


def params(megabytes):
    return pltpu.CompilerParams(vmem_limit_bytes=megabytes * 1024 * 1024)


def cost(macs, nbytes):
    return pl.CostEstimate(flops=2 * macs, bytes_accessed=nbytes, transcendentals=0)


def in_kernel(at, p0, p1, p2, p3, gain, weight, normed, rms, b_out, c_out, v_out, gated, held, sem):
    x = at[0]
    width = p0.shape[1]
    copies = [
        pltpu.make_async_copy(
            weight.at[:, rel_rows(x, j, width), :],
            held.at[:, pl.ds(j * width, width), :],
            sem.at[j],
        )
        for j in range(CH)
    ]
    for copy in copies:
        copy.start()
    pieces = [p0, p1, p2, p3]
    square = jnp.zeros((p0.shape[0], 1), F32)
    for piece in pieces:
        rows = piece[...].astype(F32)
        square = square + jnp.sum(rows * rows, axis=1, keepdims=True)
    r = lax.rsqrt(square / (CH * width) + EPS)
    rms[...] = r
    for j, piece in enumerate(pieces):
        scale = gain[:, rel_rows(x, j, width)]
        normed[:, j * width : (j + 1) * width] = (piece[...].astype(F32) * r * scale).astype(BF16)
    for copy in copies:
        copy.wait()
    b = dot_nn(normed[...], held[0])
    v = dot_nn(normed[...], held[2])
    b_out[...] = b
    v_out[...] = v
    gated[...] = (b * v).astype(BF16)
    c_out[...] = dot_nn(normed[...], held[1])


def in_project(at, pieces, gain, weight):
    rows, width = pieces[0].shape
    features = CH * width
    out = shape((rows, width), F32)
    return pl.pallas_call(
        in_kernel,
        out_shape=(
            shape((rows, features), BF16),
            shape((rows, 1), F32),
            out,
            out,
            out,
            shape((rows, width), BF16),
        ),
        in_specs=[smem()] + [vmem()] * 5 + [anywhere()],
        out_specs=(vmem(),) * 6,
        scratch_shapes=[
            pltpu.VMEM((3, features, width), BF16),
            pltpu.SemaphoreType.DMA((CH,)),
        ],
        compiler_params=params(24),
        cost_estimate=cost(rows * features * 3 * width, 6 * 2**20),
    )(at, *pieces, gain[None], weight)


def ffn_kernel(
    at,
    x0, x1, x2, x3,
    m0, m1, m2, m3,
    gain,
    half,
    other,
    planes,
    down,
    cotangent,
    h_own, rms, normed, act, d_gate_up, d_own, d1, d2, d3, inner,
    w_out, w_in, w_down, g_rows, mixed, h, acc, sem,
):
    x, core = at[0], at[1]
    width = x0.shape[1]
    units = down.shape[1]
    step = units // 3
    halves = [
        pltpu.make_async_copy(half, w_out.at[0], sem.at[0]),
        pltpu.make_async_copy(other, w_out.at[1], sem.at[1]),
    ]
    planes_in = [
        pltpu.make_async_copy(
            planes.at[:, rel_rows(x, j, width), :],
            w_in.at[:, pl.ds(j * width, width), :],
            sem.at[2 + j],
        )
        for j in range(CH)
    ]
    rest = [
        pltpu.make_async_copy(cotangent, g_rows, sem.at[6]),
        pltpu.make_async_copy(down, w_down, sem.at[7]),
    ]
    for copy in halves + planes_in + rest:
        copy.start()
    for j, piece in enumerate((m0, m1, m2, m3)):
        mixed[:, j * width : (j + 1) * width] = piece[...]
    for copy in halves:
        copy.wait()
    square = jnp.zeros((x0.shape[0], 1), F32)
    for j, piece in enumerate((x0, x1, x2, x3)):
        block = lax.rem(x + j, CH)
        which = lax.rem(block // 2 + core, 2)
        rows = pl.ds(pl.multiple_of(lax.rem(block, 2) * width, width), width)
        hj = piece[...].astype(F32) + dot_nt(mixed[...], w_out[which, rows, :])
        h[:, j * width : (j + 1) * width] = hj
        square = square + jnp.sum(hj * hj, axis=1, keepdims=True)
    r = lax.rsqrt(square / (CH * width) + EPS)
    rms[...] = r
    h_own[...] = h[:, :width]
    for j in range(CH):
        columns = slice(j * width, (j + 1) * width)
        scale = gain[:, rel_rows(x, j, width)]
        normed[:, columns] = (h[:, columns] * r * scale).astype(BF16)
    for copy in planes_in + rest:
        copy.wait()

    def part(i, carry):
        f = pl.ds(pl.multiple_of(i * step, 128), step)
        f_up = pl.ds(pl.multiple_of(units + i * step, 128), step)
        gate = dot_nn(normed[...], w_in[0, :, f])
        up = dot_nn(normed[...], w_in[1, :, f])
        d_act = dot_nn(g_rows[...], w_down[:, f])
        sigma = jax.nn.sigmoid(gate)
        swish = gate * sigma
        act[:, f] = (swish * up).astype(BF16)
        d_gate = (d_act * up * sigma * (1.0 + gate * (1.0 - sigma))).astype(BF16)
        d_up = (d_act * swish).astype(BF16)
        d_gate_up[:, f] = d_gate
        d_gate_up[:, f_up] = d_up
        for j in range(CH):
            rows = slice(j * width, (j + 1) * width)
            term = dot_nt(d_gate, w_in[0, rows, f]) + dot_nt(d_up, w_in[1, rows, f])
            acc[j] = jnp.where(i == 0, term, acc[j] + term)
        return carry

    lax.fori_loop(0, 3, part, 0)
    total = jnp.zeros((x0.shape[0], 1), F32)
    for j in range(CH):
        scale = gain[:, rel_rows(x, j, width)]
        total = total + jnp.sum(
            scale * acc[j] * h[:, j * width : (j + 1) * width], axis=1, keepdims=True
        )
    inner[...] = total
    d_own[...] = acc[0]
    d1[...] = acc[1].astype(BF16)
    d2[...] = acc[2].astype(BF16)
    d3[...] = acc[3].astype(BF16)


def ffn(at, pieces, mixed_pieces, gain, half, other, planes, down, cotangent):
    rows, width = pieces[0].shape
    features = CH * width
    units = down.shape[1]
    block, column = shape((rows, width), BF16), shape((rows, 1), F32)
    wide = shape((rows, width), F32)
    return pl.pallas_call(
        ffn_kernel,
        out_shape=(
            wide,
            column,
            shape((rows, features), BF16),
            shape((rows, units), BF16),
            shape((rows, 2 * units), BF16),
            wide,
            block,
            block,
            block,
            column,
        ),
        in_specs=[smem()] + [vmem()] * 9 + [anywhere()] * 5,
        out_specs=(vmem(),) * 10,
        scratch_shapes=[
            pltpu.VMEM((2, features // 2, features), BF16),
            pltpu.VMEM((2, features, units), BF16),
            pltpu.VMEM((features, units), BF16),
            pltpu.VMEM((rows, features), BF16),
            pltpu.VMEM((rows, features), BF16),
            pltpu.VMEM((rows, features), F32),
            pltpu.VMEM((CH, rows, width), F32),
            pltpu.SemaphoreType.DMA((8,)),
        ],
        compiler_params=params(48),
        cost_estimate=cost(rows * features * (features + 5 * units), 20 * 2**20),
    )(at, *pieces, *mixed_pieces, gain[None], half, other, planes, down, cotangent)


def pair_kernel(
    at, a_left, a_right, b_left, b_right, give, keep, held, *, a_rolled, b_rolled
):
    x, core = at[0], at[1]
    y = pl.program_id(0)
    wide = give.shape[2] * 8
    turned = lax.rem(y + CH - x, CH)
    cut = a_right.shape[1]
    for left, right, rolled, base in (
        (a_left, a_right, a_rolled, 0),
        (b_left, b_right, b_rolled, cut),
    ):
        where = turned if rolled else y
        block = left[:, pl.ds(pl.multiple_of(where * wide, wide), wide)]
        columns = right.shape[1]
        step = columns // 3 if columns % 384 == 0 else columns
        for first in range(0, columns, step):
            held[:, base + first : base + first + step] = dot_tn(
                block, right[:, first : first + step]
            )
    for z in range(4):
        mine = pl.multiple_of((2 * z + core) * 32, 32)
        theirs = pl.multiple_of((2 * z + 1 - core) * 32, 32)
        keep[z, 0] = held[pl.ds(mine, 32), :].astype(BF16)
        give[z, 0] = held[pl.ds(theirs, 32), :].astype(BF16)


def pair_products(at, a_left, a_right, b_left, b_right, a_rolled, b_rolled):
    columns = a_right.shape[1] + b_right.shape[1]
    tokens, features = a_left.shape
    out = shape((4, 4, features // 32, columns), BF16)
    spec = pl.BlockSpec((4, 1, features // 32, columns), lambda y: (0, y, 0, 0))

    def body(*refs):
        pair_kernel(*refs, a_rolled=a_rolled, b_rolled=b_rolled)

    return pl.pallas_call(
        body,
        grid=(4,),
        out_shape=(out, out),
        in_specs=[smem()] + [vmem()] * 4,
        out_specs=(spec, spec),
        scratch_shapes=[pltpu.VMEM((features // 4, columns), F32)],
        compiler_params=params(40),
        cost_estimate=cost(tokens * features * columns, 4 * features * columns),
    )(at, a_left, a_right, b_left, b_right)


def back_kernel(at, p0, p1, p2, p3, grads, gain, weight, d_own, d1, d2, d3, inner, held, sem):
    x = at[0]
    width = p0.shape[1]
    copies = [
        pltpu.make_async_copy(
            weight.at[:, rel_rows(x, j, width), :],
            held.at[:, pl.ds(j * width, width), :],
            sem.at[j],
        )
        for j in range(CH)
    ]
    for copy in copies:
        copy.start()
    total = jnp.zeros((p0.shape[0], 1), F32)
    for j, piece in enumerate((p0, p1, p2, p3)):
        copies[j].wait()
        rows = slice(j * width, (j + 1) * width)
        term = dot_nt(grads[:, :width], held[0, rows, :])
        for k in (1, 2):
            term = term + dot_nt(grads[:, k * width : (k + 1) * width], held[k, rows, :])
        scale = gain[:, rel_rows(x, j, width)]
        total = total + jnp.sum(scale * term * piece[...].astype(F32), axis=1, keepdims=True)
        if j == 0:
            d_own[...] = term
        else:
            (d1, d2, d3)[j - 1][...] = term.astype(BF16)
    inner[...] = total


def back_project(at, pieces, grads, gain, weight):
    rows, width = pieces[0].shape
    features = CH * width
    block = shape((rows, width), BF16)
    return pl.pallas_call(
        back_kernel,
        out_shape=(shape((rows, width), F32), block, block, block, shape((rows, 1), F32)),
        in_specs=[smem()] + [vmem()] * 6 + [anywhere()],
        out_specs=(vmem(),) * 5,
        scratch_shapes=[
            pltpu.VMEM((3, features, width), BF16),
            pltpu.SemaphoreType.DMA((CH,)),
        ],
        compiler_params=params(24),
        cost_estimate=cost(rows * features * 3 * width, 6 * 2**20),
    )(at, *pieces, grads, gain[None], weight)


def scatter_groups(array, groups):
    return lax.psum_scatter(array, "seq", scatter_dimension=0, axis_index_groups=groups)


def shards(
    block_input,
    segment_ids,
    norm1_gain,
    in_weight,
    conv_weight,
    out_weight,
    norm2_gain,
    ffn_in_weight,
    ffn_out_weight,
    out_grad,
):
    x = lax.axis_index("ch")
    seq = lax.axis_index("seq")
    core, z, y = seq % 2, (seq // 2) % 4, seq // 8
    features = norm1_gain.shape[0]
    width = block_input.shape[1]
    hidden_units = ffn_out_weight.shape[1]

    def rolled(array):
        blocks = array.reshape((CH, width) + array.shape[1:])
        return jnp.concatenate([pick(blocks, (x + j) % CH, 0) for j in range(CH)], axis=0)

    at = jnp.stack([x, core]).astype(jnp.int32)
    own_one = pick(norm1_gain.reshape(CH, width), x, 0)
    own_two = pick(norm2_gain.reshape(CH, width), x, 0)
    in_planes = jnp.transpose(in_weight, (1, 0, 2))

    pieces = gather_ch(block_input)
    half_rows = out_weight.shape[0] // 2
    half = lax.dynamic_slice_in_dim(out_weight, core * half_rows, half_rows, 0)
    half_pieces = gather_ch(half)
    grad_full = lax.all_gather(out_grad, "ch", axis=1, tiled=True)
    ffn_planes = jnp.transpose(ffn_in_weight, (1, 0, 2))
    ffn_planes, *pieces = tie(ffn_planes, *pieces)

    normed_one, r_one, b_gate, c_gate, value_rows, gated_rows = in_project(
        at, pieces, norm1_gain, in_planes
    )
    own_rows = block_input.astype(F32)
    carried = from_behind(gated_rows[-2:], "seq", 1)
    extended = jnp.concatenate([carried, gated_rows], axis=0).astype(F32)
    same_one, same_two = tap_masks(segment_ids)
    current = extended[2:]
    prior_one = extended[1:-1] * same_one
    prior_two = extended[:-2] * same_two
    conv_out = conv_weight[0] * current + conv_weight[1] * prior_one + conv_weight[2] * prior_two
    mixed_rows = (c_gate * conv_out).astype(BF16)

    mixed_pieces = gather_ch(mixed_rows)
    half_pieces = tie(*half_pieces, mixed_rows)[:CH]
    half_full = jnp.concatenate(half_pieces, axis=1)
    other_half = lax.ppermute(half_full, "seq", seq_pairs(0, 0, 1))
    out_rolled = rolled(tie(out_weight, mixed_rows)[0])
    (
        hidden_own,
        r_two,
        normed_two,
        act_rows,
        d_gate_up,
        d_own,
        d_one,
        d_two,
        d_three,
        inner,
    ) = ffn(
        at,
        pieces,
        mixed_pieces,
        norm2_gain,
        half_full,
        other_half,
        ffn_planes,
        ffn_out_weight,
        grad_full,
    )
    d_normed_own = scatter_ch([d_own, d_one, d_two, d_three])
    inner_two = sum_ch(inner[:, 0])[:, None]

    give, keep = pair_products(at, normed_two, d_gate_up, grad_full, act_rows, True, False)
    got = lax.ppermute(give, "seq", seq_pairs(0, 0, 1))
    down_terms = jnp.einsum(
        "tf,ef->te", act_rows, ffn_out_weight, preferred_element_type=F32
    ).astype(BF16)
    down = lax.psum_scatter(down_terms, "ch", scatter_dimension=1, tiled=True)
    block_output = (hidden_own + down.astype(F32)).astype(BF16)

    grad_gain_two = jnp.sum(d_normed_own * hidden_own * r_two, axis=0)
    d_hidden = (
        out_grad.astype(F32)
        + r_two * own_two * d_normed_own
        - hidden_own * (r_two * r_two * r_two) / features * inner_two
    )
    d_branch = jnp.concatenate(gather_ch(d_hidden.astype(BF16)), axis=1)
    ffn_kept = (keep.astype(F32) + got.astype(F32)).astype(BF16)
    d_branch, ffn_kept, out_rolled = tie(d_branch, ffn_kept, out_rolled)
    groups = [[seq_index(i, k, c) for k in range(4)] for i in range(4) for c in range(2)]
    ffn_sum = scatter_groups(ffn_kept, groups)
    groups = [[seq_index(k, i, c) for k in range(4)] for i in range(4) for c in range(2)]
    ffn_sum = scatter_groups(ffn_sum, groups).astype(F32)
    grad_ffn_in = ffn_sum[:, : 2 * hidden_units].reshape(-1, 2, hidden_units)
    grad_ffn_out = ffn_sum[:, 2 * hidden_units :]

    d_mixed = jnp.dot(d_branch, out_rolled, preferred_element_type=F32)
    d_cgate = d_mixed * conv_out
    d_conv = d_mixed * c_gate
    following = from_behind(d_conv[:2], "seq", -1)
    edge_one = d_conv * same_one
    edge_two = d_conv * same_two
    after_one = jnp.concatenate([edge_one[1:], following[:1]], axis=0)
    after_two = jnp.concatenate([edge_two[2:], following], axis=0)
    d_gated = conv_weight[0] * d_conv + conv_weight[1] * after_one + conv_weight[2] * after_two
    d_proj = jnp.concatenate(
        [d_gated * value_rows, d_cgate, d_gated * b_gate], axis=1
    ).astype(BF16)
    d_own, d_one, d_two, d_three, inner = back_project(
        at, pieces, d_proj, norm1_gain, in_planes
    )
    d_own_one = scatter_ch([d_own, d_one, d_two, d_three])
    inner_one = sum_ch(inner[:, 0])[:, None]

    give, keep = pair_products(at, normed_one, d_proj, d_branch, mixed_rows, True, True)
    got = lax.ppermute(give, "seq", seq_pairs(0, 0, 1))
    mix_sum = (keep.astype(F32) + got.astype(F32)).astype(BF16)
    mix_sum = reduce_axis(mix_sum, 0, z, False).astype(BF16)
    mix_sum = reduce_axis(mix_sum, 0, y, True)
    grad_in = mix_sum[:, : 3 * width].reshape(-1, 3, width)
    grad_out = mix_sum[:, 3 * width :]

    grad_conv = jnp.stack(
        [
            jnp.sum(d_conv * current, axis=0),
            jnp.sum(d_conv * prior_one, axis=0),
            jnp.sum(d_conv * prior_two, axis=0),
        ],
        axis=0,
    )
    grad_gain_one = jnp.sum(d_own_one * own_rows * r_one, axis=0)
    input_grad = (
        d_hidden
        + r_one * own_one * d_own_one
        - own_rows * (r_one * r_one * r_one) / features * inner_one
    ).astype(BF16)

    small = jnp.concatenate([grad_conv, grad_gain_one[None], grad_gain_two[None]], axis=0)
    small = small + lax.ppermute(small, "seq", seq_pairs(0, 0, 1))
    for along in (0, 1):
        steps = [(0, 1), (0, 2), (0, 3)] if along == 0 else [(1, 0), (2, 0), (3, 0)]
        small = small + sum(lax.ppermute(small, "seq", seq_pairs(dy, dz, 0)) for dy, dz in steps)
    return (
        block_output,
        input_grad,
        small[3],
        grad_in,
        small[:3],
        grad_out,
        small[4],
        grad_ffn_in,
        grad_ffn_out,
    )


def solution(mesh):
    return jax.shard_map(
        shards,
        mesh=mesh,
        in_specs=(
            P("seq", "ch"),
            P("seq"),
            P(),
            P(None, None, "ch"),
            P(None, "ch"),
            P(None, "ch"),
            P(),
            P(None, None, "ch"),
            P(None, "ch"),
            P("seq", "ch"),
        ),
        out_specs=(
            P("seq", "ch"),
            P("seq", "ch"),
            P("ch"),
            P("seq", None, "ch"),
            P(None, "ch"),
            P("seq", "ch"),
            P("ch"),
            P("seq", None, "ch"),
            P("seq", "ch"),
        ),
        check_vma=False,
    )
```

```python
import jax
import jax.numpy as jnp
from jax import lax
from jax.experimental import pallas as pl
from jax.experimental.pallas import tpu as pltpu
from jax.sharding import PartitionSpec as P

EPS = 1e-05
F32 = jnp.float32
BF16 = jnp.bfloat16
CH = 4


def seq_index(y, z, core):
    return ((y % 4) * 4 + z % 4) * 2 + core


def seq_pairs(dy, dz, dcore):
    return [
        (seq_index(y, z, core), seq_index(y + dy, z + dz, core ^ dcore))
        for y in range(4)
        for z in range(4)
        for core in range(2)
    ]


def ch_pairs(step):
    return [(i, (i + step) % CH) for i in range(CH)]


def gather_ch(block):
    return [block] + [lax.ppermute(block, "ch", ch_pairs(-j)) for j in range(1, CH)]


def scatter_ch(chunks):
    total = chunks[0]
    for j in range(1, CH):
        total = total + lax.ppermute(chunks[j], "ch", ch_pairs(j)).astype(F32)
    return total


def sum_ch(vector):
    total = vector
    for j in range(1, CH):
        total = total + lax.ppermute(vector, "ch", ch_pairs(j))
    return total


def pick(array, index, axis):
    return lax.dynamic_index_in_dim(array, index, axis, keepdims=False)


def from_behind(array, axis, by):
    size = lax.axis_size(axis)
    pairs = [(i, i + by) for i in range(size) if 0 <= i + by < size]
    return lax.ppermute(array, axis, pairs)


def first_count(segment_ids):
    return jnp.sum((segment_ids == segment_ids[0]).astype(jnp.int32))


def tap_masks(count, rows):
    token = lax.broadcasted_iota(jnp.int32, (rows, 1), 0)
    same_one = (token != count).astype(F32)
    same_two = ((token != count) & (token != count + 1)).astype(F32)
    return (same_one, same_two)


def tie(*arrays):
    return lax.optimization_barrier(arrays)


def reduce_axis(array, axis, me, along_y):
    total = pick(array, me, axis).astype(F32)
    for step in (1, 3, 2):
        pairs = seq_pairs(step, 0, 0) if along_y else seq_pairs(0, step, 0)
        total = total + lax.ppermute(pick(array, (me + step) % 4, axis), "seq", pairs).astype(F32)
    return total


def dot_nt(a, b):
    return lax.dot_general(a, b, (((1,), (1,)), ((), ())), preferred_element_type=F32)


def dot_tn(a, b):
    return lax.dot_general(a, b, (((0,), (0,)), ((), ())), preferred_element_type=F32)


def dot_nn(a, b):
    return lax.dot_general(a, b, (((1,), (0,)), ((), ())), preferred_element_type=F32)


def rel_rows(x, j, width):
    return pl.ds(pl.multiple_of(lax.rem(x + j, CH) * width, width), width)


def vmem():
    return pl.BlockSpec(memory_space=pltpu.VMEM)


def smem():
    return pl.BlockSpec(memory_space=pltpu.SMEM)


def anywhere():
    return pl.BlockSpec(memory_space=pl.ANY)


def shape(dims, dtype):
    return jax.ShapeDtypeStruct(dims, dtype)


def params(megabytes):
    return pltpu.CompilerParams(vmem_limit_bytes=megabytes * 1024 * 1024)


def cost(macs, nbytes):
    return pl.CostEstimate(flops=2 * macs, bytes_accessed=nbytes, transcendentals=0)


def in_kernel(at, p0, p1, p2, p3, gain, weight, normed, rms, b_out, c_out, v_out, gated, held, sem):
    x = at[0]
    width = p0.shape[1]
    copies = [
        pltpu.make_async_copy(
            weight.at[:, rel_rows(x, j, width), :],
            held.at[:, pl.ds(j * width, width), :],
            sem.at[j],
        )
        for j in range(CH)
    ]
    for copy in copies:
        copy.start()
    pieces = [p0, p1, p2, p3]
    square = jnp.zeros((p0.shape[0], 1), F32)
    for piece in pieces:
        rows = piece[...].astype(F32)
        square = square + jnp.sum(rows * rows, axis=1, keepdims=True)
    r = lax.rsqrt(square / (CH * width) + EPS)
    rms[...] = r
    for j, piece in enumerate(pieces):
        scale = gain[:, rel_rows(x, j, width)]
        normed[:, j * width : (j + 1) * width] = (piece[...].astype(F32) * r * scale).astype(BF16)
    for copy in copies:
        copy.wait()
    b = dot_nn(normed[...], held[0])
    v = dot_nn(normed[...], held[2])
    b_out[...] = b
    v_out[...] = v
    gated[...] = (b * v).astype(BF16)
    c_out[...] = dot_nn(normed[...], held[1])


def in_project(at, pieces, gain, weight):
    rows, width = pieces[0].shape
    features = CH * width
    out = shape((rows, width), F32)
    return pl.pallas_call(
        in_kernel,
        out_shape=(
            shape((rows, features), BF16),
            shape((rows, 1), F32),
            out,
            out,
            out,
            shape((rows, width), BF16),
        ),
        in_specs=[smem()] + [vmem()] * 5 + [anywhere()],
        out_specs=(vmem(),) * 6,
        scratch_shapes=[
            pltpu.VMEM((3, features, width), BF16),
            pltpu.SemaphoreType.DMA((CH,)),
        ],
        compiler_params=params(24),
        cost_estimate=cost(rows * features * 3 * width, 6 * 2**20),
    )(at, *pieces, gain[None], weight)


def ffn_kernel(
    at,
    x0, x1, x2, x3,
    m0, m1, m2, m3,
    gain,
    half,
    other,
    planes,
    down,
    cotangent,
    h, rms, normed, act, d_gate_up, d_own, d1, d2, d3,
    w_out, w_in, w_down, g_rows, mixed, acc, sem,
):
    x, core = at[0], at[1]
    width = x0.shape[1]
    units = down.shape[1]
    step = units // 3
    halves = [
        pltpu.make_async_copy(half, w_out.at[0], sem.at[0]),
        pltpu.make_async_copy(other, w_out.at[1], sem.at[1]),
    ]
    planes_in = [
        pltpu.make_async_copy(
            planes.at[:, rel_rows(x, j, width), :],
            w_in.at[:, pl.ds(j * width, width), :],
            sem.at[2 + j],
        )
        for j in range(CH)
    ]
    rest = [
        pltpu.make_async_copy(cotangent, g_rows, sem.at[6]),
        pltpu.make_async_copy(down, w_down, sem.at[7]),
    ]
    for copy in halves + planes_in + rest:
        copy.start()
    for j, piece in enumerate((m0, m1, m2, m3)):
        mixed[:, j * width : (j + 1) * width] = piece[...]
    for copy in halves:
        copy.wait()
    square = jnp.zeros((x0.shape[0], 1), F32)
    for j, piece in enumerate((x0, x1, x2, x3)):
        block = lax.rem(x + j, CH)
        which = lax.rem(block // 2 + core, 2)
        rows = pl.ds(pl.multiple_of(lax.rem(block, 2) * width, width), width)
        hj = piece[...].astype(F32) + dot_nt(mixed[...], w_out[which, rows, :])
        h[:, j * width : (j + 1) * width] = hj
        square = square + jnp.sum(hj * hj, axis=1, keepdims=True)
    r = lax.rsqrt(square / (CH * width) + EPS)
    rms[...] = r
    for j in range(CH):
        columns = slice(j * width, (j + 1) * width)
        scale = gain[:, rel_rows(x, j, width)]
        normed[:, columns] = (h[:, columns] * r * scale).astype(BF16)
    for copy in planes_in + rest:
        copy.wait()

    def part(i, carry):
        f = pl.ds(pl.multiple_of(i * step, 128), step)
        f_up = pl.ds(pl.multiple_of(units + i * step, 128), step)
        gate = dot_nn(normed[...], w_in[0, :, f])
        up = dot_nn(normed[...], w_in[1, :, f])
        d_act = dot_nn(g_rows[...], w_down[:, f])
        sigma = jax.nn.sigmoid(gate)
        swish = gate * sigma
        act[:, f] = (swish * up).astype(BF16)
        d_gate = (d_act * up * sigma * (1.0 + gate * (1.0 - sigma))).astype(BF16)
        d_up = (d_act * swish).astype(BF16)
        d_gate_up[:, f] = d_gate
        d_gate_up[:, f_up] = d_up
        for j in range(CH):
            rows = slice(j * width, (j + 1) * width)
            term = dot_nt(d_gate, w_in[0, rows, f]) + dot_nt(d_up, w_in[1, rows, f])
            acc[j] = jnp.where(i == 0, term, acc[j] + term)
        return carry

    lax.fori_loop(0, 3, part, 0)
    d_own[...] = acc[0]
    d1[...] = acc[1].astype(BF16)
    d2[...] = acc[2].astype(BF16)
    d3[...] = acc[3].astype(BF16)


def ffn(at, pieces, mixed_pieces, gain, half, other, planes, down, cotangent):
    rows, width = pieces[0].shape
    features = CH * width
    units = down.shape[1]
    block = shape((rows, width), BF16)
    return pl.pallas_call(
        ffn_kernel,
        out_shape=(
            shape((rows, features), F32),
            shape((rows, 1), F32),
            shape((rows, features), BF16),
            shape((rows, units), BF16),
            shape((rows, 2 * units), BF16),
            shape((rows, width), F32),
            block,
            block,
            block,
        ),
        in_specs=[smem()] + [vmem()] * 9 + [anywhere()] * 5,
        out_specs=(vmem(),) * 9,
        scratch_shapes=[
            pltpu.VMEM((2, features // 2, features), BF16),
            pltpu.VMEM((2, features, units), BF16),
            pltpu.VMEM((features, units), BF16),
            pltpu.VMEM((rows, features), BF16),
            pltpu.VMEM((rows, features), BF16),
            pltpu.VMEM((CH, rows, width), F32),
            pltpu.SemaphoreType.DMA((8,)),
        ],
        compiler_params=params(48),
        cost_estimate=cost(rows * features * (features + 5 * units), 20 * 2**20),
    )(at, *pieces, *mixed_pieces, gain[None], half, other, planes, down, cotangent)


def pair_kernel(
    at, a_left, a_right, b_left, b_right, give_a, give_b, keep, held, *, a_rolled, b_rolled
):
    x, core = at[0], at[1]
    y = pl.program_id(0)
    wide = keep.shape[2] * 8
    turned = lax.rem(y + CH - x, CH)
    cut = a_right.shape[1]
    for left, right, rolled, base in (
        (a_left, a_right, a_rolled, 0),
        (b_left, b_right, b_rolled, cut),
    ):
        where = turned if rolled else y
        block = left[:, pl.ds(pl.multiple_of(where * wide, wide), wide)]
        columns = right.shape[1]
        step = columns // 3 if columns % 384 == 0 else columns
        for first in range(0, columns, step):
            held[:, base + first : base + first + step] = dot_tn(
                block, right[:, first : first + step]
            )
    for z in range(4):
        mine = pl.multiple_of((2 * z + core) * 32, 32)
        theirs = pl.multiple_of((2 * z + 1 - core) * 32, 32)
        keep[z, 0] = held[pl.ds(mine, 32), :].astype(BF16)
        (give_a, give_b)[z // 2][z % 2, 0] = held[pl.ds(theirs, 32), :].astype(BF16)


def pair_products(at, a_left, a_right, b_left, b_right, a_rolled, b_rolled):
    columns = a_right.shape[1] + b_right.shape[1]
    tokens, features = a_left.shape
    out = shape((4, 4, features // 32, columns), BF16)
    spec = pl.BlockSpec((4, 1, features // 32, columns), lambda y: (0, y, 0, 0))
    half = shape((2, 4, features // 32, columns), BF16)
    half_spec = pl.BlockSpec((2, 1, features // 32, columns), lambda y: (0, y, 0, 0))

    def body(*refs):
        pair_kernel(*refs, a_rolled=a_rolled, b_rolled=b_rolled)

    return pl.pallas_call(
        body,
        grid=(4,),
        out_shape=(half, half, out),
        in_specs=[smem()] + [vmem()] * 4,
        out_specs=(half_spec, half_spec, spec),
        scratch_shapes=[pltpu.VMEM((features // 4, columns), F32)],
        compiler_params=params(40),
        cost_estimate=cost(tokens * features * columns, 4 * features * columns),
    )(at, a_left, a_right, b_left, b_right)


def swap_cores(halves):
    return [lax.ppermute(half, "seq", seq_pairs(0, 0, 1)) for half in halves]


def add_kernel(keep, got_a, got_b, out):
    out[:2] = (keep[:2].astype(F32) + got_a[...].astype(F32)).astype(BF16)
    out[2:] = (keep[2:].astype(F32) + got_b[...].astype(F32)).astype(BF16)


def add_cores(keep, got):
    spec = pl.BlockSpec((4, 1) + keep.shape[2:], lambda y: (0, y, 0, 0))
    half = pl.BlockSpec((2, 1) + keep.shape[2:], lambda y: (0, y, 0, 0))
    return pl.pallas_call(
        add_kernel,
        grid=(4,),
        out_shape=shape(keep.shape, BF16),
        in_specs=[spec, half, half],
        out_specs=spec,
        compiler_params=params(24),
        cost_estimate=cost(2**20, 6 * keep.size),
    )(keep, *got)


def spread(small):
    high = small.astype(BF16)
    low = (small - high.astype(F32)).astype(BF16)
    return high, low


def join(message, width):
    return message[:8, :width].astype(F32) + message[:8, width : 2 * width].astype(F32)


def send_kernel(at, keep, got_a, got_b, small, own, m1, m2, m3):
    z = at[3]
    rows = own.shape[0]
    width = small.shape[1]
    for j, out in enumerate((own, m1, m2, m3)):
        block = lax.rem(z + j, 4)
        inside = lax.rem(block, 2)
        got = jnp.where(block < 2, got_a[inside].astype(F32), got_b[inside].astype(F32))
        total = keep[block].astype(F32) + got
        out[:rows] = total.reshape(own.shape).astype(out.dtype)
    high, low = spread(jnp.concatenate([small[...], jnp.zeros_like(small[...])], axis=0))
    for out in (m1, m2, m3):
        out[rows:, :width] = high
        out[rows:, width : 2 * width] = low


def send_z(at, keep, got, small):
    rows, columns = keep.shape[1] * keep.shape[2], keep.shape[3]
    message = shape((rows + 16, columns), BF16)
    return pl.pallas_call(
        send_kernel,
        out_shape=(shape((rows, columns), F32), message, message, message),
        in_specs=[smem()] + [vmem()] * 4,
        out_specs=(vmem(),) * 4,
        compiler_params=params(24),
        cost_estimate=cost(2**20, 2**22),
    )(at, keep, *got, small)


def turn_kernel(at, own, m1, m2, m3, small, left, n1, n2, n3, small_out, total):
    y = at[4]
    rows = own.shape[0]
    width = small.shape[1]
    total[...] = own[...]
    small_sum = small[...]
    for m in (m1, m2, m3):
        total[...] += m[:rows].astype(F32)
        small_sum = small_sum + join(m[rows:], width)
    small_out[...] = small_sum
    part = rows // 4
    for j, out in enumerate((left, n1, n2, n3)):
        block = pl.multiple_of(lax.rem(y + j, 4) * part, part)
        out[:part] = total[pl.ds(block, part)].astype(out.dtype)
    high, low = spread(jnp.concatenate([small_sum, jnp.zeros_like(small_sum)], axis=0))
    for out in (n1, n2, n3):
        out[part:, :width] = high
        out[part:, width : 2 * width] = low


def turn(at, own, messages, small):
    rows, columns = own.shape
    message = shape((rows // 4 + 16, columns), BF16)
    return pl.pallas_call(
        turn_kernel,
        out_shape=(
            shape((rows // 4, columns), F32),
            message,
            message,
            message,
            shape(small.shape, F32),
        ),
        in_specs=[smem()] + [vmem()] * 5,
        out_specs=(vmem(),) * 5,
        scratch_shapes=[pltpu.VMEM((rows, columns), F32)],
        compiler_params=params(24),
        cost_estimate=cost(2**20, 2**21),
    )(at, own, *messages, small)


def last_kernel(own, m1, m2, m3, small, in_out, out_out, small_out):
    rows = own.shape[0]
    width = small.shape[1]
    total = own[...]
    small_sum = small[...]
    for m in (m1, m2, m3):
        total = total + m[:rows].astype(F32)
        small_sum = small_sum + join(m[rows:], width)
    for k in range(3):
        in_out[k] = total[:, k * width : (k + 1) * width]
    out_out[...] = total[:, 3 * width :]
    small_out[...] = small_sum


def last(own, messages, small):
    rows, columns = own.shape
    width = small.shape[1]
    return pl.pallas_call(
        last_kernel,
        out_shape=(
            shape((3, rows, width), F32),
            shape((rows, columns - 3 * width), F32),
            shape(small.shape, F32),
        ),
        in_specs=[vmem()] * 5,
        out_specs=(vmem(),) * 3,
        compiler_params=params(24),
        cost_estimate=cost(2**20, 2**20),
    )(own, *messages, small)


def end_kernel(d_own, d1, d2, d3, inner, d_hidden, rows_in, rms, gain, grad, gain_grad):
    rows, width = d_own.shape
    total = d_own[...]
    line = inner[...]
    for d in (d1, d2, d3):
        total = total + d[:rows].astype(F32)
        high = [d[rows + 16 * i : rows + 16 * (i + 1)].astype(F32) for i in range(4)]
        line = line + jnp.concatenate(
            [high[0] + high[2], high[1] + high[3]], axis=1
        )
    column = lax.dot_general(
        line, jnp.full((16, width), 1.0 / 16, F32), (((0,), (0,)), ((), ())),
        precision=lax.Precision.HIGHEST, preferred_element_type=F32,
    )
    r = rms[...]
    xs = rows_in[...].astype(F32)
    gain_grad[...] = jnp.sum(total * xs * r, axis=0, keepdims=True)
    grad[...] = (
        d_hidden[...] + r * gain[...] * total - xs * (r * r * r / (CH * width)) * column
    ).astype(BF16)


def end(d_own, received, inner, d_hidden, rows_in, rms, gain):
    rows, width = d_own.shape
    return pl.pallas_call(
        end_kernel,
        out_shape=(shape((rows, width), BF16), shape((1, width), F32)),
        in_specs=[vmem()] * 9,
        out_specs=(vmem(),) * 2,
        compiler_params=params(24),
        cost_estimate=cost(2**20, 2**21),
    )(d_own, *received, inner, d_hidden, rows_in, rms, gain[None])


def mid_kernel(
    at, u_own, u1, u2, u3, h, rms, cotangent, weight, c_gate, conv_out,
    d_branch, d_hidden, d_conv, d_cgate,
):
    x = at[0]
    width = u_own.shape[1]
    dot = jnp.zeros((u_own.shape[0], 1), F32)
    us = (u_own, u1, u2, u3)
    for j, u in enumerate(us):
        g = cotangent[:, rel_rows(x, j, width)].astype(F32)
        hj = h[:, j * width : (j + 1) * width]
        dot = dot + jnp.sum((u[...].astype(F32) - g) * hj, axis=1, keepdims=True)
    r = rms[...]
    scale = dot * (r * r / (CH * width))
    d_mixed = jnp.zeros(u_own.shape, F32)
    for j, u in enumerate(us):
        columns = slice(j * width, (j + 1) * width)
        full = u[...].astype(F32) - h[:, columns] * scale
        if j == 0:
            d_hidden[...] = full
        rounded = full.astype(BF16)
        d_branch[:, columns] = rounded
        d_mixed = d_mixed + dot_nn(rounded, weight[rel_rows(x, j, width), :])
    d_conv[...] = d_mixed * c_gate[...]
    d_cgate[...] = (d_mixed * conv_out[...]).astype(BF16)


def mid(at, pieces, h, rms, cotangent, weight, c_gate, conv_out):
    rows, width = c_gate.shape
    wide = shape((rows, width), F32)
    return pl.pallas_call(
        mid_kernel,
        out_shape=(shape((rows, CH * width), BF16), wide, wide, shape((rows, width), BF16)),
        in_specs=[smem()] + [vmem()] * 10,
        out_specs=(vmem(),) * 4,
        compiler_params=params(24),
        cost_estimate=cost(rows * CH * width * width, 6 * 2**20),
    )(at, *pieces, h, rms, cotangent, weight, c_gate, conv_out)


def back_kernel(
    at, p0, p1, p2, p3, d_conv, following, taps, value, b_gate, d_cgate, gain, weight,
    grads, d_own, d1, d2, d3, inner, held, sem,
):
    x, count = at[0], at[2]
    rows, width = p0.shape
    copies = [
        pltpu.make_async_copy(
            weight.at[:, rel_rows(x, j, width), :],
            held.at[:, pl.ds(j * width, width), :],
            sem.at[j],
        )
        for j in range(CH)
    ]
    for copy in copies:
        copy.start()
    token = lax.broadcasted_iota(jnp.int32, (rows, width), 0)
    d = d_conv[...]
    next_one, next_two = following[0:1, :], following[1:2, :]
    after_one = jnp.where(token + 1 == count, 0.0, pltpu.roll(d, rows - 1, 0))
    after_one = jnp.where(token == rows - 1, next_one, after_one)
    after_two = pltpu.roll(d, rows - 2, 0)
    after_two = jnp.where((token + 2 == count) | (token + 1 == count), 0.0, after_two)
    after_two = jnp.where(token == rows - 2, next_one, after_two)
    after_two = jnp.where(token == rows - 1, next_two, after_two)
    d_gated = taps[0:1, :] * d + taps[1:2, :] * after_one + taps[2:3, :] * after_two
    grads[:, :width] = (d_gated * value[...]).astype(BF16)
    grads[:, width : 2 * width] = d_cgate[...]
    grads[:, 2 * width :] = (d_gated * b_gate[...]).astype(BF16)
    total = jnp.zeros((rows, width), F32)
    for j, piece in enumerate((p0, p1, p2, p3)):
        copies[j].wait()
        block = slice(j * width, (j + 1) * width)
        term = dot_nt(grads[:, :width], held[0, block, :])
        for k in (1, 2):
            term = term + dot_nt(grads[:, k * width : (k + 1) * width], held[k, block, :])
        scale = gain[:, rel_rows(x, j, width)]
        total = total + scale * term * piece[...].astype(F32)
        if j == 0:
            d_own[...] = term
        else:
            (d1, d2, d3)[j - 1][:rows, :] = term.astype(BF16)
    ones = jnp.ones((16, width), F32)
    row = lax.dot_general(
        ones, total, (((1,), (1,)), ((), ())),
        precision=lax.Precision.HIGHEST, preferred_element_type=F32,
    )
    inner[...] = row
    high = row.astype(BF16)
    low = (row - high.astype(F32)).astype(BF16)
    for out in (d1, d2, d3):
        out[rows : rows + 16, :] = high[:, :width]
        out[rows + 16 : rows + 32, :] = high[:, width:]
        out[rows + 32 : rows + 48, :] = low[:, :width]
        out[rows + 48 : rows + 64, :] = low[:, width:]


def back_project(at, pieces, d_conv, following, taps, value, b_gate, d_cgate, gain, weight):
    rows, width = pieces[0].shape
    features = CH * width
    block = shape((rows + 64, width), BF16)
    return pl.pallas_call(
        back_kernel,
        out_shape=(
            shape((rows, 3 * width), BF16),
            shape((rows, width), F32),
            block,
            block,
            block,
            shape((16, rows), F32),
        ),
        in_specs=[smem()] + [vmem()] * 11 + [anywhere()],
        out_specs=(vmem(),) * 6,
        scratch_shapes=[
            pltpu.VMEM((3, features, width), BF16),
            pltpu.SemaphoreType.DMA((CH,)),
        ],
        compiler_params=params(32),
        cost_estimate=cost(rows * features * 3 * width, 6 * 2**20),
    )(at, *pieces, d_conv, following, taps, value, b_gate, d_cgate, gain[None], weight)


def scatter_groups(array, groups):
    return lax.psum_scatter(array, "seq", scatter_dimension=0, axis_index_groups=groups)


def shards(
    block_input,
    segment_ids,
    norm1_gain,
    in_weight,
    conv_weight,
    out_weight,
    norm2_gain,
    ffn_in_weight,
    ffn_out_weight,
    out_grad,
):
    x = lax.axis_index("ch")
    seq = lax.axis_index("seq")
    core, z, y = seq % 2, (seq // 2) % 4, seq // 8
    features = norm1_gain.shape[0]
    width = block_input.shape[1]
    hidden_units = ffn_out_weight.shape[1]

    def rolled(array):
        blocks = array.reshape((CH, width) + array.shape[1:])
        return jnp.concatenate([pick(blocks, (x + j) % CH, 0) for j in range(CH)], axis=0)

    count = first_count(segment_ids)
    at = jnp.stack([x, core, count, z, y]).astype(jnp.int32)
    own_one = pick(norm1_gain.reshape(CH, width), x, 0)
    own_two = pick(norm2_gain.reshape(CH, width), x, 0)
    in_planes = jnp.transpose(in_weight, (1, 0, 2))

    pieces = gather_ch(block_input)
    half_rows = out_weight.shape[0] // 2
    half = lax.dynamic_slice_in_dim(out_weight, core * half_rows, half_rows, 0)
    half_pieces = gather_ch(half)
    grad_full = lax.all_gather(out_grad, "ch", axis=1, tiled=True)
    ffn_planes = jnp.transpose(ffn_in_weight, (1, 0, 2))
    ffn_planes, *pieces = tie(ffn_planes, *pieces)

    normed_one, r_one, b_gate, c_gate, value_rows, gated_rows = in_project(
        at, pieces, norm1_gain, in_planes
    )
    own_rows = block_input.astype(F32)
    carried = from_behind(gated_rows[-2:], "seq", 1)
    extended = jnp.concatenate([carried, gated_rows], axis=0).astype(F32)
    same_one, same_two = tap_masks(count, block_input.shape[0])
    current = extended[2:]
    prior_one = extended[1:-1] * same_one
    prior_two = extended[:-2] * same_two
    conv_out = conv_weight[0] * current + conv_weight[1] * prior_one + conv_weight[2] * prior_two
    mixed_rows = (c_gate * conv_out).astype(BF16)

    mixed_pieces = gather_ch(mixed_rows)
    half_pieces = tie(*half_pieces, mixed_rows)[:CH]
    half_full = jnp.concatenate(half_pieces, axis=1)
    other_half = lax.ppermute(half_full, "seq", seq_pairs(0, 0, 1))
    (
        hidden,
        r_two,
        normed_two,
        act_rows,
        d_gate_up,
        d_own,
        d_one,
        d_two,
        d_three,
    ) = ffn(
        at,
        pieces,
        mixed_pieces,
        norm2_gain,
        half_full,
        other_half,
        ffn_planes,
        ffn_out_weight,
        grad_full,
    )
    hidden_own = hidden[:, :width]
    d_normed_own = scatter_ch([d_own, d_one, d_two, d_three])
    down_terms = jnp.einsum(
        "tf,ef->te", act_rows, ffn_out_weight, preferred_element_type=F32
    ).astype(BF16)
    down = lax.psum_scatter(down_terms, "ch", scatter_dimension=1, tiled=True)
    *gives, keep = pair_products(at, normed_two, d_gate_up, grad_full, act_rows, True, False)
    got = swap_cores(gives)

    grad_gain_two = jnp.sum(d_normed_own * hidden_own * r_two, axis=0)
    u_own = out_grad.astype(F32) + r_two * own_two * d_normed_own
    u_pieces = [u_own] + gather_ch(u_own.astype(BF16))[1:]
    ffn_kept = add_cores(keep, got)
    ffn_kept, *u_pieces = tie(ffn_kept, *u_pieces)
    groups = [[seq_index(i, k, c) for k in range(4)] for i in range(4) for c in range(2)]
    ffn_sum = scatter_groups(ffn_kept, groups)

    d_branch, d_hidden, d_conv, d_cgate = mid(
        at, u_pieces, hidden, r_two, grad_full, out_weight, c_gate, conv_out
    )
    following = from_behind(d_conv[:2], "seq", -1)
    d_proj, d_own, d_one, d_two, d_three, inner = back_project(
        at, pieces, d_conv, following, conv_weight, value_rows, b_gate, d_cgate, norm1_gain,
        in_planes,
    )
    received = [lax.ppermute(d, "ch", ch_pairs(j)) for j, d in ((1, d_one), (2, d_two), (3, d_three))]

    *gives, keep = pair_products(at, normed_one, d_proj, d_branch, mixed_rows, True, True)
    got = swap_cores(gives)
    grad_conv = jnp.stack(
        [
            jnp.sum(d_conv * current, axis=0),
            jnp.sum(d_conv * prior_one, axis=0),
            jnp.sum(d_conv * prior_two, axis=0),
        ],
        axis=0,
    )
    input_grad, grad_gain_one = end(
        d_own, received, inner, d_hidden, block_input, r_one, own_one
    )
    small = jnp.concatenate(
        [grad_conv, grad_gain_one, grad_gain_two[None], jnp.zeros((3, width), F32)], axis=0
    )
    small = small + lax.ppermute(small, "seq", seq_pairs(0, 0, 1))
    own, *messages = send_z(at, keep, got, small)
    messages = [
        lax.ppermute(m, "seq", seq_pairs(0, j, 0)) for j, m in ((1, messages[0]), (2, messages[1]), (3, messages[2]))
    ]
    down, ffn_sum, *messages = tie(down, ffn_sum, *messages)
    block_output = (hidden_own + down.astype(F32)).astype(BF16)
    own, *messages, small = turn(at, own, messages, small)
    messages = [
        lax.ppermute(m, "seq", seq_pairs(j, 0, 0)) for j, m in ((1, messages[0]), (2, messages[1]), (3, messages[2]))
    ]
    grad_in, grad_out, small = last(own, messages, small)

    groups = [[seq_index(k, i, c) for k in range(4)] for i in range(4) for c in range(2)]
    ffn_sum = scatter_groups(ffn_sum, groups).astype(F32)
    grad_ffn_in = ffn_sum[:, : 2 * hidden_units].reshape(-1, 2, hidden_units)
    grad_ffn_out = ffn_sum[:, 2 * hidden_units :]
    return (
        block_output,
        input_grad,
        small[3],
        jnp.transpose(grad_in, (1, 0, 2)),
        small[:3],
        grad_out,
        small[4],
        grad_ffn_in,
        grad_ffn_out,
    )


def solution(mesh):
    return jax.shard_map(
        shards,
        mesh=mesh,
        in_specs=(
            P("seq", "ch"),
            P("seq"),
            P(),
            P(None, None, "ch"),
            P(None, "ch"),
            P(None, "ch"),
            P(),
            P(None, None, "ch"),
            P(None, "ch"),
            P("seq", "ch"),
        ),
        out_specs=(
            P("seq", "ch"),
            P("seq", "ch"),
            P("ch"),
            P("seq", None, "ch"),
            P(None, "ch"),
            P("seq", "ch"),
            P("ch"),
            P("seq", None, "ch"),
            P("seq", "ch"),
        ),
        check_vma=False,
    )
```

```python
import jax
import jax.numpy as jnp
from jax import lax
from jax.experimental import pallas as pl
from jax.experimental.pallas import tpu as pltpu
from jax.sharding import PartitionSpec as P

EPS = 1e-05
F32 = jnp.float32
BF16 = jnp.bfloat16
CH = 4
LONG = 2**36


def seq_index(y, z, core):
    return ((y % 4) * 4 + z % 4) * 2 + core


def seq_pairs(dy, dz, dcore):
    return [
        (seq_index(y, z, core), seq_index(y + dy, z + dz, core ^ dcore))
        for y in range(4)
        for z in range(4)
        for core in range(2)
    ]


def ch_pairs(step):
    return [(i, (i + step) % CH) for i in range(CH)]


def gather_ch(block):
    return [block] + [lax.ppermute(block, "ch", ch_pairs(-j)) for j in range(1, CH)]


def scatter_ch(chunks):
    total = chunks[0]
    for j in range(1, CH):
        total = total + lax.ppermute(chunks[j], "ch", ch_pairs(j)).astype(F32)
    return total


def sum_ch(vector):
    total = vector
    for j in range(1, CH):
        total = total + lax.ppermute(vector, "ch", ch_pairs(j))
    return total


def pick(array, index, axis):
    return lax.dynamic_index_in_dim(array, index, axis, keepdims=False)


def from_behind(array, axis, by):
    size = lax.axis_size(axis)
    pairs = [(i, i + by) for i in range(size) if 0 <= i + by < size]
    return lax.ppermute(array, axis, pairs)


def first_count(segment_ids):
    return jnp.sum((segment_ids == segment_ids[0]).astype(jnp.int32))


def tap_masks(count, rows):
    token = lax.broadcasted_iota(jnp.int32, (rows, 1), 0)
    same_one = (token != count).astype(F32)
    same_two = ((token != count) & (token != count + 1)).astype(F32)
    return (same_one, same_two)


def tie(*arrays):
    return lax.optimization_barrier(arrays)


def reduce_axis(array, axis, me, along_y):
    total = pick(array, me, axis).astype(F32)
    for step in (1, 3, 2):
        pairs = seq_pairs(step, 0, 0) if along_y else seq_pairs(0, step, 0)
        total = total + lax.ppermute(pick(array, (me + step) % 4, axis), "seq", pairs).astype(F32)
    return total


def dot_nt(a, b):
    return lax.dot_general(a, b, (((1,), (1,)), ((), ())), preferred_element_type=F32)


def dot_tn(a, b):
    return lax.dot_general(a, b, (((0,), (0,)), ((), ())), preferred_element_type=F32)


def dot_nn(a, b):
    return lax.dot_general(a, b, (((1,), (0,)), ((), ())), preferred_element_type=F32)


def rel_rows(x, j, width):
    return pl.ds(pl.multiple_of(lax.rem(x + j, CH) * width, width), width)


def vmem():
    return pl.BlockSpec(memory_space=pltpu.VMEM)


def smem():
    return pl.BlockSpec(memory_space=pltpu.SMEM)


def anywhere():
    return pl.BlockSpec(memory_space=pl.ANY)


def shape(dims, dtype):
    return jax.ShapeDtypeStruct(dims, dtype)


def params(megabytes):
    return pltpu.CompilerParams(vmem_limit_bytes=megabytes * 1024 * 1024)


def cost(macs, nbytes):
    return pl.CostEstimate(flops=2 * macs, bytes_accessed=nbytes, transcendentals=0)


def in_kernel(at, p0, p1, p2, p3, gain, weight, normed, rms, b_out, c_out, v_out, gated, held, sem):
    x = at[0]
    width = p0.shape[1]
    copies = [
        pltpu.make_async_copy(
            weight.at[:, rel_rows(x, j, width), :],
            held.at[:, pl.ds(j * width, width), :],
            sem.at[j],
        )
        for j in range(CH)
    ]
    for copy in copies:
        copy.start()
    pieces = [p0, p1, p2, p3]
    square = jnp.zeros((p0.shape[0], 1), F32)
    for piece in pieces:
        rows = piece[...].astype(F32)
        square = square + jnp.sum(rows * rows, axis=1, keepdims=True)
    r = lax.rsqrt(square / (CH * width) + EPS)
    rms[...] = r
    for j, piece in enumerate(pieces):
        scale = gain[:, rel_rows(x, j, width)]
        normed[:, j * width : (j + 1) * width] = (piece[...].astype(F32) * r * scale).astype(BF16)
    for copy in copies:
        copy.wait()
    b = dot_nn(normed[...], held[0])
    v = dot_nn(normed[...], held[2])
    b_out[...] = b
    v_out[...] = v
    gated[...] = (b * v).astype(BF16)
    c_out[...] = dot_nn(normed[...], held[1])


def in_project(at, pieces, gain, weight):
    rows, width = pieces[0].shape
    features = CH * width
    out = shape((rows, width), F32)
    return pl.pallas_call(
        in_kernel,
        out_shape=(
            shape((rows, features), BF16),
            shape((rows, 1), F32),
            out,
            out,
            out,
            shape((rows, width), BF16),
        ),
        in_specs=[smem()] + [vmem()] * 5 + [anywhere()],
        out_specs=(vmem(),) * 6,
        scratch_shapes=[
            pltpu.VMEM((3, features, width), BF16),
            pltpu.SemaphoreType.DMA((CH,)),
        ],
        compiler_params=params(16),
        cost_estimate=cost(rows * features * 3 * width, 6 * 2**20),
    )(at, *pieces, gain[None], weight)


def columns_kernel(p0, p1, p2, p3, out):
    width = p0.shape[1]
    for j, piece in enumerate((p0, p1, p2, p3)):
        out[:, j * width : (j + 1) * width] = piece[...]


def join_columns(pieces, weight):
    rows, width = pieces[0].shape
    return pl.pallas_call(
        columns_kernel,
        out_shape=shape((rows, CH * width), BF16),
        in_specs=[vmem()] * CH,
        out_specs=vmem(),
        compiler_params=params(8),
        cost_estimate=cost(weight, 2**21),
    )(*pieces)


def ffn_kernel(
    at,
    x0, x1, x2, x3,
    mixed,
    gain,
    half,
    other,
    planes,
    down,
    cotangent,
    h, rms, normed, act, d_gate_up, d_own, d1, d2, d3, down_out,
    w_out, w_in, w_down, g_rows, acc, down_acc, sem,
):
    x, core = at[0], at[1]
    width = x0.shape[1]
    units = down.shape[1]
    step = units // 3
    halves = [
        pltpu.make_async_copy(half, w_out.at[0], sem.at[0]),
        pltpu.make_async_copy(other, w_out.at[1], sem.at[1]),
    ]
    planes_in = [
        pltpu.make_async_copy(
            planes.at[:, rel_rows(x, j, width), :],
            w_in.at[:, pl.ds(j * width, width), :],
            sem.at[2 + j],
        )
        for j in range(CH)
    ]
    rest = [
        pltpu.make_async_copy(cotangent, g_rows, sem.at[6]),
        pltpu.make_async_copy(down, w_down, sem.at[7]),
    ]
    for copy in halves + planes_in + rest:
        copy.start()
    for copy in halves:
        copy.wait()
    square = jnp.zeros((x0.shape[0], 1), F32)
    for j, piece in enumerate((x0, x1, x2, x3)):
        block = lax.rem(x + j, CH)
        which = lax.rem(block // 2 + core, 2)
        rows = pl.ds(pl.multiple_of(lax.rem(block, 2) * width, width), width)
        hj = piece[...].astype(F32) + dot_nt(mixed[...], w_out[which, rows, :])
        h[:, j * width : (j + 1) * width] = hj
        square = square + jnp.sum(hj * hj, axis=1, keepdims=True)
    r = lax.rsqrt(square / (CH * width) + EPS)
    rms[...] = r
    for j in range(CH):
        columns = slice(j * width, (j + 1) * width)
        scale = gain[:, rel_rows(x, j, width)]
        normed[:, columns] = (h[:, columns] * r * scale).astype(BF16)
    for copy in planes_in + rest:
        copy.wait()

    def part(i, carry):
        f = pl.ds(pl.multiple_of(i * step, 128), step)
        f_up = pl.ds(pl.multiple_of(units + i * step, 128), step)
        gate = dot_nn(normed[...], w_in[0, :, f])
        up = dot_nn(normed[...], w_in[1, :, f])
        d_act = dot_nn(g_rows[...], w_down[:, f])
        sigma = jax.nn.sigmoid(gate)
        swish = gate * sigma
        active = (swish * up).astype(BF16)
        act[:, f] = active
        for j in range(CH):
            rows = slice(j * width, (j + 1) * width)
            term = dot_nt(active, w_down[rows, f])
            down_acc[j] = jnp.where(i == 0, term, down_acc[j] + term)
        d_gate = (d_act * up * sigma * (1.0 + gate * (1.0 - sigma))).astype(BF16)
        d_up = (d_act * swish).astype(BF16)
        d_gate_up[:, f] = d_gate
        d_gate_up[:, f_up] = d_up
        for j in range(CH):
            rows = slice(j * width, (j + 1) * width)
            term = dot_nt(d_gate, w_in[0, rows, f]) + dot_nt(d_up, w_in[1, rows, f])
            acc[j] = jnp.where(i == 0, term, acc[j] + term)
        return carry

    lax.fori_loop(0, 3, part, 0)
    d_own[...] = acc[0]
    d1[...] = acc[1].astype(BF16)
    d2[...] = acc[2].astype(BF16)
    d3[...] = acc[3].astype(BF16)
    for j in range(CH):
        down_out[:, j * width : (j + 1) * width] = down_acc[j].astype(BF16)


def ffn(at, pieces, mixed, gain, half, other, planes, down, cotangent):
    rows, width = pieces[0].shape
    features = CH * width
    units = down.shape[1]
    block = shape((rows, width), BF16)
    return pl.pallas_call(
        ffn_kernel,
        out_shape=(
            shape((rows, features), F32),
            shape((rows, 1), F32),
            shape((rows, features), BF16),
            shape((rows, units), BF16),
            shape((rows, 2 * units), BF16),
            shape((rows, width), F32),
            block,
            block,
            block,
            shape((rows, features), BF16),
        ),
        in_specs=[smem()] + [vmem()] * 6 + [anywhere()] * 5,
        out_specs=(vmem(),) * 10,
        scratch_shapes=[
            pltpu.VMEM((2, features // 2, features), BF16),
            pltpu.VMEM((2, features, units), BF16),
            pltpu.VMEM((features, units), BF16),
            pltpu.VMEM((rows, features), BF16),
            pltpu.VMEM((CH, rows, width), F32),
            pltpu.VMEM((CH, rows, width), F32),
            pltpu.SemaphoreType.DMA((8,)),
        ],
        compiler_params=params(34),
        cost_estimate=cost(rows * features * (features + 6 * units), 20 * 2**20),
    )(at, *pieces, mixed, gain[None], half, other, planes, down, cotangent)


def pair_kernel(
    at, a_left, a_right, b_left, b_right, give_a, give_b, keep, held, *, a_rolled, b_rolled
):
    x, core = at[0], at[1]
    y = pl.program_id(0)
    wide = keep.shape[2] * 8
    turned = lax.rem(y + CH - x, CH)
    cut = a_right.shape[1]
    for left, right, rolled, base in (
        (a_left, a_right, a_rolled, 0),
        (b_left, b_right, b_rolled, cut),
    ):
        where = turned if rolled else y
        block = left[:, pl.ds(pl.multiple_of(where * wide, wide), wide)]
        columns = right.shape[1]
        step = columns // 3 if columns % 384 == 0 else columns
        for first in range(0, columns, step):
            held[:, base + first : base + first + step] = dot_tn(
                block, right[:, first : first + step]
            )
    for z in range(4):
        mine = pl.multiple_of((2 * z + core) * 32, 32)
        theirs = pl.multiple_of((2 * z + 1 - core) * 32, 32)
        keep[z, 0] = held[pl.ds(mine, 32), :].astype(BF16)
        (give_a, give_b)[z // 2][z % 2, 0] = held[pl.ds(theirs, 32), :].astype(BF16)


def pair_products(at, a_left, a_right, b_left, b_right, a_rolled, b_rolled):
    columns = a_right.shape[1] + b_right.shape[1]
    tokens, features = a_left.shape
    out = shape((4, 4, features // 32, columns), BF16)
    spec = pl.BlockSpec((4, 1, features // 32, columns), lambda y: (0, y, 0, 0))
    half = shape((2, 4, features // 32, columns), BF16)
    half_spec = pl.BlockSpec((2, 1, features // 32, columns), lambda y: (0, y, 0, 0))

    def body(*refs):
        pair_kernel(*refs, a_rolled=a_rolled, b_rolled=b_rolled)

    return pl.pallas_call(
        body,
        grid=(4,),
        out_shape=(half, half, out),
        in_specs=[smem()] + [vmem()] * 4,
        out_specs=(half_spec, half_spec, spec),
        scratch_shapes=[pltpu.VMEM((features // 4, columns), F32)],
        compiler_params=params(22),
        cost_estimate=cost(tokens * features * columns, 4 * features * columns),
    )(at, a_left, a_right, b_left, b_right)


def swap_cores(halves):
    return [lax.ppermute(half, "seq", seq_pairs(0, 0, 1)) for half in halves]


def add_kernel(keep, got_a, got_b, out):
    out[:2] = (keep[:2].astype(F32) + got_a[...].astype(F32)).astype(BF16)
    out[2:] = (keep[2:].astype(F32) + got_b[...].astype(F32)).astype(BF16)


def add_cores(keep, got):
    spec = pl.BlockSpec((4, 1) + keep.shape[2:], lambda y: (0, y, 0, 0))
    half = pl.BlockSpec((2, 1) + keep.shape[2:], lambda y: (0, y, 0, 0))
    return pl.pallas_call(
        add_kernel,
        grid=(4,),
        out_shape=shape(keep.shape, BF16),
        in_specs=[spec, half, half],
        out_specs=spec,
        compiler_params=params(16),
        cost_estimate=cost(2**20, 6 * keep.size),
    )(keep, *got)


def spread(small):
    high = small.astype(BF16)
    low = (small - high.astype(F32)).astype(BF16)
    return high, low


def join(message, width):
    return message[:8, :width].astype(F32) + message[:8, width : 2 * width].astype(F32)


def send_kernel(at, keep, got_a, got_b, small, own, m1, m2, m3):
    z = at[3]
    rows = own.shape[0]
    width = small.shape[1]
    for j, out in enumerate((own, m1, m2, m3)):
        block = lax.rem(z + j, 4)
        inside = lax.rem(block, 2)
        got = jnp.where(block < 2, got_a[inside].astype(F32), got_b[inside].astype(F32))
        total = keep[block].astype(F32) + got
        out[:rows] = total.reshape(own.shape).astype(out.dtype)
    high, low = spread(jnp.concatenate([small[...], jnp.zeros_like(small[...])], axis=0))
    for out in (m1, m2, m3):
        out[rows:, :width] = high
        out[rows:, width : 2 * width] = low


def send_z(at, keep, got, small):
    rows, columns = keep.shape[1] * keep.shape[2], keep.shape[3]
    message = shape((rows + 16, columns), BF16)
    return pl.pallas_call(
        send_kernel,
        out_shape=(shape((rows, columns), F32), message, message, message),
        in_specs=[smem()] + [vmem()] * 4,
        out_specs=(vmem(),) * 4,
        compiler_params=params(16),
        cost_estimate=cost(2**20, 2**22),
    )(at, keep, *got, small)


def turn_kernel(at, own, m1, m2, m3, small, left, n1, n2, n3, small_out, total):
    y = at[4]
    rows = own.shape[0]
    width = small.shape[1]
    total[...] = own[...]
    small_sum = small[...]
    for m in (m1, m2, m3):
        total[...] += m[:rows].astype(F32)
        small_sum = small_sum + join(m[rows:], width)
    small_out[...] = small_sum
    part = rows // 4
    for j, out in enumerate((left, n1, n2, n3)):
        block = pl.multiple_of(lax.rem(y + j, 4) * part, part)
        out[:part] = total[pl.ds(block, part)].astype(out.dtype)
    high, low = spread(jnp.concatenate([small_sum, jnp.zeros_like(small_sum)], axis=0))
    for out in (n1, n2, n3):
        out[part:, :width] = high
        out[part:, width : 2 * width] = low


def turn(at, own, messages, small):
    rows, columns = own.shape
    message = shape((rows // 4 + 16, columns), BF16)
    return pl.pallas_call(
        turn_kernel,
        out_shape=(
            shape((rows // 4, columns), F32),
            message,
            message,
            message,
            shape(small.shape, F32),
        ),
        in_specs=[smem()] + [vmem()] * 5,
        out_specs=(vmem(),) * 5,
        scratch_shapes=[pltpu.VMEM((rows, columns), F32)],
        compiler_params=params(16),
        cost_estimate=cost(2**20, 2**21),
    )(at, own, *messages, small)


def last_kernel(own, m1, m2, m3, small, in_out, out_out, small_out):
    rows = own.shape[0]
    width = small.shape[1]
    total = own[...]
    small_sum = small[...]
    for m in (m1, m2, m3):
        total = total + m[:rows].astype(F32)
        small_sum = small_sum + join(m[rows:], width)
    for k in range(3):
        in_out[k] = total[:, k * width : (k + 1) * width]
    out_out[...] = total[:, 3 * width :]
    small_out[...] = small_sum


def last(own, messages, small):
    rows, columns = own.shape
    width = small.shape[1]
    return pl.pallas_call(
        last_kernel,
        out_shape=(
            shape((3, rows, width), F32),
            shape((rows, columns - 3 * width), F32),
            shape(small.shape, F32),
        ),
        in_specs=[vmem()] * 5,
        out_specs=(vmem(),) * 3,
        compiler_params=params(16),
        cost_estimate=cost(2**20, 2**20),
    )(own, *messages, small)


def end_kernel(d_own, d1, d2, d3, inner, d_hidden, rows_in, rms, gain, grad, gain_grad):
    rows, width = d_own.shape
    total = d_own[...]
    line = inner[...]
    for d in (d1, d2, d3):
        total = total + d[:rows].astype(F32)
        high = [d[rows + 16 * i : rows + 16 * (i + 1)].astype(F32) for i in range(4)]
        line = line + jnp.concatenate(
            [high[0] + high[2], high[1] + high[3]], axis=1
        )
    column = lax.dot_general(
        line, jnp.full((16, width), 1.0 / 16, F32), (((0,), (0,)), ((), ())),
        precision=lax.Precision.HIGHEST, preferred_element_type=F32,
    )
    r = rms[...]
    xs = rows_in[...].astype(F32)
    gain_grad[...] = jnp.sum(total * xs * r, axis=0, keepdims=True)
    grad[...] = (
        d_hidden[...] + r * gain[...] * total - xs * (r * r * r / (CH * width)) * column
    ).astype(BF16)


def end(d_own, received, inner, d_hidden, rows_in, rms, gain):
    rows, width = d_own.shape
    return pl.pallas_call(
        end_kernel,
        out_shape=(shape((rows, width), BF16), shape((1, width), F32)),
        in_specs=[vmem()] * 9,
        out_specs=(vmem(),) * 2,
        compiler_params=params(16),
        cost_estimate=cost(2**32, 2**21),
    )(d_own, *received, inner, d_hidden, rows_in, rms, gain[None])


def norm_kernel(d_own, d1, d2, d3, h, rms, gain, cotangent, u, u_low, gain_grad):
    total = d_own[...]
    for d in (d1, d2, d3):
        total = total + d[...].astype(F32)
    r = rms[...]
    gain_grad[...] = jnp.sum(total * h[...] * r, axis=0, keepdims=True)
    full = cotangent[...].astype(F32) + r * gain[...] * total
    u[...] = full
    u_low[...] = full.astype(BF16)


def norm_back(d_own, received, h, rms, gain, cotangent):
    rows, width = d_own.shape
    return pl.pallas_call(
        norm_kernel,
        out_shape=(
            shape((rows, width), F32),
            shape((rows, width), BF16),
            shape((1, width), F32),
        ),
        in_specs=[vmem()] * 8,
        out_specs=(vmem(),) * 3,
        compiler_params=params(10),
        cost_estimate=cost(LONG, 2**21),
    )(d_own, *received, h, rms, gain[None], cotangent)


def mid_kernel(
    at, u_own, u1, u2, u3, h, rms, cotangent, weight, c_gate, conv_out,
    d_branch, d_hidden, d_conv, d_cgate,
):
    x = at[0]
    width = u_own.shape[1]
    dot = jnp.zeros((u_own.shape[0], 1), F32)
    us = (u_own, u1, u2, u3)
    for j, u in enumerate(us):
        g = cotangent[:, rel_rows(x, j, width)].astype(F32)
        hj = h[:, j * width : (j + 1) * width]
        dot = dot + jnp.sum((u[...].astype(F32) - g) * hj, axis=1, keepdims=True)
    r = rms[...]
    scale = dot * (r * r / (CH * width))
    d_mixed = jnp.zeros(u_own.shape, F32)
    for j, u in enumerate(us):
        columns = slice(j * width, (j + 1) * width)
        full = u[...].astype(F32) - h[:, columns] * scale
        if j == 0:
            d_hidden[...] = full
        rounded = full.astype(BF16)
        d_branch[:, columns] = rounded
        d_mixed = d_mixed + dot_nn(rounded, weight[rel_rows(x, j, width), :])
    d_conv[...] = d_mixed * c_gate[...]
    d_cgate[...] = (d_mixed * conv_out[...]).astype(BF16)


def mid(at, pieces, h, rms, cotangent, weight, c_gate, conv_out):
    rows, width = c_gate.shape
    wide = shape((rows, width), F32)
    return pl.pallas_call(
        mid_kernel,
        out_shape=(shape((rows, CH * width), BF16), wide, wide, shape((rows, width), BF16)),
        in_specs=[smem()] + [vmem()] * 10,
        out_specs=(vmem(),) * 4,
        compiler_params=params(16),
        cost_estimate=cost(rows * CH * width * width, 6 * 2**20),
    )(at, *pieces, h, rms, cotangent, weight, c_gate, conv_out)


def back_kernel(
    at, p0, p1, p2, p3, d_conv, following, taps, value, b_gate, d_cgate, gain, weight,
    grads, d_own, d1, d2, d3, inner, held, sem,
):
    x, count = at[0], at[2]
    rows, width = p0.shape
    copies = [
        pltpu.make_async_copy(
            weight.at[:, rel_rows(x, j, width), :],
            held.at[:, pl.ds(j * width, width), :],
            sem.at[j],
        )
        for j in range(CH)
    ]
    for copy in copies:
        copy.start()
    token = lax.broadcasted_iota(jnp.int32, (rows, width), 0)
    d = d_conv[...]
    next_one, next_two = following[0:1, :], following[1:2, :]
    after_one = jnp.where(token + 1 == count, 0.0, pltpu.roll(d, rows - 1, 0))
    after_one = jnp.where(token == rows - 1, next_one, after_one)
    after_two = pltpu.roll(d, rows - 2, 0)
    after_two = jnp.where((token + 2 == count) | (token + 1 == count), 0.0, after_two)
    after_two = jnp.where(token == rows - 2, next_one, after_two)
    after_two = jnp.where(token == rows - 1, next_two, after_two)
    d_gated = taps[0:1, :] * d + taps[1:2, :] * after_one + taps[2:3, :] * after_two
    grads[:, :width] = (d_gated * value[...]).astype(BF16)
    grads[:, width : 2 * width] = d_cgate[...]
    grads[:, 2 * width :] = (d_gated * b_gate[...]).astype(BF16)
    total = jnp.zeros((rows, width), F32)
    for j, piece in enumerate((p0, p1, p2, p3)):
        copies[j].wait()
        block = slice(j * width, (j + 1) * width)
        term = dot_nt(grads[:, :width], held[0, block, :])
        for k in (1, 2):
            term = term + dot_nt(grads[:, k * width : (k + 1) * width], held[k, block, :])
        scale = gain[:, rel_rows(x, j, width)]
        total = total + scale * term * piece[...].astype(F32)
        if j == 0:
            d_own[...] = term
        else:
            (d1, d2, d3)[j - 1][:rows, :] = term.astype(BF16)
    ones = jnp.ones((16, width), F32)
    row = lax.dot_general(
        ones, total, (((1,), (1,)), ((), ())),
        precision=lax.Precision.HIGHEST, preferred_element_type=F32,
    )
    inner[...] = row
    high = row.astype(BF16)
    low = (row - high.astype(F32)).astype(BF16)
    for out in (d1, d2, d3):
        out[rows : rows + 16, :] = high[:, :width]
        out[rows + 16 : rows + 32, :] = high[:, width:]
        out[rows + 32 : rows + 48, :] = low[:, :width]
        out[rows + 48 : rows + 64, :] = low[:, width:]


def back_project(at, pieces, d_conv, following, taps, value, b_gate, d_cgate, gain, weight):
    rows, width = pieces[0].shape
    features = CH * width
    block = shape((rows + 64, width), BF16)
    return pl.pallas_call(
        back_kernel,
        out_shape=(
            shape((rows, 3 * width), BF16),
            shape((rows, width), F32),
            block,
            block,
            block,
            shape((16, rows), F32),
        ),
        in_specs=[smem()] + [vmem()] * 11 + [anywhere()],
        out_specs=(vmem(),) * 6,
        scratch_shapes=[
            pltpu.VMEM((3, features, width), BF16),
            pltpu.SemaphoreType.DMA((CH,)),
        ],
        compiler_params=params(18),
        cost_estimate=cost(rows * features * 3 * width, 6 * 2**20),
    )(at, *pieces, d_conv, following, taps, value, b_gate, d_cgate, gain[None], weight)


def scatter_groups(array, groups):
    return lax.psum_scatter(array, "seq", scatter_dimension=0, axis_index_groups=groups)


def shards(
    block_input,
    segment_ids,
    norm1_gain,
    in_weight,
    conv_weight,
    out_weight,
    norm2_gain,
    ffn_in_weight,
    ffn_out_weight,
    out_grad,
):
    x = lax.axis_index("ch")
    seq = lax.axis_index("seq")
    core, z, y = seq % 2, (seq // 2) % 4, seq // 8
    features = norm1_gain.shape[0]
    width = block_input.shape[1]
    hidden_units = ffn_out_weight.shape[1]

    def rolled(array):
        blocks = array.reshape((CH, width) + array.shape[1:])
        return jnp.concatenate([pick(blocks, (x + j) % CH, 0) for j in range(CH)], axis=0)

    count = first_count(segment_ids)
    at = jnp.stack([x, core, count, z, y]).astype(jnp.int32)
    own_one = pick(norm1_gain.reshape(CH, width), x, 0)
    own_two = pick(norm2_gain.reshape(CH, width), x, 0)
    in_planes = jnp.transpose(in_weight, (1, 0, 2))

    pieces = gather_ch(block_input)
    half_rows = out_weight.shape[0] // 2
    half = lax.dynamic_slice_in_dim(out_weight, core * half_rows, half_rows, 0)
    half_pieces = gather_ch(half)
    grad_full = lax.all_gather(out_grad, "ch", axis=1, tiled=True)

    normed_one, r_one, b_gate, c_gate, value_rows, gated_rows = in_project(
        at, pieces, norm1_gain, in_planes
    )
    own_rows = block_input.astype(F32)
    carried = from_behind(gated_rows[-2:], "seq", 1)
    extended = jnp.concatenate([carried, gated_rows], axis=0).astype(F32)
    same_one, same_two = tap_masks(count, block_input.shape[0])
    current = extended[2:]
    prior_one = extended[1:-1] * same_one
    prior_two = extended[:-2] * same_two
    conv_out = conv_weight[0] * current + conv_weight[1] * prior_one + conv_weight[2] * prior_two
    mixed_rows = (c_gate * conv_out).astype(BF16)

    mixed_pieces = gather_ch(mixed_rows)
    *half_pieces, ffn_weight, _ = tie(*half_pieces, ffn_in_weight, mixed_rows)
    ffn_planes = jnp.transpose(ffn_weight, (1, 0, 2))
    half_full = join_columns(half_pieces, 2**20)
    mixed_full = join_columns(mixed_pieces, 2**32)
    ffn_planes, mixed_full = tie(ffn_planes, mixed_full)
    other_half = lax.ppermute(half_full, "seq", seq_pairs(0, 0, 1))
    (
        hidden,
        r_two,
        normed_two,
        act_rows,
        d_gate_up,
        d_own,
        d_one,
        d_two,
        d_three,
        down_terms,
    ) = ffn(
        at,
        pieces,
        mixed_full,
        norm2_gain,
        half_full,
        other_half,
        ffn_planes,
        ffn_out_weight,
        grad_full,
    )
    hidden_own = hidden[:, :width]
    received = [
        lax.ppermute(d, "ch", ch_pairs(j)) for j, d in ((1, d_one), (2, d_two), (3, d_three))
    ]
    down = lax.psum_scatter(down_terms, "ch", scatter_dimension=1, tiled=True)
    *gives, keep = pair_products(at, normed_two, d_gate_up, grad_full, act_rows, True, False)
    got = swap_cores(gives)

    u_own, u_low, grad_gain_two = norm_back(
        d_own, received, hidden_own, r_two, own_two, out_grad
    )
    u_pieces = [u_own] + gather_ch(u_low)[1:]
    ffn_kept = add_cores(keep, got)
    ffn_kept, *u_pieces = tie(ffn_kept, *u_pieces)
    groups = [[seq_index(i, k, c) for k in range(4)] for i in range(4) for c in range(2)]
    ffn_sum = scatter_groups(ffn_kept, groups)

    d_branch, d_hidden, d_conv, d_cgate = mid(
        at, u_pieces, hidden, r_two, grad_full, out_weight, c_gate, conv_out
    )
    following = from_behind(d_conv[:2], "seq", -1)
    d_proj, d_own, d_one, d_two, d_three, inner = back_project(
        at, pieces, d_conv, following, conv_weight, value_rows, b_gate, d_cgate, norm1_gain,
        in_planes,
    )
    received = [lax.ppermute(d, "ch", ch_pairs(j)) for j, d in ((1, d_one), (2, d_two), (3, d_three))]

    *gives, keep = pair_products(at, normed_one, d_proj, d_branch, mixed_rows, True, True)
    got = swap_cores(gives)
    grad_conv = jnp.stack(
        [
            jnp.sum(d_conv * current, axis=0),
            jnp.sum(d_conv * prior_one, axis=0),
            jnp.sum(d_conv * prior_two, axis=0),
        ],
        axis=0,
    )
    input_grad, grad_gain_one = end(
        d_own, received, inner, d_hidden, block_input, r_one, own_one
    )
    small = jnp.concatenate(
        [grad_conv, grad_gain_one, grad_gain_two, jnp.zeros((3, width), F32)], axis=0
    )
    small = small + lax.ppermute(small, "seq", seq_pairs(0, 0, 1))
    own, *messages = send_z(at, keep, got, small)
    messages = [
        lax.ppermute(m, "seq", seq_pairs(0, j, 0)) for j, m in ((1, messages[0]), (2, messages[1]), (3, messages[2]))
    ]
    down, ffn_sum, *messages = tie(down, ffn_sum, *messages)
    block_output = (hidden_own + down.astype(F32)).astype(BF16)
    own, *messages, small = turn(at, own, messages, small)
    messages = [
        lax.ppermute(m, "seq", seq_pairs(j, 0, 0)) for j, m in ((1, messages[0]), (2, messages[1]), (3, messages[2]))
    ]
    grad_in, grad_out, small = last(own, messages, small)

    groups = [[seq_index(k, i, c) for k in range(4)] for i in range(4) for c in range(2)]
    ffn_sum = scatter_groups(ffn_sum, groups).astype(F32)
    grad_ffn_in = ffn_sum[:, : 2 * hidden_units].reshape(-1, 2, hidden_units)
    grad_ffn_out = ffn_sum[:, 2 * hidden_units :]
    return (
        block_output,
        input_grad,
        small[3],
        jnp.transpose(grad_in, (1, 0, 2)),
        small[:3],
        grad_out,
        small[4],
        grad_ffn_in,
        grad_ffn_out,
    )


def solution(mesh):
    return jax.shard_map(
        shards,
        mesh=mesh,
        in_specs=(
            P("seq", "ch"),
            P("seq"),
            P(),
            P(None, None, "ch"),
            P(None, "ch"),
            P(None, "ch"),
            P(),
            P(None, None, "ch"),
            P(None, "ch"),
            P("seq", "ch"),
        ),
        out_specs=(
            P("seq", "ch"),
            P("seq", "ch"),
            P("ch"),
            P("seq", None, "ch"),
            P(None, "ch"),
            P("seq", "ch"),
            P("ch"),
            P("seq", None, "ch"),
            P("seq", "ch"),
        ),
        check_vma=False,
    )
```

```python
import jax
import jax.numpy as jnp
from jax import lax
from jax.experimental import pallas as pl
from jax.experimental.pallas import tpu as pltpu
from jax.sharding import PartitionSpec as P

EPS = 1e-05
F32 = jnp.float32
BF16 = jnp.bfloat16
CH = 4
LONG = 2**36


def seq_index(y, z, core):
    return ((y % 4) * 4 + z % 4) * 2 + core


def seq_pairs(dy, dz, dcore):
    return [
        (seq_index(y, z, core), seq_index(y + dy, z + dz, core ^ dcore))
        for y in range(4)
        for z in range(4)
        for core in range(2)
    ]


def ch_pairs(step):
    return [(i, (i + step) % CH) for i in range(CH)]


def gather_ch(block):
    return [block] + [lax.ppermute(block, "ch", ch_pairs(-j)) for j in range(1, CH)]


def scatter_ch(chunks):
    total = chunks[0]
    for j in range(1, CH):
        total = total + lax.ppermute(chunks[j], "ch", ch_pairs(j)).astype(F32)
    return total


def sum_ch(vector):
    total = vector
    for j in range(1, CH):
        total = total + lax.ppermute(vector, "ch", ch_pairs(j))
    return total


def pick(array, index, axis):
    return lax.dynamic_index_in_dim(array, index, axis, keepdims=False)


def from_behind(array, axis, by):
    size = lax.axis_size(axis)
    pairs = [(i, i + by) for i in range(size) if 0 <= i + by < size]
    return lax.ppermute(array, axis, pairs)


def first_count(segment_ids):
    return jnp.sum((segment_ids == segment_ids[0]).astype(jnp.int32))


def tap_masks(count, rows):
    token = lax.broadcasted_iota(jnp.int32, (rows, 1), 0)
    same_one = (token != count).astype(F32)
    same_two = ((token != count) & (token != count + 1)).astype(F32)
    return (same_one, same_two)


def tie(*arrays):
    return lax.optimization_barrier(arrays)


def reduce_axis(array, axis, me, along_y):
    total = pick(array, me, axis).astype(F32)
    for step in (1, 3, 2):
        pairs = seq_pairs(step, 0, 0) if along_y else seq_pairs(0, step, 0)
        total = total + lax.ppermute(pick(array, (me + step) % 4, axis), "seq", pairs).astype(F32)
    return total


def dot_nt(a, b):
    return lax.dot_general(a, b, (((1,), (1,)), ((), ())), preferred_element_type=F32)


def dot_tn(a, b):
    return lax.dot_general(a, b, (((0,), (0,)), ((), ())), preferred_element_type=F32)


def dot_nn(a, b):
    return lax.dot_general(a, b, (((1,), (0,)), ((), ())), preferred_element_type=F32)


def rel_rows(x, j, width):
    return pl.ds(pl.multiple_of(lax.rem(x + j, CH) * width, width), width)


def vmem():
    return pl.BlockSpec(memory_space=pltpu.VMEM)


def smem():
    return pl.BlockSpec(memory_space=pltpu.SMEM)


def anywhere():
    return pl.BlockSpec(memory_space=pl.ANY)


def shape(dims, dtype):
    return jax.ShapeDtypeStruct(dims, dtype)


def params(megabytes):
    return pltpu.CompilerParams(vmem_limit_bytes=megabytes * 1024 * 1024)


def cost(macs, nbytes):
    return pl.CostEstimate(flops=2 * macs, bytes_accessed=nbytes, transcendentals=0)


def in_kernel(at, p0, p1, p2, p3, gain, weight, normed, rms, b_out, c_out, v_out, gated, held, sem):
    x = at[0]
    width = p0.shape[1]
    copies = [
        pltpu.make_async_copy(
            weight.at[:, rel_rows(x, j, width), :],
            held.at[:, pl.ds(j * width, width), :],
            sem.at[j],
        )
        for j in range(CH)
    ]
    for copy in copies:
        copy.start()
    pieces = [p0, p1, p2, p3]
    square = jnp.zeros((p0.shape[0], 1), F32)
    for piece in pieces:
        rows = piece[...].astype(F32)
        square = square + jnp.sum(rows * rows, axis=1, keepdims=True)
    r = lax.rsqrt(square / (CH * width) + EPS)
    rms[...] = r
    for j, piece in enumerate(pieces):
        scale = gain[:, rel_rows(x, j, width)]
        normed[:, j * width : (j + 1) * width] = (piece[...].astype(F32) * r * scale).astype(BF16)
    for copy in copies:
        copy.wait()
    b = dot_nn(normed[...], held[0])
    v = dot_nn(normed[...], held[2])
    b_out[...] = b
    v_out[...] = v
    gated[...] = (b * v).astype(BF16)
    c_out[...] = dot_nn(normed[...], held[1])


def in_project(at, pieces, gain, weight):
    rows, width = pieces[0].shape
    features = CH * width
    out = shape((rows, width), F32)
    return pl.pallas_call(
        in_kernel,
        out_shape=(
            shape((rows, features), BF16),
            shape((rows, 1), F32),
            out,
            out,
            out,
            shape((rows, width), BF16),
        ),
        in_specs=[smem()] + [vmem()] * 5 + [anywhere()],
        out_specs=(vmem(),) * 6,
        scratch_shapes=[
            pltpu.VMEM((3, features, width), BF16),
            pltpu.SemaphoreType.DMA((CH,)),
        ],
        compiler_params=params(56),
        cost_estimate=cost(rows * features * 3 * width, 6 * 2**20),
    )(at, *pieces, gain[None], weight)


def columns_kernel(p0, p1, p2, p3, out):
    width = p0.shape[1]
    for j, piece in enumerate((p0, p1, p2, p3)):
        out[:, j * width : (j + 1) * width] = piece[...]


def join_columns(pieces, weight):
    rows, width = pieces[0].shape
    return pl.pallas_call(
        columns_kernel,
        out_shape=shape((rows, CH * width), BF16),
        in_specs=[vmem()] * CH,
        out_specs=vmem(),
        compiler_params=params(56),
        cost_estimate=cost(weight, 2**21),
    )(*pieces)


def ffn_kernel(
    at,
    x0, x1, x2, x3,
    mixed,
    gain,
    half,
    other,
    planes,
    down,
    cotangent,
    h, rms, normed, act, d_gate_up, d_own, d1, d2, d3, f0, f1, f2, f3,
    w_out, w_in, w_down, g_rows, acc, down_acc, sem,
):
    x, core = at[0], at[1]
    width = x0.shape[1]
    units = down.shape[1]
    step = units // 3
    halves = [
        pltpu.make_async_copy(half, w_out.at[0], sem.at[0]),
        pltpu.make_async_copy(other, w_out.at[1], sem.at[1]),
    ]
    planes_in = [
        pltpu.make_async_copy(
            planes.at[:, rel_rows(x, j, width), :],
            w_in.at[:, pl.ds(j * width, width), :],
            sem.at[2 + j],
        )
        for j in range(CH)
    ]
    rest = [
        pltpu.make_async_copy(cotangent, g_rows, sem.at[6]),
        pltpu.make_async_copy(down, w_down, sem.at[7]),
    ]
    for copy in halves + planes_in + rest:
        copy.start()
    for copy in halves:
        copy.wait()
    square = jnp.zeros((x0.shape[0], 1), F32)
    for j, piece in enumerate((x0, x1, x2, x3)):
        block = lax.rem(x + j, CH)
        which = lax.rem(block // 2 + core, 2)
        rows = pl.ds(pl.multiple_of(lax.rem(block, 2) * width, width), width)
        hj = piece[...].astype(F32) + dot_nt(mixed[...], w_out[which, rows, :])
        h[:, j * width : (j + 1) * width] = hj
        square = square + jnp.sum(hj * hj, axis=1, keepdims=True)
    r = lax.rsqrt(square / (CH * width) + EPS)
    rms[...] = r
    for j in range(CH):
        columns = slice(j * width, (j + 1) * width)
        scale = gain[:, rel_rows(x, j, width)]
        normed[:, columns] = (h[:, columns] * r * scale).astype(BF16)
    for copy in planes_in + rest:
        copy.wait()

    def part(i, carry):
        f = pl.ds(pl.multiple_of(i * step, 128), step)
        f_up = pl.ds(pl.multiple_of(units + i * step, 128), step)
        gate = dot_nn(normed[...], w_in[0, :, f])
        up = dot_nn(normed[...], w_in[1, :, f])
        d_act = dot_nn(g_rows[...], w_down[:, f])
        sigma = jax.nn.sigmoid(gate)
        swish = gate * sigma
        active = (swish * up).astype(BF16)
        act[:, f] = active
        for j in range(CH):
            rows = slice(j * width, (j + 1) * width)
            term = dot_nt(active, w_down[rows, f])
            down_acc[j] = jnp.where(i == 0, term, down_acc[j] + term)
        d_gate = (d_act * up * sigma * (1.0 + gate * (1.0 - sigma))).astype(BF16)
        d_up = (d_act * swish).astype(BF16)
        d_gate_up[:, f] = d_gate
        d_gate_up[:, f_up] = d_up
        for j in range(CH):
            rows = slice(j * width, (j + 1) * width)
            term = dot_nt(d_gate, w_in[0, rows, f]) + dot_nt(d_up, w_in[1, rows, f])
            acc[j] = jnp.where(i == 0, term, acc[j] + term)
        return carry

    lax.fori_loop(0, 3, part, 0)
    d_own[...] = acc[0]
    d1[...] = acc[1].astype(BF16)
    d2[...] = acc[2].astype(BF16)
    d3[...] = acc[3].astype(BF16)
    for j, out in enumerate((f0, f1, f2, f3)):
        out[...] = down_acc[lax.rem(x + j, CH)].astype(BF16)


def ffn(at, pieces, mixed, gain, half, other, planes, down, cotangent):
    rows, width = pieces[0].shape
    features = CH * width
    units = down.shape[1]
    block = shape((rows, width), BF16)
    return pl.pallas_call(
        ffn_kernel,
        out_shape=(
            shape((rows, features), F32),
            shape((rows, 1), F32),
            shape((rows, features), BF16),
            shape((rows, units), BF16),
            shape((rows, 2 * units), BF16),
            shape((rows, width), F32),
        )
        + (block,) * 7,
        in_specs=[smem()] + [vmem()] * 6 + [anywhere()] * 5,
        out_specs=(vmem(),) * 13,
        scratch_shapes=[
            pltpu.VMEM((2, features // 2, features), BF16),
            pltpu.VMEM((2, features, units), BF16),
            pltpu.VMEM((features, units), BF16),
            pltpu.VMEM((rows, features), BF16),
            pltpu.VMEM((CH, rows, width), F32),
            pltpu.VMEM((CH, rows, width), F32),
            pltpu.SemaphoreType.DMA((8,)),
        ],
        compiler_params=params(56),
        cost_estimate=cost(rows * features * (features + 6 * units), 20 * 2**20),
    )(at, *pieces, mixed, gain[None], half, other, planes, down, cotangent)


def pair_kernel(
    at, a_left, a_right, b_left, b_right, give_a, give_b, keep, held, *, a_rolled, b_rolled
):
    x, core = at[0], at[1]
    y = pl.program_id(0)
    wide = keep.shape[2] * 8
    turned = lax.rem(y + CH - x, CH)
    cut = a_right.shape[1]
    for left, right, rolled, base in (
        (a_left, a_right, a_rolled, 0),
        (b_left, b_right, b_rolled, cut),
    ):
        where = turned if rolled else y
        block = left[:, pl.ds(pl.multiple_of(where * wide, wide), wide)]
        columns = right.shape[1]
        step = columns // 3 if columns % 384 == 0 else columns
        for first in range(0, columns, step):
            held[:, base + first : base + first + step] = dot_tn(
                block, right[:, first : first + step]
            )
    for z in range(4):
        mine = pl.multiple_of((2 * z + core) * 32, 32)
        theirs = pl.multiple_of((2 * z + 1 - core) * 32, 32)
        keep[z, 0] = held[pl.ds(mine, 32), :].astype(BF16)
        (give_a, give_b)[z // 2][z % 2, 0] = held[pl.ds(theirs, 32), :].astype(BF16)


def pair_products(at, a_left, a_right, b_left, b_right, a_rolled, b_rolled):
    columns = a_right.shape[1] + b_right.shape[1]
    tokens, features = a_left.shape
    out = shape((4, 4, features // 32, columns), BF16)
    spec = pl.BlockSpec((4, 1, features // 32, columns), lambda y: (0, y, 0, 0))
    half = shape((2, 4, features // 32, columns), BF16)
    half_spec = pl.BlockSpec((2, 1, features // 32, columns), lambda y: (0, y, 0, 0))

    def body(*refs):
        pair_kernel(*refs, a_rolled=a_rolled, b_rolled=b_rolled)

    return pl.pallas_call(
        body,
        grid=(4,),
        out_shape=(half, half, out),
        in_specs=[smem()] + [vmem()] * 4,
        out_specs=(half_spec, half_spec, spec),
        scratch_shapes=[pltpu.VMEM((features // 4, columns), F32)],
        compiler_params=params(56),
        cost_estimate=cost(tokens * features * columns, 4 * features * columns),
    )(at, a_left, a_right, b_left, b_right)


def swap_cores(halves):
    return [lax.ppermute(half, "seq", seq_pairs(0, 0, 1)) for half in halves]


def add_kernel(keep, got_a, got_b, out):
    out[:2] = (keep[:2].astype(F32) + got_a[...].astype(F32)).astype(BF16)
    out[2:] = (keep[2:].astype(F32) + got_b[...].astype(F32)).astype(BF16)


def add_cores(keep, got):
    spec = pl.BlockSpec((4, 1) + keep.shape[2:], lambda y: (0, y, 0, 0))
    half = pl.BlockSpec((2, 1) + keep.shape[2:], lambda y: (0, y, 0, 0))
    return pl.pallas_call(
        add_kernel,
        grid=(4,),
        out_shape=shape(keep.shape, BF16),
        in_specs=[spec, half, half],
        out_specs=spec,
        compiler_params=params(56),
        cost_estimate=cost(2**20, 6 * keep.size),
    )(keep, *got)


def spread(small):
    high = small.astype(BF16)
    low = (small - high.astype(F32)).astype(BF16)
    return high, low


def join(message, width):
    return message[:8, :width].astype(F32) + message[:8, width : 2 * width].astype(F32)


def send_kernel(at, keep, got_a, got_b, small, own, m1, m2, m3):
    z = at[3]
    rows = own.shape[0]
    width = small.shape[1]
    for j, out in enumerate((own, m1, m2, m3)):
        block = lax.rem(z + j, 4)
        inside = lax.rem(block, 2)
        got = jnp.where(block < 2, got_a[inside].astype(F32), got_b[inside].astype(F32))
        total = keep[block].astype(F32) + got
        out[:rows] = total.reshape(own.shape).astype(out.dtype)
    high, low = spread(jnp.concatenate([small[...], jnp.zeros_like(small[...])], axis=0))
    for out in (m1, m2, m3):
        out[rows:, :width] = high
        out[rows:, width : 2 * width] = low


def send_z(at, keep, got, small):
    rows, columns = keep.shape[1] * keep.shape[2], keep.shape[3]
    message = shape((rows + 16, columns), BF16)
    return pl.pallas_call(
        send_kernel,
        out_shape=(shape((rows, columns), F32), message, message, message),
        in_specs=[smem()] + [vmem()] * 4,
        out_specs=(vmem(),) * 4,
        compiler_params=params(56),
        cost_estimate=cost(2**20, 2**22),
    )(at, keep, *got, small)


def turn_kernel(at, own, m1, m2, m3, small, left, n1, n2, n3, small_out, total):
    y = at[4]
    rows = own.shape[0]
    width = small.shape[1]
    total[...] = own[...]
    small_sum = small[...]
    for m in (m1, m2, m3):
        total[...] += m[:rows].astype(F32)
        small_sum = small_sum + join(m[rows:], width)
    small_out[...] = small_sum
    part = rows // 4
    for j, out in enumerate((left, n1, n2, n3)):
        block = pl.multiple_of(lax.rem(y + j, 4) * part, part)
        out[:part] = total[pl.ds(block, part)].astype(out.dtype)
    high, low = spread(jnp.concatenate([small_sum, jnp.zeros_like(small_sum)], axis=0))
    for out in (n1, n2, n3):
        out[part:, :width] = high
        out[part:, width : 2 * width] = low


def turn(at, own, messages, small):
    rows, columns = own.shape
    message = shape((rows // 4 + 16, columns), BF16)
    return pl.pallas_call(
        turn_kernel,
        out_shape=(
            shape((rows // 4, columns), F32),
            message,
            message,
            message,
            shape(small.shape, F32),
        ),
        in_specs=[smem()] + [vmem()] * 5,
        out_specs=(vmem(),) * 5,
        scratch_shapes=[pltpu.VMEM((rows, columns), F32)],
        compiler_params=params(56),
        cost_estimate=cost(2**20, 2**21),
    )(at, own, *messages, small)


def last_kernel(own, m1, m2, m3, small, in_out, out_out, small_out):
    rows = own.shape[0]
    width = small.shape[1]
    total = own[...]
    small_sum = small[...]
    for m in (m1, m2, m3):
        total = total + m[:rows].astype(F32)
        small_sum = small_sum + join(m[rows:], width)
    for k in range(3):
        in_out[k] = total[:, k * width : (k + 1) * width]
    out_out[...] = total[:, 3 * width :]
    small_out[...] = small_sum


def last(own, messages, small):
    rows, columns = own.shape
    width = small.shape[1]
    return pl.pallas_call(
        last_kernel,
        out_shape=(
            shape((3, rows, width), F32),
            shape((rows, columns - 3 * width), F32),
            shape(small.shape, F32),
        ),
        in_specs=[vmem()] * 5,
        out_specs=(vmem(),) * 3,
        compiler_params=params(56),
        cost_estimate=cost(2**20, 2**20),
    )(own, *messages, small)


def end_kernel(d_own, d1, d2, d3, inner, d_hidden, rows_in, rms, gain, grad, gain_grad):
    rows, width = d_own.shape
    total = d_own[...]
    line = inner[...]
    for d in (d1, d2, d3):
        total = total + d[:rows].astype(F32)
        high = [d[rows + 16 * i : rows + 16 * (i + 1)].astype(F32) for i in range(4)]
        line = line + jnp.concatenate(
            [high[0] + high[2], high[1] + high[3]], axis=1
        )
    column = lax.dot_general(
        line, jnp.full((16, width), 1.0 / 16, F32), (((0,), (0,)), ((), ())),
        precision=lax.Precision.HIGHEST, preferred_element_type=F32,
    )
    r = rms[...]
    xs = rows_in[...].astype(F32)
    gain_grad[...] = jnp.sum(total * xs * r, axis=0, keepdims=True)
    grad[...] = (
        d_hidden[...] + r * gain[...] * total - xs * (r * r * r / (CH * width)) * column
    ).astype(BF16)


def end(d_own, received, inner, d_hidden, rows_in, rms, gain):
    rows, width = d_own.shape
    return pl.pallas_call(
        end_kernel,
        out_shape=(shape((rows, width), BF16), shape((1, width), F32)),
        in_specs=[vmem()] * 9,
        out_specs=(vmem(),) * 2,
        compiler_params=params(56),
        cost_estimate=cost(2**32, 2**21),
    )(d_own, *received, inner, d_hidden, rows_in, rms, gain[None])


def norm_kernel(d_own, d1, d2, d3, h, rms, gain, cotangent, u, u_low, gain_grad):
    total = d_own[...]
    for d in (d1, d2, d3):
        total = total + d[...].astype(F32)
    r = rms[...]
    gain_grad[...] = jnp.sum(total * h[...] * r, axis=0, keepdims=True)
    full = cotangent[...].astype(F32) + r * gain[...] * total
    u[...] = full
    u_low[...] = full.astype(BF16)


def norm_back(d_own, received, h, rms, gain, cotangent):
    rows, width = d_own.shape
    return pl.pallas_call(
        norm_kernel,
        out_shape=(
            shape((rows, width), F32),
            shape((rows, width), BF16),
            shape((1, width), F32),
        ),
        in_specs=[vmem()] * 8,
        out_specs=(vmem(),) * 3,
        compiler_params=params(56),
        cost_estimate=cost(LONG, 2**21),
    )(d_own, *received, h, rms, gain[None], cotangent)


def mid_kernel(
    at, u_own, u1, u2, u3, h, rms, cotangent, weight, c_gate, conv_out,
    d_branch, d_hidden, d_conv, d_cgate,
):
    x = at[0]
    width = u_own.shape[1]
    dot = jnp.zeros((u_own.shape[0], 1), F32)
    us = (u_own, u1, u2, u3)
    for j, u in enumerate(us):
        g = cotangent[:, rel_rows(x, j, width)].astype(F32)
        hj = h[:, j * width : (j + 1) * width]
        dot = dot + jnp.sum((u[...].astype(F32) - g) * hj, axis=1, keepdims=True)
    r = rms[...]
    scale = dot * (r * r / (CH * width))
    d_mixed = jnp.zeros(u_own.shape, F32)
    for j, u in enumerate(us):
        columns = slice(j * width, (j + 1) * width)
        full = u[...].astype(F32) - h[:, columns] * scale
        if j == 0:
            d_hidden[...] = full
        rounded = full.astype(BF16)
        d_branch[:, columns] = rounded
        d_mixed = d_mixed + dot_nn(rounded, weight[rel_rows(x, j, width), :])
    d_conv[...] = d_mixed * c_gate[...]
    d_cgate[...] = (d_mixed * conv_out[...]).astype(BF16)


def mid(at, pieces, h, rms, cotangent, weight, c_gate, conv_out):
    rows, width = c_gate.shape
    wide = shape((rows, width), F32)
    return pl.pallas_call(
        mid_kernel,
        out_shape=(shape((rows, CH * width), BF16), wide, wide, shape((rows, width), BF16)),
        in_specs=[smem()] + [vmem()] * 10,
        out_specs=(vmem(),) * 4,
        compiler_params=params(56),
        cost_estimate=cost(rows * CH * width * width, 6 * 2**20),
    )(at, *pieces, h, rms, cotangent, weight, c_gate, conv_out)


def back_kernel(
    at, p0, p1, p2, p3, d_conv, following, taps, value, b_gate, d_cgate, gain, weight,
    grads, d_own, d1, d2, d3, inner, held, sem,
):
    x, count = at[0], at[2]
    rows, width = p0.shape
    copies = [
        pltpu.make_async_copy(
            weight.at[:, rel_rows(x, j, width), :],
            held.at[:, pl.ds(j * width, width), :],
            sem.at[j],
        )
        for j in range(CH)
    ]
    for copy in copies:
        copy.start()
    token = lax.broadcasted_iota(jnp.int32, (rows, width), 0)
    d = d_conv[...]
    next_one, next_two = following[0:1, :], following[1:2, :]
    after_one = jnp.where(token + 1 == count, 0.0, pltpu.roll(d, rows - 1, 0))
    after_one = jnp.where(token == rows - 1, next_one, after_one)
    after_two = pltpu.roll(d, rows - 2, 0)
    after_two = jnp.where((token + 2 == count) | (token + 1 == count), 0.0, after_two)
    after_two = jnp.where(token == rows - 2, next_one, after_two)
    after_two = jnp.where(token == rows - 1, next_two, after_two)
    d_gated = taps[0:1, :] * d + taps[1:2, :] * after_one + taps[2:3, :] * after_two
    grads[:, :width] = (d_gated * value[...]).astype(BF16)
    grads[:, width : 2 * width] = d_cgate[...]
    grads[:, 2 * width :] = (d_gated * b_gate[...]).astype(BF16)
    total = jnp.zeros((rows, width), F32)
    for j, piece in enumerate((p0, p1, p2, p3)):
        copies[j].wait()
        block = slice(j * width, (j + 1) * width)
        term = dot_nt(grads[:, :width], held[0, block, :])
        for k in (1, 2):
            term = term + dot_nt(grads[:, k * width : (k + 1) * width], held[k, block, :])
        scale = gain[:, rel_rows(x, j, width)]
        total = total + scale * term * piece[...].astype(F32)
        if j == 0:
            d_own[...] = term
        else:
            (d1, d2, d3)[j - 1][:rows, :] = term.astype(BF16)
    ones = jnp.ones((16, width), F32)
    row = lax.dot_general(
        ones, total, (((1,), (1,)), ((), ())),
        precision=lax.Precision.HIGHEST, preferred_element_type=F32,
    )
    inner[...] = row
    high = row.astype(BF16)
    low = (row - high.astype(F32)).astype(BF16)
    for out in (d1, d2, d3):
        out[rows : rows + 16, :] = high[:, :width]
        out[rows + 16 : rows + 32, :] = high[:, width:]
        out[rows + 32 : rows + 48, :] = low[:, :width]
        out[rows + 48 : rows + 64, :] = low[:, width:]


def back_project(at, pieces, d_conv, following, taps, value, b_gate, d_cgate, gain, weight):
    rows, width = pieces[0].shape
    features = CH * width
    block = shape((rows + 64, width), BF16)
    return pl.pallas_call(
        back_kernel,
        out_shape=(
            shape((rows, 3 * width), BF16),
            shape((rows, width), F32),
            block,
            block,
            block,
            shape((16, rows), F32),
        ),
        in_specs=[smem()] + [vmem()] * 11 + [anywhere()],
        out_specs=(vmem(),) * 6,
        scratch_shapes=[
            pltpu.VMEM((3, features, width), BF16),
            pltpu.SemaphoreType.DMA((CH,)),
        ],
        compiler_params=params(56),
        cost_estimate=cost(rows * features * 3 * width, 6 * 2**20),
    )(at, *pieces, d_conv, following, taps, value, b_gate, d_cgate, gain[None], weight)


def scatter_groups(array, groups):
    return lax.psum_scatter(array, "seq", scatter_dimension=0, axis_index_groups=groups)


def shards(
    block_input,
    segment_ids,
    norm1_gain,
    in_weight,
    conv_weight,
    out_weight,
    norm2_gain,
    ffn_in_weight,
    ffn_out_weight,
    out_grad,
):
    x = lax.axis_index("ch")
    seq = lax.axis_index("seq")
    core, z, y = seq % 2, (seq // 2) % 4, seq // 8
    features = norm1_gain.shape[0]
    width = block_input.shape[1]
    hidden_units = ffn_out_weight.shape[1]

    def rolled(array):
        blocks = array.reshape((CH, width) + array.shape[1:])
        return jnp.concatenate([pick(blocks, (x + j) % CH, 0) for j in range(CH)], axis=0)

    count = first_count(segment_ids)
    at = jnp.stack([x, core, count, z, y]).astype(jnp.int32)
    own_one = pick(norm1_gain.reshape(CH, width), x, 0)
    own_two = pick(norm2_gain.reshape(CH, width), x, 0)
    in_planes = jnp.transpose(in_weight, (1, 0, 2))

    pieces = gather_ch(block_input)
    half_rows = out_weight.shape[0] // 2
    half = lax.dynamic_slice_in_dim(out_weight, core * half_rows, half_rows, 0)
    half_pieces = gather_ch(half)
    grad_full = lax.all_gather(out_grad, "ch", axis=1, tiled=True)

    normed_one, r_one, b_gate, c_gate, value_rows, gated_rows = in_project(
        at, pieces, norm1_gain, in_planes
    )
    own_rows = block_input.astype(F32)
    carried = from_behind(gated_rows[-2:], "seq", 1)
    extended = jnp.concatenate([carried, gated_rows], axis=0).astype(F32)
    same_one, same_two = tap_masks(count, block_input.shape[0])
    current = extended[2:]
    prior_one = extended[1:-1] * same_one
    prior_two = extended[:-2] * same_two
    conv_out = conv_weight[0] * current + conv_weight[1] * prior_one + conv_weight[2] * prior_two
    mixed_rows = (c_gate * conv_out).astype(BF16)

    mixed_pieces = gather_ch(mixed_rows)
    *half_pieces, ffn_weight, _ = tie(*half_pieces, ffn_in_weight, mixed_rows)
    ffn_planes = jnp.transpose(ffn_weight, (1, 0, 2))
    half_full = join_columns(half_pieces, 2**20)
    mixed_full = join_columns(mixed_pieces, 2**32)
    ffn_planes, mixed_full = tie(ffn_planes, mixed_full)
    other_half = lax.ppermute(half_full, "seq", seq_pairs(0, 0, 1))
    (
        hidden,
        r_two,
        normed_two,
        act_rows,
        d_gate_up,
        d_own,
        d_one,
        d_two,
        d_three,
        *down_parts,
    ) = ffn(
        at,
        pieces,
        mixed_full,
        norm2_gain,
        half_full,
        other_half,
        ffn_planes,
        ffn_out_weight,
        grad_full,
    )
    hidden_own = hidden[:, :width]
    received = [
        lax.ppermute(d, "ch", ch_pairs(j)) for j, d in ((1, d_one), (2, d_two), (3, d_three))
    ]
    *gives, keep = pair_products(at, normed_two, d_gate_up, grad_full, act_rows, True, False)
    got = swap_cores(gives)

    u_own, u_low, grad_gain_two = norm_back(
        d_own, received, hidden_own, r_two, own_two, out_grad
    )
    u_pieces = [u_own] + gather_ch(u_low)[1:]
    ffn_kept = add_cores(keep, got)
    ffn_kept, *u_pieces = tie(ffn_kept, *u_pieces)
    groups = [[seq_index(i, k, c) for k in range(4)] for i in range(4) for c in range(2)]
    ffn_sum = scatter_groups(ffn_kept, groups)

    d_branch, d_hidden, d_conv, d_cgate = mid(
        at, u_pieces, hidden, r_two, grad_full, out_weight, c_gate, conv_out
    )
    following = from_behind(d_conv[:2], "seq", -1)
    d_proj, d_own, d_one, d_two, d_three, inner = back_project(
        at, pieces, d_conv, following, conv_weight, value_rows, b_gate, d_cgate, norm1_gain,
        in_planes,
    )
    received = [lax.ppermute(d, "ch", ch_pairs(j)) for j, d in ((1, d_one), (2, d_two), (3, d_three))]

    *gives, keep = pair_products(at, normed_one, d_proj, d_branch, mixed_rows, True, True)
    got = swap_cores(gives)
    grad_conv = jnp.stack(
        [
            jnp.sum(d_conv * current, axis=0),
            jnp.sum(d_conv * prior_one, axis=0),
            jnp.sum(d_conv * prior_two, axis=0),
        ],
        axis=0,
    )
    input_grad, grad_gain_one = end(
        d_own, received, inner, d_hidden, block_input, r_one, own_one
    )
    small = jnp.concatenate(
        [grad_conv, grad_gain_one, grad_gain_two, jnp.zeros((3, width), F32)], axis=0
    )
    small = small + lax.ppermute(small, "seq", seq_pairs(0, 0, 1))
    small, ffn_sum, *got = tie(small, ffn_sum, *got)
    own, *messages = send_z(at, keep, got, small)
    down_parts, messages = lax.optimization_barrier((down_parts, messages))
    downs = [lax.ppermute(down_parts[j], "ch", ch_pairs(j)) for j in (1, 2, 3)]
    messages = [
        lax.ppermute(m, "seq", seq_pairs(0, j, 0)) for j, m in ((1, messages[0]), (2, messages[1]), (3, messages[2]))
    ]
    downs, messages = lax.optimization_barrier((downs, messages))
    block_output = hidden_own + down_parts[0].astype(F32)
    for down in downs:
        block_output = block_output + down.astype(F32)
    block_output = block_output.astype(BF16)
    own, *messages, small = turn(at, own, messages, small)
    messages = [
        lax.ppermute(m, "seq", seq_pairs(j, 0, 0)) for j, m in ((1, messages[0]), (2, messages[1]), (3, messages[2]))
    ]
    grad_in, grad_out, small = last(own, messages, small)

    groups = [[seq_index(k, i, c) for k in range(4)] for i in range(4) for c in range(2)]
    ffn_sum = scatter_groups(ffn_sum, groups).astype(F32)
    grad_ffn_in = ffn_sum[:, : 2 * hidden_units].reshape(-1, 2, hidden_units)
    grad_ffn_out = ffn_sum[:, 2 * hidden_units :]
    return (
        block_output,
        input_grad,
        small[3],
        jnp.transpose(grad_in, (1, 0, 2)),
        small[:3],
        grad_out,
        small[4],
        grad_ffn_in,
        grad_ffn_out,
    )


def solution(mesh):
    return jax.shard_map(
        shards,
        mesh=mesh,
        in_specs=(
            P("seq", "ch"),
            P("seq"),
            P(),
            P(None, None, "ch"),
            P(None, "ch"),
            P(None, "ch"),
            P(),
            P(None, None, "ch"),
            P(None, "ch"),
            P("seq", "ch"),
        ),
        out_specs=(
            P("seq", "ch"),
            P("seq", "ch"),
            P("ch"),
            P("seq", None, "ch"),
            P(None, "ch"),
            P("seq", "ch"),
            P("ch"),
            P("seq", None, "ch"),
            P("seq", "ch"),
        ),
        check_vma=False,
    )
```

```python
import jax
import jax.numpy as jnp
from jax import lax
from jax.experimental import pallas as pl
from jax.experimental.pallas import tpu as pltpu
from jax.sharding import PartitionSpec as P

EPS = 1e-05
F32 = jnp.float32
BF16 = jnp.bfloat16
CH = 4
LONG = 2**36


def seq_index(y, z, core):
    return ((y % 4) * 4 + z % 4) * 2 + core


def seq_pairs(dy, dz, dcore):
    return [
        (seq_index(y, z, core), seq_index(y + dy, z + dz, core ^ dcore))
        for y in range(4)
        for z in range(4)
        for core in range(2)
    ]


def ch_pairs(step):
    return [(i, (i + step) % CH) for i in range(CH)]


def gather_ch(block):
    far = lax.ppermute(block, "ch", ch_pairs(2))
    near = [lax.ppermute(block, "ch", ch_pairs(-j)) for j in (1, 3)]
    return [block, near[0], far, near[1]]


def scatter_ch(chunks):
    total = chunks[0]
    for j in range(1, CH):
        total = total + lax.ppermute(chunks[j], "ch", ch_pairs(j)).astype(F32)
    return total


def sum_ch(vector):
    total = vector
    for j in range(1, CH):
        total = total + lax.ppermute(vector, "ch", ch_pairs(j))
    return total


def pick(array, index, axis):
    return lax.dynamic_index_in_dim(array, index, axis, keepdims=False)


def from_behind(array, axis, by):
    size = lax.axis_size(axis)
    pairs = [(i, i + by) for i in range(size) if 0 <= i + by < size]
    return lax.ppermute(array, axis, pairs)


def first_count(segment_ids):
    return jnp.sum((segment_ids == segment_ids[0]).astype(jnp.int32))


def tie(*arrays):
    return lax.optimization_barrier(arrays)


def reduce_axis(array, axis, me, along_y):
    total = pick(array, me, axis).astype(F32)
    for step in (1, 3, 2):
        pairs = seq_pairs(step, 0, 0) if along_y else seq_pairs(0, step, 0)
        total = total + lax.ppermute(pick(array, (me + step) % 4, axis), "seq", pairs).astype(F32)
    return total


def dot_nt(a, b):
    return lax.dot_general(a, b, (((1,), (1,)), ((), ())), preferred_element_type=F32)


def dot_tn(a, b):
    return lax.dot_general(a, b, (((0,), (0,)), ((), ())), preferred_element_type=F32)


def dot_nn(a, b):
    return lax.dot_general(a, b, (((1,), (0,)), ((), ())), preferred_element_type=F32)


def rel_rows(x, j, width):
    return pl.ds(pl.multiple_of(lax.rem(x + j, CH) * width, width), width)


def vmem():
    return pl.BlockSpec(memory_space=pltpu.VMEM)


def smem():
    return pl.BlockSpec(memory_space=pltpu.SMEM)


def anywhere():
    return pl.BlockSpec(memory_space=pl.ANY)


def shape(dims, dtype):
    return jax.ShapeDtypeStruct(dims, dtype)


def params(megabytes):
    return pltpu.CompilerParams(vmem_limit_bytes=megabytes * 1024 * 1024)


def cost(macs, nbytes):
    return pl.CostEstimate(flops=2 * macs, bytes_accessed=nbytes, transcendentals=0)


def in_kernel(at, p0, p1, p2, p3, gain, weight, normed, rms, b_out, c_out, v_out, gated, edge, held, sem):
    x = at[0]
    width = p0.shape[1]
    copies = [
        pltpu.make_async_copy(
            weight.at[:, rel_rows(x, j, width), :],
            held.at[:, pl.ds(j * width, width), :],
            sem.at[j],
        )
        for j in range(CH)
    ]
    for copy in copies:
        copy.start()
    pieces = [p0, p1, p2, p3]
    square = jnp.zeros((p0.shape[0], 1), F32)
    for piece in pieces:
        rows = piece[...].astype(F32)
        square = square + jnp.sum(rows * rows, axis=1, keepdims=True)
    r = lax.rsqrt(square / (CH * width) + EPS)
    rms[...] = r
    for j, piece in enumerate(pieces):
        scale = gain[:, rel_rows(x, j, width)]
        normed[:, j * width : (j + 1) * width] = (piece[...].astype(F32) * r * scale).astype(BF16)
    for copy in copies:
        copy.wait()
    b = dot_nn(normed[...], held[0])
    v = dot_nn(normed[...], held[2])
    b_out[...] = b
    v_out[...] = v
    product = (b * v).astype(BF16)
    gated[...] = product
    edge[...] = product[-16:]
    c_out[...] = dot_nn(normed[...], held[1])


def in_project(at, pieces, gain, weight):
    rows, width = pieces[0].shape
    features = CH * width
    out = shape((rows, width), F32)
    return pl.pallas_call(
        in_kernel,
        out_shape=(
            shape((rows, features), BF16),
            shape((rows, 1), F32),
            out,
            out,
            out,
            shape((rows, width), BF16),
            shape((16, width), BF16),
        ),
        in_specs=[smem()] + [vmem()] * 5 + [anywhere()],
        out_specs=(vmem(),) * 7,
        scratch_shapes=[
            pltpu.VMEM((3, features, width), BF16),
            pltpu.SemaphoreType.DMA((CH,)),
        ],
        compiler_params=params(56),
        cost_estimate=cost(rows * features * 3 * width, 6 * 2**20),
    )(at, *pieces, gain[None], weight)


def columns_kernel(p0, p1, p2, p3, out):
    width = p0.shape[1]
    for j, piece in enumerate((p0, p1, p2, p3)):
        out[:, j * width : (j + 1) * width] = piece[...]


def join_columns(pieces, weight):
    rows, width = pieces[0].shape
    return pl.pallas_call(
        columns_kernel,
        out_shape=shape((rows, CH * width), BF16),
        in_specs=[vmem()] * CH,
        out_specs=vmem(),
        compiler_params=params(56),
        cost_estimate=cost(weight, 2**21),
    )(*pieces)


def conv_kernel(at, gated, carried, c_gate, taps, mixed, conv_out, one_out, two_out):
    count = at[2]
    rows, width = gated.shape
    token = lax.broadcasted_iota(jnp.int32, (rows, width), 0)
    current = gated[...].astype(F32)
    before = carried[...].astype(F32)
    last, second = before[15:16], before[14:15]
    one = jnp.where(token == 0, last, pltpu.roll(current, 1, 0))
    one = jnp.where(token == count, 0.0, one)
    two = jnp.where(token == 0, second, pltpu.roll(current, 2, 0))
    two = jnp.where(token == 1, last, two)
    two = jnp.where((token == count) | (token == count + 1), 0.0, two)
    out = taps[0:1] * current + taps[1:2] * one + taps[2:3] * two
    mixed[...] = (c_gate[...] * out).astype(BF16)
    conv_out[...] = out
    one_out[...] = one.astype(BF16)
    two_out[...] = two.astype(BF16)


def convolve(at, gated, carried, c_gate, taps):
    rows, width = gated.shape
    low = shape((rows, width), BF16)
    mixed, out, one, two = pl.pallas_call(
        conv_kernel,
        out_shape=(low, shape((rows, width), F32), low, low),
        in_specs=[smem()] + [vmem()] * 4,
        out_specs=(vmem(),) * 4,
        compiler_params=params(56),
        cost_estimate=cost(2**22, 2**21),
    )(at, gated, carried, c_gate, taps)
    return mixed, out, gated, one, two


def copy_kernel(row, out):
    out[...] = row[...]


def copy_row(row):
    return pl.pallas_call(
        copy_kernel,
        out_shape=shape(row.shape, F32),
        in_specs=[vmem()],
        out_specs=vmem(),
        compiler_params=params(56),
        cost_estimate=cost(LONG, 2**13),
    )(row)


def ffn_kernel(
    at,
    x0, x1, x2, x3,
    m0, m1, m2, m3,
    gain,
    half,
    other,
    planes,
    down,
    cotangent,
    h, h_own, rms, normed, act, d_gate_up, d_own, d1, d2, d3, f0, f1, f2, f3,
    w_out, w_in, w_down, g_rows, mixed, acc, down_acc, sem,
):
    x, core = at[0], at[1]
    width = x0.shape[1]
    units = down.shape[1]
    step = units // 3
    halves = [
        pltpu.make_async_copy(half, w_out.at[0], sem.at[0]),
        pltpu.make_async_copy(other, w_out.at[1], sem.at[1]),
    ]
    planes_in = [
        pltpu.make_async_copy(
            planes.at[:, rel_rows(x, j, width), :],
            w_in.at[:, pl.ds(j * width, width), :],
            sem.at[2 + j],
        )
        for j in range(CH)
    ]
    rest = [
        pltpu.make_async_copy(cotangent, g_rows, sem.at[6]),
        pltpu.make_async_copy(down, w_down, sem.at[7]),
    ]
    for copy in halves + planes_in + rest:
        copy.start()
    for j, piece in enumerate((m0, m1, m2, m3)):
        mixed[:, j * width : (j + 1) * width] = piece[...]
    for copy in halves:
        copy.wait()
    square = jnp.zeros((x0.shape[0], 1), F32)
    for j, piece in enumerate((x0, x1, x2, x3)):
        block = lax.rem(x + j, CH)
        which = lax.rem(block // 2 + core, 2)
        rows = pl.ds(pl.multiple_of(lax.rem(block, 2) * width, width), width)
        hj = piece[...].astype(F32) + dot_nt(mixed[...], w_out[which, rows, :])
        h[:, j * width : (j + 1) * width] = hj
        square = square + jnp.sum(hj * hj, axis=1, keepdims=True)
    r = lax.rsqrt(square / (CH * width) + EPS)
    rms[...] = r
    h_own[...] = h[:, :width]
    for j in range(CH):
        columns = slice(j * width, (j + 1) * width)
        scale = gain[:, rel_rows(x, j, width)]
        normed[:, columns] = (h[:, columns] * r * scale).astype(BF16)
    for copy in planes_in + rest:
        copy.wait()

    def part(i, carry):
        f = pl.ds(pl.multiple_of(i * step, 128), step)
        f_up = pl.ds(pl.multiple_of(units + i * step, 128), step)
        gate = dot_nn(normed[...], w_in[0, :, f])
        up = dot_nn(normed[...], w_in[1, :, f])
        d_act = dot_nn(g_rows[...], w_down[:, f])
        sigma = jax.nn.sigmoid(gate)
        swish = gate * sigma
        active = (swish * up).astype(BF16)
        act[:, f] = active
        for j in range(CH):
            rows = slice(j * width, (j + 1) * width)
            term = dot_nt(active, w_down[rows, f])
            down_acc[j] = jnp.where(i == 0, term, down_acc[j] + term)
        d_gate = (d_act * up * sigma * (1.0 + gate * (1.0 - sigma))).astype(BF16)
        d_up = (d_act * swish).astype(BF16)
        d_gate_up[:, f] = d_gate
        d_gate_up[:, f_up] = d_up
        for j in range(CH):
            rows = slice(j * width, (j + 1) * width)
            term = dot_nt(d_gate, w_in[0, rows, f]) + dot_nt(d_up, w_in[1, rows, f])
            acc[j] = jnp.where(i == 0, term, acc[j] + term)
        return carry

    lax.fori_loop(0, 3, part, 0)
    d_own[...] = acc[0]
    d1[...] = acc[1].astype(BF16)
    d2[...] = acc[2].astype(BF16)
    d3[...] = acc[3].astype(BF16)
    for j, out in enumerate((f0, f1, f2, f3)):
        out[...] = down_acc[lax.rem(x + j, CH)].astype(BF16)


def ffn(at, pieces, mixed_pieces, gain, half, other, planes, down, cotangent):
    rows, width = pieces[0].shape
    features = CH * width
    units = down.shape[1]
    block = shape((rows, width), BF16)
    return pl.pallas_call(
        ffn_kernel,
        out_shape=(
            shape((rows, features), F32),
            shape((rows, width), F32),
            shape((rows, 1), F32),
            shape((rows, features), BF16),
            shape((rows, units), BF16),
            shape((rows, 2 * units), BF16),
            shape((rows, width), F32),
        )
        + (block,) * 7,
        in_specs=[smem()] + [vmem()] * 9 + [anywhere()] * 5,
        out_specs=(vmem(),) * 14,
        scratch_shapes=[
            pltpu.VMEM((2, features // 2, features), BF16),
            pltpu.VMEM((2, features, units), BF16),
            pltpu.VMEM((features, units), BF16),
            pltpu.VMEM((rows, features), BF16),
            pltpu.VMEM((rows, features), BF16),
            pltpu.VMEM((CH, rows, width), F32),
            pltpu.VMEM((CH, rows, width), F32),
            pltpu.SemaphoreType.DMA((8,)),
        ],
        compiler_params=params(56),
        cost_estimate=cost(rows * features * (features + 6 * units), 20 * 2**20),
    )(at, *pieces, *mixed_pieces, gain, half, other, planes, down, cotangent)


def pair_kernel(
    at, a_left, a_right, b_left, b_right, give_a, give_b, keep, held, *, a_rolled, b_rolled
):
    x, core = at[0], at[1]
    y = pl.program_id(0)
    wide = keep.shape[2] * 8
    turned = lax.rem(y + CH - x, CH)
    cut = a_right.shape[1]
    for left, right, rolled, base in (
        (a_left, a_right, a_rolled, 0),
        (b_left, b_right, b_rolled, cut),
    ):
        where = turned if rolled else y
        block = left[:, pl.ds(pl.multiple_of(where * wide, wide), wide)]
        columns = right.shape[1]
        step = columns // 3 if columns % 384 == 0 else columns
        for first in range(0, columns, step):
            held[:, base + first : base + first + step] = dot_tn(
                block, right[:, first : first + step]
            )
    for z in range(4):
        mine = pl.multiple_of((2 * z + core) * 32, 32)
        theirs = pl.multiple_of((2 * z + 1 - core) * 32, 32)
        keep[z, 0] = held[pl.ds(mine, 32), :].astype(BF16)
        (give_a, give_b)[z // 2][z % 2, 0] = held[pl.ds(theirs, 32), :].astype(BF16)


def pair_products(at, a_left, a_right, b_left, b_right, a_rolled, b_rolled):
    columns = a_right.shape[1] + b_right.shape[1]
    tokens, features = a_left.shape
    out = shape((4, 4, features // 32, columns), BF16)
    spec = pl.BlockSpec((4, 1, features // 32, columns), lambda y: (0, y, 0, 0))
    half = shape((2, 4, features // 32, columns), BF16)
    half_spec = pl.BlockSpec((2, 1, features // 32, columns), lambda y: (0, y, 0, 0))

    def body(*refs):
        pair_kernel(*refs, a_rolled=a_rolled, b_rolled=b_rolled)

    return pl.pallas_call(
        body,
        grid=(4,),
        out_shape=(half, half, out),
        in_specs=[smem()] + [vmem()] * 4,
        out_specs=(half_spec, half_spec, spec),
        scratch_shapes=[pltpu.VMEM((features // 4, columns), F32)],
        compiler_params=params(56),
        cost_estimate=cost(tokens * features * columns, 4 * features * columns),
    )(at, a_left, a_right, b_left, b_right)


def swap_cores(halves):
    return [lax.ppermute(half, "seq", seq_pairs(0, 0, 1)) for half in halves]


def add_kernel(keep, got_a, got_b, out):
    out[:2] = (keep[:2].astype(F32) + got_a[...].astype(F32)).astype(BF16)
    out[2:] = (keep[2:].astype(F32) + got_b[...].astype(F32)).astype(BF16)


def add_cores(keep, got):
    spec = pl.BlockSpec((4, 1) + keep.shape[2:], lambda y: (0, y, 0, 0))
    half = pl.BlockSpec((2, 1) + keep.shape[2:], lambda y: (0, y, 0, 0))
    return pl.pallas_call(
        add_kernel,
        grid=(4,),
        out_shape=shape(keep.shape, BF16),
        in_specs=[spec, half, half],
        out_specs=spec,
        compiler_params=params(56),
        cost_estimate=cost(2**20, 6 * keep.size),
    )(keep, *got)


def spread(small):
    high = small.astype(BF16)
    low = (small - high.astype(F32)).astype(BF16)
    return high, low


def join(message, width):
    return message[:8, :width].astype(F32) + message[:8, width : 2 * width].astype(F32)


def send_kernel(at, keep, got_a, got_b, small, own, m1, m2, m3):
    z = at[3]
    rows = own.shape[0]
    width = small.shape[1]
    for j, out in enumerate((own, m1, m2, m3)):
        block = lax.rem(z + j, 4)
        inside = lax.rem(block, 2)
        got = jnp.where(block < 2, got_a[inside].astype(F32), got_b[inside].astype(F32))
        total = keep[block].astype(F32) + got
        out[:rows] = total.reshape(own.shape).astype(out.dtype)
    high, low = spread(jnp.concatenate([small[...], jnp.zeros_like(small[...])], axis=0))
    for out in (m1, m2, m3):
        out[rows:, :width] = high
        out[rows:, width : 2 * width] = low


def send_z(at, keep, got, small):
    rows, columns = keep.shape[1] * keep.shape[2], keep.shape[3]
    message = shape((rows + 16, columns), BF16)
    return pl.pallas_call(
        send_kernel,
        out_shape=(shape((rows, columns), F32), message, message, message),
        in_specs=[smem()] + [vmem()] * 4,
        out_specs=(vmem(),) * 4,
        compiler_params=params(56),
        cost_estimate=cost(2**20, 2**22),
    )(at, keep, *got, small)


def turn_kernel(at, own, m1, m2, m3, small, left, n1, n2, n3, small_out, total):
    y = at[4]
    rows = own.shape[0]
    width = small.shape[1]
    total[...] = own[...]
    small_sum = small[...]
    for m in (m1, m2, m3):
        total[...] += m[:rows].astype(F32)
        small_sum = small_sum + join(m[rows:], width)
    small_out[...] = small_sum
    part = rows // 4
    for j, out in enumerate((left, n1, n2, n3)):
        block = pl.multiple_of(lax.rem(y + j, 4) * part, part)
        out[:part] = total[pl.ds(block, part)].astype(out.dtype)
    high, low = spread(jnp.concatenate([small_sum, jnp.zeros_like(small_sum)], axis=0))
    for out in (n1, n2, n3):
        out[part:, :width] = high
        out[part:, width : 2 * width] = low


def turn(at, own, messages, small):
    rows, columns = own.shape
    message = shape((rows // 4 + 16, columns), BF16)
    return pl.pallas_call(
        turn_kernel,
        out_shape=(
            shape((rows // 4, columns), F32),
            message,
            message,
            message,
            shape(small.shape, F32),
        ),
        in_specs=[smem()] + [vmem()] * 5,
        out_specs=(vmem(),) * 5,
        scratch_shapes=[pltpu.VMEM((rows, columns), F32)],
        compiler_params=params(56),
        cost_estimate=cost(2**20, 2**21),
    )(at, own, *messages, small)


def last_kernel(own, m1, m2, m3, small, in_out, out_out, small_out):
    rows = own.shape[0]
    width = small.shape[1]
    total = own[...]
    small_sum = small[...]
    for m in (m1, m2, m3):
        total = total + m[:rows].astype(F32)
        small_sum = small_sum + join(m[rows:], width)
    for k in range(3):
        in_out[k] = total[:, k * width : (k + 1) * width]
    out_out[...] = total[:, 3 * width :]
    small_out[...] = small_sum


def last(own, messages, small):
    rows, columns = own.shape
    width = small.shape[1]
    return pl.pallas_call(
        last_kernel,
        out_shape=(
            shape((3, rows, width), F32),
            shape((rows, columns - 3 * width), F32),
            shape(small.shape, F32),
        ),
        in_specs=[vmem()] * 5,
        out_specs=(vmem(),) * 3,
        compiler_params=params(56),
        cost_estimate=cost(2**20, 2**20),
    )(own, *messages, small)


def end_kernel(d_own, d1, d2, d3, inner, d_hidden, rows_in, rms, gain, grad, gain_grad):
    rows, width = d_own.shape
    total = d_own[...]
    line = inner[...]
    for d in (d1, d2, d3):
        total = total + d[:rows].astype(F32)
        high = [d[rows + 16 * i : rows + 16 * (i + 1)].astype(F32) for i in range(4)]
        line = line + jnp.concatenate(
            [high[0] + high[2], high[1] + high[3]], axis=1
        )
    column = lax.dot_general(
        line, jnp.full((16, width), 1.0 / 16, F32), (((0,), (0,)), ((), ())),
        precision=lax.Precision.HIGHEST, preferred_element_type=F32,
    )
    r = rms[...]
    xs = rows_in[...].astype(F32)
    gain_grad[...] = jnp.sum(total * xs * r, axis=0, keepdims=True)
    grad[...] = (
        d_hidden[...] + r * gain[...] * total - xs * (r * r * r / (CH * width)) * column
    ).astype(BF16)


def end(d_own, received, inner, d_hidden, rows_in, rms, gain):
    rows, width = d_own.shape
    return pl.pallas_call(
        end_kernel,
        out_shape=(shape((rows, width), BF16), shape((1, width), F32)),
        in_specs=[vmem()] * 9,
        out_specs=(vmem(),) * 2,
        compiler_params=params(56),
        cost_estimate=cost(2**32, 2**21),
    )(d_own, *received, inner, d_hidden, rows_in, rms, gain[None])


def norm_kernel(d_own, d1, d2, d3, h, rms, gain, cotangent, u, u_low, gain_grad):
    total = d_own[...]
    for d in (d1, d2, d3):
        total = total + d[...].astype(F32)
    r = rms[...]
    gain_grad[...] = jnp.sum(total * h[...] * r, axis=0, keepdims=True)
    full = cotangent[...].astype(F32) + r * gain[...] * total
    u[...] = full
    u_low[...] = full.astype(BF16)


def norm_back(d_own, received, h, rms, gain, cotangent):
    rows, width = d_own.shape
    return pl.pallas_call(
        norm_kernel,
        out_shape=(
            shape((rows, width), F32),
            shape((rows, width), BF16),
            shape((1, width), F32),
        ),
        in_specs=[vmem()] * 8,
        out_specs=(vmem(),) * 3,
        compiler_params=params(56),
        cost_estimate=cost(LONG, 2**21),
    )(d_own, *received, h, rms, gain[None], cotangent)


def mid_kernel(
    at, u_own, u1, u2, u3, h, rms, cotangent, weight, c_gate, conv_out,
    d_branch, d_hidden, d_conv, d_cgate, edge,
):
    x = at[0]
    width = u_own.shape[1]
    dot = jnp.zeros((u_own.shape[0], 1), F32)
    us = (u_own, u1, u2, u3)
    for j, u in enumerate(us):
        g = cotangent[:, rel_rows(x, j, width)].astype(F32)
        hj = h[:, j * width : (j + 1) * width]
        dot = dot + jnp.sum((u[...].astype(F32) - g) * hj, axis=1, keepdims=True)
    r = rms[...]
    scale = dot * (r * r / (CH * width))
    d_mixed = jnp.zeros(u_own.shape, F32)
    for j, u in enumerate(us):
        columns = slice(j * width, (j + 1) * width)
        full = u[...].astype(F32) - h[:, columns] * scale
        if j == 0:
            d_hidden[...] = full
        rounded = full.astype(BF16)
        d_branch[:, columns] = rounded
        d_mixed = d_mixed + dot_nn(rounded, weight[rel_rows(x, j, width), :])
    product = d_mixed * c_gate[...]
    d_conv[...] = product
    edge[...] = product[:8]
    d_cgate[...] = (d_mixed * conv_out[...]).astype(BF16)


def mid(at, pieces, h, rms, cotangent, weight, c_gate, conv_out):
    rows, width = c_gate.shape
    wide = shape((rows, width), F32)
    return pl.pallas_call(
        mid_kernel,
        out_shape=(
            shape((rows, CH * width), BF16),
            wide,
            wide,
            shape((rows, width), BF16),
            shape((8, width), F32),
        ),
        in_specs=[smem()] + [vmem()] * 10,
        out_specs=(vmem(),) * 5,
        compiler_params=params(56),
        cost_estimate=cost(rows * CH * width * width, 6 * 2**20),
    )(at, *pieces, h, rms, cotangent, weight, c_gate, conv_out)


def back_kernel(
    at, p0, p1, p2, p3, d_conv, following, taps, value, b_gate, d_cgate, gain, weight,
    grads, d_own, d1, d2, d3, inner, held, sem,
):
    x, count = at[0], at[2]
    rows, width = p0.shape
    copies = [
        pltpu.make_async_copy(
            weight.at[:, rel_rows(x, j, width), :],
            held.at[:, pl.ds(j * width, width), :],
            sem.at[j],
        )
        for j in range(CH)
    ]
    for copy in copies:
        copy.start()
    token = lax.broadcasted_iota(jnp.int32, (rows, width), 0)
    d = d_conv[...]
    next_one, next_two = following[0:1, :], following[1:2, :]
    after_one = jnp.where(token + 1 == count, 0.0, pltpu.roll(d, rows - 1, 0))
    after_one = jnp.where(token == rows - 1, next_one, after_one)
    after_two = pltpu.roll(d, rows - 2, 0)
    after_two = jnp.where((token + 2 == count) | (token + 1 == count), 0.0, after_two)
    after_two = jnp.where(token == rows - 2, next_one, after_two)
    after_two = jnp.where(token == rows - 1, next_two, after_two)
    d_gated = taps[0:1, :] * d + taps[1:2, :] * after_one + taps[2:3, :] * after_two
    grads[:, :width] = (d_gated * value[...]).astype(BF16)
    grads[:, width : 2 * width] = d_cgate[...]
    grads[:, 2 * width :] = (d_gated * b_gate[...]).astype(BF16)
    total = jnp.zeros((rows, width), F32)
    for j, piece in enumerate((p0, p1, p2, p3)):
        copies[j].wait()
        block = slice(j * width, (j + 1) * width)
        term = dot_nt(grads[:, :width], held[0, block, :])
        for k in (1, 2):
            term = term + dot_nt(grads[:, k * width : (k + 1) * width], held[k, block, :])
        scale = gain[:, rel_rows(x, j, width)]
        total = total + scale * term * piece[...].astype(F32)
        if j == 0:
            d_own[...] = term
        else:
            (d1, d2, d3)[j - 1][:rows, :] = term.astype(BF16)
    ones = jnp.ones((16, width), F32)
    row = lax.dot_general(
        ones, total, (((1,), (1,)), ((), ())),
        precision=lax.Precision.HIGHEST, preferred_element_type=F32,
    )
    inner[...] = row
    high = row.astype(BF16)
    low = (row - high.astype(F32)).astype(BF16)
    for out in (d1, d2, d3):
        out[rows : rows + 16, :] = high[:, :width]
        out[rows + 16 : rows + 32, :] = high[:, width:]
        out[rows + 32 : rows + 48, :] = low[:, :width]
        out[rows + 48 : rows + 64, :] = low[:, width:]


def back_project(at, pieces, d_conv, following, taps, value, b_gate, d_cgate, gain, weight):
    rows, width = pieces[0].shape
    features = CH * width
    block = shape((rows + 64, width), BF16)
    return pl.pallas_call(
        back_kernel,
        out_shape=(
            shape((rows, 3 * width), BF16),
            shape((rows, width), F32),
            block,
            block,
            block,
            shape((16, rows), F32),
        ),
        in_specs=[smem()] + [vmem()] * 11 + [anywhere()],
        out_specs=(vmem(),) * 6,
        scratch_shapes=[
            pltpu.VMEM((3, features, width), BF16),
            pltpu.SemaphoreType.DMA((CH,)),
        ],
        compiler_params=params(56),
        cost_estimate=cost(rows * features * 3 * width, 6 * 2**20),
    )(at, *pieces, d_conv, following, taps, value, b_gate, d_cgate, gain[None], weight)


def scatter_groups(array, groups):
    return lax.psum_scatter(array, "seq", scatter_dimension=0, axis_index_groups=groups)


def shards(
    block_input,
    segment_ids,
    norm1_gain,
    in_weight,
    conv_weight,
    out_weight,
    norm2_gain,
    ffn_in_weight,
    ffn_out_weight,
    out_grad,
):
    x = lax.axis_index("ch")
    seq = lax.axis_index("seq")
    core, z, y = seq % 2, (seq // 2) % 4, seq // 8
    features = norm1_gain.shape[0]
    width = block_input.shape[1]
    hidden_units = ffn_out_weight.shape[1]

    def rolled(array):
        blocks = array.reshape((CH, width) + array.shape[1:])
        return jnp.concatenate([pick(blocks, (x + j) % CH, 0) for j in range(CH)], axis=0)

    count = first_count(segment_ids)
    at = jnp.stack([x, core, count, z, y]).astype(jnp.int32)
    own_one = pick(norm1_gain.reshape(CH, width), x, 0)
    own_two = pick(norm2_gain.reshape(CH, width), x, 0)
    in_planes = jnp.transpose(in_weight, (1, 0, 2))

    pieces = gather_ch(block_input)
    half_rows = out_weight.shape[0] // 2
    half = lax.dynamic_slice_in_dim(out_weight, core * half_rows, half_rows, 0)
    half_pieces = gather_ch(half)
    grad_full = lax.all_gather(out_grad, "ch", axis=1, tiled=True)

    normed_one, r_one, b_gate, c_gate, value_rows, gated_rows, edge = in_project(
        at, pieces, norm1_gain, in_planes
    )
    carried = from_behind(edge, "seq", 1)
    mixed_rows, conv_out, current, prior_one, prior_two = convolve(
        at, gated_rows, carried, c_gate, conv_weight
    )

    mixed_pieces = gather_ch(mixed_rows)
    *half_pieces, ffn_weight, _ = tie(*half_pieces, ffn_in_weight, mixed_rows)
    ffn_planes = jnp.transpose(ffn_weight, (1, 0, 2))
    half_full = join_columns(half_pieces, 2**20)
    gain_row = copy_row(tie(norm2_gain, mixed_rows)[0][None])
    ffn_planes, gain_row = tie(ffn_planes, gain_row)
    other_half = lax.ppermute(half_full, "seq", seq_pairs(0, 0, 1))
    (
        hidden,
        hidden_own,
        r_two,
        normed_two,
        act_rows,
        d_gate_up,
        d_own,
        d_one,
        d_two,
        d_three,
        *down_parts,
    ) = ffn(
        at,
        pieces,
        mixed_pieces,
        gain_row,
        half_full,
        other_half,
        ffn_planes,
        ffn_out_weight,
        grad_full,
    )
    received = [
        lax.ppermute(d, "ch", ch_pairs(j)) for j, d in ((2, d_two), (1, d_one), (3, d_three))
    ]
    *gives, keep = pair_products(at, normed_two, d_gate_up, grad_full, act_rows, True, False)
    got = swap_cores(gives)

    u_own, u_low, grad_gain_two = norm_back(
        d_own, received, hidden_own, r_two, own_two, out_grad
    )
    u_pieces = [u_own] + gather_ch(u_low)[1:]
    ffn_kept = add_cores(keep, got)
    ffn_kept, *u_pieces = tie(ffn_kept, *u_pieces)
    groups = [[seq_index(i, k, c) for k in range(4)] for i in range(4) for c in range(2)]
    ffn_sum = scatter_groups(ffn_kept, groups)

    d_branch, d_hidden, d_conv, d_cgate, edge = mid(
        at, u_pieces, hidden, r_two, grad_full, out_weight, c_gate, conv_out
    )
    following = from_behind(edge, "seq", -1)
    d_proj, d_own, d_one, d_two, d_three, inner = back_project(
        at, pieces, d_conv, following, conv_weight, value_rows, b_gate, d_cgate, norm1_gain,
        in_planes,
    )
    received = [lax.ppermute(d, "ch", ch_pairs(j)) for j, d in ((2, d_two), (1, d_one), (3, d_three))]

    *gives, keep = pair_products(at, normed_one, d_proj, d_branch, mixed_rows, True, True)
    got = swap_cores(gives)
    grad_conv = jnp.stack(
        [
            jnp.sum(d_conv * current.astype(F32), axis=0),
            jnp.sum(d_conv * prior_one.astype(F32), axis=0),
            jnp.sum(d_conv * prior_two.astype(F32), axis=0),
        ],
        axis=0,
    )
    input_grad, grad_gain_one = end(
        d_own, received, inner, d_hidden, block_input, r_one, own_one
    )
    small = jnp.concatenate(
        [grad_conv, grad_gain_one, grad_gain_two, jnp.zeros((3, width), F32)], axis=0
    )
    small = small + lax.ppermute(small, "seq", seq_pairs(0, 0, 1))
    small, ffn_sum, *got = tie(small, ffn_sum, *got)
    own, *messages = send_z(at, keep, got, small)
    down_parts, messages = lax.optimization_barrier((down_parts, messages))
    downs = [lax.ppermute(down_parts[j], "ch", ch_pairs(j)) for j in (2, 1, 3)]
    messages = [
        lax.ppermute(m, "seq", seq_pairs(0, j, 0)) for j, m in ((2, messages[1]), (1, messages[0]), (3, messages[2]))
    ]
    downs, messages = lax.optimization_barrier((downs, messages))
    block_output = hidden_own + down_parts[0].astype(F32)
    for down in downs:
        block_output = block_output + down.astype(F32)
    block_output = block_output.astype(BF16)
    own, *messages, small = turn(at, own, messages, small)
    messages = [
        lax.ppermute(m, "seq", seq_pairs(j, 0, 0)) for j, m in ((2, messages[1]), (1, messages[0]), (3, messages[2]))
    ]
    grad_in, grad_out, small = last(own, messages, small)

    groups = [[seq_index(k, i, c) for k in range(4)] for i in range(4) for c in range(2)]
    ffn_sum = scatter_groups(ffn_sum, groups).astype(F32)
    grad_ffn_in = ffn_sum[:, : 2 * hidden_units].reshape(-1, 2, hidden_units)
    grad_ffn_out = ffn_sum[:, 2 * hidden_units :]
    return (
        block_output,
        input_grad,
        small[3],
        jnp.transpose(grad_in, (1, 0, 2)),
        small[:3],
        grad_out,
        small[4],
        grad_ffn_in,
        grad_ffn_out,
    )


def solution(mesh):
    return jax.shard_map(
        shards,
        mesh=mesh,
        in_specs=(
            P("seq", "ch"),
            P("seq"),
            P(),
            P(None, None, "ch"),
            P(None, "ch"),
            P(None, "ch"),
            P(),
            P(None, None, "ch"),
            P(None, "ch"),
            P("seq", "ch"),
        ),
        out_specs=(
            P("seq", "ch"),
            P("seq", "ch"),
            P("ch"),
            P("seq", None, "ch"),
            P(None, "ch"),
            P("seq", "ch"),
            P("ch"),
            P("seq", None, "ch"),
            P("seq", "ch"),
        ),
        check_vma=False,
    )
```

```python
import jax
import jax.numpy as jnp
from jax import lax
from jax.experimental import pallas as pl
from jax.experimental.pallas import tpu as pltpu
from jax.sharding import PartitionSpec as P

EPS = 1e-05
F32 = jnp.float32
BF16 = jnp.bfloat16
CH = 4
LONG = 2**36


def seq_index(y, z, core):
    return ((y % 4) * 4 + z % 4) * 2 + core


def seq_pairs(dy, dz, dcore):
    return [
        (seq_index(y, z, core), seq_index(y + dy, z + dz, core ^ dcore))
        for y in range(4)
        for z in range(4)
        for core in range(2)
    ]


def ch_pairs(step):
    return [(i, (i + step) % CH) for i in range(CH)]


def gather_ch(block):
    far = lax.ppermute(block, "ch", ch_pairs(2))
    near = [lax.ppermute(block, "ch", ch_pairs(-j)) for j in (1, 3)]
    return [block, near[0], far, near[1]]


def scatter_ch(chunks):
    total = chunks[0]
    for j in range(1, CH):
        total = total + lax.ppermute(chunks[j], "ch", ch_pairs(j)).astype(F32)
    return total


def sum_ch(vector):
    total = vector
    for j in range(1, CH):
        total = total + lax.ppermute(vector, "ch", ch_pairs(j))
    return total


def pick(array, index, axis):
    return lax.dynamic_index_in_dim(array, index, axis, keepdims=False)


def from_behind(array, axis, by):
    size = lax.axis_size(axis)
    pairs = [(i, i + by) for i in range(size) if 0 <= i + by < size]
    return lax.ppermute(array, axis, pairs)


def first_count(segment_ids):
    return jnp.sum((segment_ids == segment_ids[0]).astype(jnp.int32))


def tie(*arrays):
    return lax.optimization_barrier(arrays)


def reduce_axis(array, axis, me, along_y):
    total = pick(array, me, axis).astype(F32)
    for step in (1, 3, 2):
        pairs = seq_pairs(step, 0, 0) if along_y else seq_pairs(0, step, 0)
        total = total + lax.ppermute(pick(array, (me + step) % 4, axis), "seq", pairs).astype(F32)
    return total


def dot_nt(a, b):
    return lax.dot_general(a, b, (((1,), (1,)), ((), ())), preferred_element_type=F32)


def dot_tn(a, b):
    return lax.dot_general(a, b, (((0,), (0,)), ((), ())), preferred_element_type=F32)


def dot_nn(a, b):
    return lax.dot_general(a, b, (((1,), (0,)), ((), ())), preferred_element_type=F32)


def rel_rows(x, j, width):
    return pl.ds(pl.multiple_of(lax.rem(x + j, CH) * width, width), width)


def vmem():
    return pl.BlockSpec(memory_space=pltpu.VMEM)


def smem():
    return pl.BlockSpec(memory_space=pltpu.SMEM)


def anywhere():
    return pl.BlockSpec(memory_space=pl.ANY)


def shape(dims, dtype):
    return jax.ShapeDtypeStruct(dims, dtype)


def params(megabytes):
    return pltpu.CompilerParams(vmem_limit_bytes=megabytes * 1024 * 1024)


def cost(macs, nbytes):
    return pl.CostEstimate(flops=2 * macs, bytes_accessed=nbytes, transcendentals=0)


def in_kernel(at, p0, p1, p2, p3, gain, weight, normed, rms, b_out, c_out, v_out, gated, edge, held, sem):
    x = at[0]
    width = p0.shape[1]
    copies = [
        pltpu.make_async_copy(
            weight.at[:, rel_rows(x, j, width), :],
            held.at[:, pl.ds(j * width, width), :],
            sem.at[j],
        )
        for j in range(CH)
    ]
    for copy in copies:
        copy.start()
    pieces = [p0, p1, p2, p3]
    square = jnp.zeros((p0.shape[0], 1), F32)
    for piece in pieces:
        rows = piece[...].astype(F32)
        square = square + jnp.sum(rows * rows, axis=1, keepdims=True)
    r = lax.rsqrt(square / (CH * width) + EPS)
    rms[...] = r
    for j, piece in enumerate(pieces):
        scale = gain[:, rel_rows(x, j, width)]
        normed[:, j * width : (j + 1) * width] = (piece[...].astype(F32) * r * scale).astype(BF16)
    for copy in copies:
        copy.wait()
    b = dot_nn(normed[...], held[0])
    v = dot_nn(normed[...], held[2])
    b_out[...] = b
    v_out[...] = v
    product = (b * v).astype(BF16)
    gated[...] = product
    edge[...] = product[-16:]
    c_out[...] = dot_nn(normed[...], held[1])


def in_project(at, pieces, gain, weight):
    rows, width = pieces[0].shape
    features = CH * width
    out = shape((rows, width), F32)
    return pl.pallas_call(
        in_kernel,
        out_shape=(
            shape((rows, features), BF16),
            shape((rows, 1), F32),
            out,
            out,
            out,
            shape((rows, width), BF16),
            shape((16, width), BF16),
        ),
        in_specs=[smem()] + [vmem()] * 5 + [anywhere()],
        out_specs=(vmem(),) * 7,
        scratch_shapes=[
            pltpu.VMEM((3, features, width), BF16),
            pltpu.SemaphoreType.DMA((CH,)),
        ],
        compiler_params=params(56),
        cost_estimate=cost(rows * features * 3 * width, 6 * 2**20),
    )(at, *pieces, gain[None], weight)


def columns_kernel(p0, p1, p2, p3, out):
    width = p0.shape[1]
    for j, piece in enumerate((p0, p1, p2, p3)):
        out[:, j * width : (j + 1) * width] = piece[...]


def join_columns(pieces, weight):
    rows, width = pieces[0].shape
    return pl.pallas_call(
        columns_kernel,
        out_shape=shape((rows, CH * width), BF16),
        in_specs=[vmem()] * CH,
        out_specs=vmem(),
        compiler_params=params(56),
        cost_estimate=cost(weight, 2**21),
    )(*pieces)


def conv_kernel(at, gated, carried, c_gate, taps, mixed, conv_out, one_out, two_out):
    count = at[2]
    rows, width = gated.shape
    token = lax.broadcasted_iota(jnp.int32, (rows, width), 0)
    current = gated[...].astype(F32)
    before = carried[...].astype(F32)
    last, second = before[15:16], before[14:15]
    one = jnp.where(token == 0, last, pltpu.roll(current, 1, 0))
    one = jnp.where(token == count, 0.0, one)
    two = jnp.where(token == 0, second, pltpu.roll(current, 2, 0))
    two = jnp.where(token == 1, last, two)
    two = jnp.where((token == count) | (token == count + 1), 0.0, two)
    out = taps[0:1] * current + taps[1:2] * one + taps[2:3] * two
    mixed[...] = (c_gate[...] * out).astype(BF16)
    conv_out[...] = out
    one_out[...] = one.astype(BF16)
    two_out[...] = two.astype(BF16)


def convolve(at, gated, carried, c_gate, taps):
    rows, width = gated.shape
    low = shape((rows, width), BF16)
    mixed, out, one, two = pl.pallas_call(
        conv_kernel,
        out_shape=(low, shape((rows, width), F32), low, low),
        in_specs=[smem()] + [vmem()] * 4,
        out_specs=(vmem(),) * 4,
        compiler_params=params(56),
        cost_estimate=cost(2**22, 2**21),
    )(at, gated, carried, c_gate, taps)
    return mixed, out, gated, one, two


def copy_kernel(row, out):
    out[...] = row[...]


def copy_row(row):
    return pl.pallas_call(
        copy_kernel,
        out_shape=shape(row.shape, F32),
        in_specs=[vmem()],
        out_specs=vmem(),
        compiler_params=params(56),
        cost_estimate=cost(LONG, 2**13),
    )(row)


def ffn_kernel(
    at,
    x0, x1, x2, x3,
    m0, m1, m2, m3,
    gain,
    half,
    other,
    planes,
    down,
    cotangent,
    h_out, h_own, rms, normed_out, act_out, d_out, d_own, d1, d2, d3, f0, f1, f2, f3,
    w_out, w_in, w_down, g_rows, mixed, acc, down_acc, h, normed, act, d_gate_up, sem, out_sem,
):
    x, core = at[0], at[1]
    leaving = []

    def leave(source, target):
        copy = pltpu.make_async_copy(source, target, out_sem.at[len(leaving)])
        copy.start()
        leaving.append(copy)

    width = x0.shape[1]
    units = down.shape[1]
    step = units // 3
    halves = [
        pltpu.make_async_copy(half, w_out.at[0], sem.at[0]),
        pltpu.make_async_copy(other, w_out.at[1], sem.at[1]),
    ]
    planes_in = [
        pltpu.make_async_copy(
            planes.at[:, rel_rows(x, j, width), :],
            w_in.at[:, pl.ds(j * width, width), :],
            sem.at[2 + j],
        )
        for j in range(CH)
    ]
    rest = [
        pltpu.make_async_copy(cotangent, g_rows, sem.at[6]),
        pltpu.make_async_copy(down, w_down, sem.at[7]),
    ]
    for copy in halves + planes_in + rest:
        copy.start()
    for j, piece in enumerate((m0, m1, m2, m3)):
        mixed[:, j * width : (j + 1) * width] = piece[...]
    for copy in halves:
        copy.wait()
    square = jnp.zeros((x0.shape[0], 1), F32)
    for j, piece in enumerate((x0, x1, x2, x3)):
        block = lax.rem(x + j, CH)
        which = lax.rem(block // 2 + core, 2)
        rows = pl.ds(pl.multiple_of(lax.rem(block, 2) * width, width), width)
        hj = piece[...].astype(F32) + dot_nt(mixed[...], w_out[which, rows, :])
        h[:, j * width : (j + 1) * width] = hj
        square = square + jnp.sum(hj * hj, axis=1, keepdims=True)
    r = lax.rsqrt(square / (CH * width) + EPS)
    rms[...] = r
    h_own[...] = h[:, :width]
    for j in range(CH):
        columns = slice(j * width, (j + 1) * width)
        scale = gain[:, rel_rows(x, j, width)]
        normed[:, columns] = (h[:, columns] * r * scale).astype(BF16)
    leave(h, h_out)
    leave(normed, normed_out)
    for copy in planes_in + rest:
        copy.wait()

    for i in range(3):
        f = slice(i * step, (i + 1) * step)
        f_up = slice(units + i * step, units + (i + 1) * step)
        gate = dot_nn(normed[...], w_in[0, :, f])
        up = dot_nn(normed[...], w_in[1, :, f])
        d_act = dot_nn(g_rows[...], w_down[:, f])
        sigma = jax.nn.sigmoid(gate)
        swish = gate * sigma
        active = (swish * up).astype(BF16)
        act[:, f] = active
        for j in range(CH):
            rows = slice(j * width, (j + 1) * width)
            term = dot_nt(active, w_down[rows, f])
            down_acc[j] = term if i == 0 else down_acc[j] + term
        d_gate = (d_act * up * sigma * (1.0 + gate * (1.0 - sigma))).astype(BF16)
        d_up = (d_act * swish).astype(BF16)
        d_gate_up[:, f] = d_gate
        d_gate_up[:, f_up] = d_up
        leave(act.at[:, f], act_out.at[:, f])
        leave(d_gate_up.at[:, f], d_out.at[:, f])
        leave(d_gate_up.at[:, f_up], d_out.at[:, f_up])
        for j in range(CH):
            rows = slice(j * width, (j + 1) * width)
            term = dot_nt(d_gate, w_in[0, rows, f]) + dot_nt(d_up, w_in[1, rows, f])
            acc[j] = term if i == 0 else acc[j] + term
    d_own[...] = acc[0]
    d1[...] = acc[1].astype(BF16)
    d2[...] = acc[2].astype(BF16)
    d3[...] = acc[3].astype(BF16)
    for j, out in enumerate((f0, f1, f2, f3)):
        out[...] = down_acc[lax.rem(x + j, CH)].astype(BF16)
    for copy in leaving:
        copy.wait()


def ffn(at, pieces, mixed_pieces, gain, half, other, planes, down, cotangent):
    rows, width = pieces[0].shape
    features = CH * width
    units = down.shape[1]
    block = shape((rows, width), BF16)
    return pl.pallas_call(
        ffn_kernel,
        out_shape=(
            shape((rows, features), F32),
            shape((rows, width), F32),
            shape((rows, 1), F32),
            shape((rows, features), BF16),
            shape((rows, units), BF16),
            shape((rows, 2 * units), BF16),
            shape((rows, width), F32),
        )
        + (block,) * 7,
        in_specs=[smem()] + [vmem()] * 9 + [anywhere()] * 5,
        out_specs=(anywhere(), vmem(), vmem()) + (anywhere(),) * 3 + (vmem(),) * 8,
        scratch_shapes=[
            pltpu.VMEM((2, features // 2, features), BF16),
            pltpu.VMEM((2, features, units), BF16),
            pltpu.VMEM((features, units), BF16),
            pltpu.VMEM((rows, features), BF16),
            pltpu.VMEM((rows, features), BF16),
            pltpu.VMEM((CH, rows, width), F32),
            pltpu.VMEM((CH, rows, width), F32),
            pltpu.VMEM((rows, features), F32),
            pltpu.VMEM((rows, features), BF16),
            pltpu.VMEM((rows, units), BF16),
            pltpu.VMEM((rows, 2 * units), BF16),
            pltpu.SemaphoreType.DMA((8,)),
            pltpu.SemaphoreType.DMA((11,)),
        ],
        compiler_params=params(56),
        cost_estimate=cost(rows * features * (features + 6 * units), 20 * 2**20),
    )(at, *pieces, *mixed_pieces, gain, half, other, planes, down, cotangent)


def pair_kernel(
    at, a_left, a_right, b_left, b_right, give_a, give_b, keep, held, *, a_rolled, b_rolled
):
    x, core = at[0], at[1]
    y = pl.program_id(0)
    wide = keep.shape[2] * 8
    turned = lax.rem(y + CH - x, CH)
    cut = a_right.shape[1]
    for left, right, rolled, base in (
        (a_left, a_right, a_rolled, 0),
        (b_left, b_right, b_rolled, cut),
    ):
        where = turned if rolled else y
        block = left[:, pl.ds(pl.multiple_of(where * wide, wide), wide)]
        columns = right.shape[1]
        step = columns // 3 if columns % 384 == 0 else columns
        for first in range(0, columns, step):
            held[:, base + first : base + first + step] = dot_tn(
                block, right[:, first : first + step]
            )
    for z in range(4):
        mine = pl.multiple_of((2 * z + core) * 32, 32)
        theirs = pl.multiple_of((2 * z + 1 - core) * 32, 32)
        keep[z, 0] = held[pl.ds(mine, 32), :].astype(BF16)
        (give_a, give_b)[z // 2][z % 2, 0] = held[pl.ds(theirs, 32), :].astype(BF16)


def pair_products(at, a_left, a_right, b_left, b_right, a_rolled, b_rolled):
    columns = a_right.shape[1] + b_right.shape[1]
    tokens, features = a_left.shape
    out = shape((4, 4, features // 32, columns), BF16)
    spec = pl.BlockSpec((4, 1, features // 32, columns), lambda y: (0, y, 0, 0))
    half = shape((2, 4, features // 32, columns), BF16)
    half_spec = pl.BlockSpec((2, 1, features // 32, columns), lambda y: (0, y, 0, 0))

    def body(*refs):
        pair_kernel(*refs, a_rolled=a_rolled, b_rolled=b_rolled)

    return pl.pallas_call(
        body,
        grid=(4,),
        out_shape=(half, half, out),
        in_specs=[smem()] + [vmem()] * 4,
        out_specs=(half_spec, half_spec, spec),
        scratch_shapes=[pltpu.VMEM((features // 4, columns), F32)],
        compiler_params=params(56),
        cost_estimate=cost(tokens * features * columns, 4 * features * columns),
    )(at, a_left, a_right, b_left, b_right)


def swap_cores(halves):
    return [lax.ppermute(half, "seq", seq_pairs(0, 0, 1)) for half in halves]


def add_kernel(keep, got_a, got_b, out):
    out[:2] = (keep[:2].astype(F32) + got_a[...].astype(F32)).astype(BF16)
    out[2:] = (keep[2:].astype(F32) + got_b[...].astype(F32)).astype(BF16)


def add_cores(keep, got):
    spec = pl.BlockSpec((4, 1) + keep.shape[2:], lambda y: (0, y, 0, 0))
    half = pl.BlockSpec((2, 1) + keep.shape[2:], lambda y: (0, y, 0, 0))
    return pl.pallas_call(
        add_kernel,
        grid=(4,),
        out_shape=shape(keep.shape, BF16),
        in_specs=[spec, half, half],
        out_specs=spec,
        compiler_params=params(56),
        cost_estimate=cost(2**20, 6 * keep.size),
    )(keep, *got)


def spread(small):
    high = small.astype(BF16)
    low = (small - high.astype(F32)).astype(BF16)
    return high, low


def join(message, width):
    return message[:8, :width].astype(F32) + message[:8, width : 2 * width].astype(F32)


def send_kernel(at, keep, got_a, got_b, small, own, m1, m2, m3):
    z = at[3]
    rows = own.shape[0]
    width = small.shape[1]
    for j, out in enumerate((own, m1, m2, m3)):
        block = lax.rem(z + j, 4)
        inside = lax.rem(block, 2)
        got = jnp.where(block < 2, got_a[inside].astype(F32), got_b[inside].astype(F32))
        total = keep[block].astype(F32) + got
        out[:rows] = total.reshape(own.shape).astype(out.dtype)
    high, low = spread(jnp.concatenate([small[...], jnp.zeros_like(small[...])], axis=0))
    for out in (m1, m2, m3):
        out[rows:, :width] = high
        out[rows:, width : 2 * width] = low


def send_z(at, keep, got, small):
    rows, columns = keep.shape[1] * keep.shape[2], keep.shape[3]
    message = shape((rows + 16, columns), BF16)
    return pl.pallas_call(
        send_kernel,
        out_shape=(shape((rows, columns), F32), message, message, message),
        in_specs=[smem()] + [vmem()] * 4,
        out_specs=(vmem(),) * 4,
        compiler_params=params(56),
        cost_estimate=cost(2**20, 2**22),
    )(at, keep, *got, small)


def turn_kernel(at, own, m1, m2, m3, small, left, n1, n2, n3, small_out, total):
    y = at[4]
    rows = own.shape[0]
    width = small.shape[1]
    total[...] = own[...]
    small_sum = small[...]
    for m in (m1, m2, m3):
        total[...] += m[:rows].astype(F32)
        small_sum = small_sum + join(m[rows:], width)
    small_out[...] = small_sum
    part = rows // 4
    for j, out in enumerate((left, n1, n2, n3)):
        block = pl.multiple_of(lax.rem(y + j, 4) * part, part)
        out[:part] = total[pl.ds(block, part)].astype(out.dtype)
    high, low = spread(jnp.concatenate([small_sum, jnp.zeros_like(small_sum)], axis=0))
    for out in (n1, n2, n3):
        out[part:, :width] = high
        out[part:, width : 2 * width] = low


def turn(at, own, messages, small):
    rows, columns = own.shape
    message = shape((rows // 4 + 16, columns), BF16)
    return pl.pallas_call(
        turn_kernel,
        out_shape=(
            shape((rows // 4, columns), F32),
            message,
            message,
            message,
            shape(small.shape, F32),
        ),
        in_specs=[smem()] + [vmem()] * 5,
        out_specs=(vmem(),) * 5,
        scratch_shapes=[pltpu.VMEM((rows, columns), F32)],
        compiler_params=params(56),
        cost_estimate=cost(2**20, 2**21),
    )(at, own, *messages, small)


def last_kernel(own, m1, m2, m3, small, in_out, out_out, conv_out, gain_one, gain_two):
    rows = own.shape[0]
    width = small.shape[1]
    total = own[...]
    small_sum = small[...]
    for m in (m1, m2, m3):
        total = total + m[:rows].astype(F32)
        small_sum = small_sum + join(m[rows:], width)
    for k in range(3):
        in_out[k] = total[:, k * width : (k + 1) * width]
    out_out[...] = total[:, 3 * width :]
    conv_out[...] = small_sum[:3]
    gain_one[...] = small_sum[3:4]
    gain_two[...] = small_sum[4:5]


def last(own, messages, small):
    rows, columns = own.shape
    width = small.shape[1]
    return pl.pallas_call(
        last_kernel,
        out_shape=(
            shape((3, rows, width), F32),
            shape((rows, columns - 3 * width), F32),
            shape((3, width), F32),
            shape((1, width), F32),
            shape((1, width), F32),
        ),
        in_specs=[vmem()] * 5,
        out_specs=(vmem(),) * 5,
        compiler_params=params(56),
        cost_estimate=cost(2**20, 2**20),
    )(own, *messages, small)


def end_kernel(
    d_own, d1, d2, d3, inner, d_hidden, rows_in, rms, gain, conv_grad, gain_two, grad, small
):
    rows, width = d_own.shape
    total = d_own[...]
    line = inner[...]
    for d in (d1, d2, d3):
        total = total + d[:rows].astype(F32)
        high = [d[rows + 16 * i : rows + 16 * (i + 1)].astype(F32) for i in range(4)]
        line = line + jnp.concatenate(
            [high[0] + high[2], high[1] + high[3]], axis=1
        )
    column = lax.dot_general(
        line, jnp.full((16, width), 1.0 / 16, F32), (((0,), (0,)), ((), ())),
        precision=lax.Precision.HIGHEST, preferred_element_type=F32,
    )
    r = rms[...]
    xs = rows_in[...].astype(F32)
    small[0:3] = conv_grad[...]
    small[3:4] = jnp.sum(total * xs * r, axis=0, keepdims=True)
    small[4:5] = gain_two[...]
    small[5:8] = jnp.zeros((3, width), F32)
    grad[...] = (
        d_hidden[...] + r * gain[...] * total - xs * (r * r * r / (CH * width)) * column
    ).astype(BF16)


def end(d_own, received, inner, d_hidden, rows_in, rms, gain, conv_grad, gain_two):
    rows, width = d_own.shape
    return pl.pallas_call(
        end_kernel,
        out_shape=(shape((rows, width), BF16), shape((8, width), F32)),
        in_specs=[vmem()] * 11,
        out_specs=(vmem(),) * 2,
        compiler_params=params(56),
        cost_estimate=cost(2**32, 2**21),
    )(d_own, *received, inner, d_hidden, rows_in, rms, gain[None], conv_grad, gain_two)


def norm_kernel(d_own, d1, d2, d3, h, rms, gain, cotangent, u, u_low, gain_grad):
    total = d_own[...]
    for d in (d1, d2, d3):
        total = total + d[...].astype(F32)
    r = rms[...]
    gain_grad[...] = jnp.sum(total * h[...] * r, axis=0, keepdims=True)
    full = cotangent[...].astype(F32) + r * gain[...] * total
    u[...] = full
    u_low[...] = full.astype(BF16)


def norm_back(d_own, received, h, rms, gain, cotangent):
    rows, width = d_own.shape
    return pl.pallas_call(
        norm_kernel,
        out_shape=(
            shape((rows, width), F32),
            shape((rows, width), BF16),
            shape((1, width), F32),
        ),
        in_specs=[vmem()] * 8,
        out_specs=(vmem(),) * 3,
        compiler_params=params(56),
        cost_estimate=cost(LONG, 2**21),
    )(d_own, *received, h, rms, gain[None], cotangent)


def mid_kernel(
    at, u_own, u1, u2, u3, h, rms, cotangent, weight, c_gate, conv_out,
    d_branch, d_hidden, d_conv, d_cgate, edge,
):
    x = at[0]
    width = u_own.shape[1]
    dot = jnp.zeros((u_own.shape[0], 1), F32)
    us = (u_own, u1, u2, u3)
    for j, u in enumerate(us):
        g = cotangent[:, rel_rows(x, j, width)].astype(F32)
        hj = h[:, j * width : (j + 1) * width]
        dot = dot + jnp.sum((u[...].astype(F32) - g) * hj, axis=1, keepdims=True)
    r = rms[...]
    scale = dot * (r * r / (CH * width))
    d_mixed = jnp.zeros(u_own.shape, F32)
    for j, u in enumerate(us):
        columns = slice(j * width, (j + 1) * width)
        full = u[...].astype(F32) - h[:, columns] * scale
        if j == 0:
            d_hidden[...] = full
        rounded = full.astype(BF16)
        d_branch[:, columns] = rounded
        d_mixed = d_mixed + dot_nn(rounded, weight[rel_rows(x, j, width), :])
    product = d_mixed * c_gate[...]
    d_conv[...] = product
    edge[...] = product[:8]
    d_cgate[...] = (d_mixed * conv_out[...]).astype(BF16)


def mid(at, pieces, h, rms, cotangent, weight, c_gate, conv_out):
    rows, width = c_gate.shape
    wide = shape((rows, width), F32)
    return pl.pallas_call(
        mid_kernel,
        out_shape=(
            shape((rows, CH * width), BF16),
            wide,
            wide,
            shape((rows, width), BF16),
            shape((8, width), F32),
        ),
        in_specs=[smem()] + [vmem()] * 10,
        out_specs=(vmem(),) * 5,
        compiler_params=params(56),
        cost_estimate=cost(rows * CH * width * width, 6 * 2**20),
    )(at, *pieces, h, rms, cotangent, weight, c_gate, conv_out)


def back_kernel(
    at, p0, p1, p2, p3, d_conv, following, taps, value, b_gate, d_cgate, gain, weight,
    grads, d_own, d1, d2, d3, inner, held, sem,
):
    x, count = at[0], at[2]
    rows, width = p0.shape
    copies = [
        pltpu.make_async_copy(
            weight.at[:, rel_rows(x, j, width), :],
            held.at[:, pl.ds(j * width, width), :],
            sem.at[j],
        )
        for j in range(CH)
    ]
    for copy in copies:
        copy.start()
    token = lax.broadcasted_iota(jnp.int32, (rows, width), 0)
    d = d_conv[...]
    next_one, next_two = following[0:1, :], following[1:2, :]
    after_one = jnp.where(token + 1 == count, 0.0, pltpu.roll(d, rows - 1, 0))
    after_one = jnp.where(token == rows - 1, next_one, after_one)
    after_two = pltpu.roll(d, rows - 2, 0)
    after_two = jnp.where((token + 2 == count) | (token + 1 == count), 0.0, after_two)
    after_two = jnp.where(token == rows - 2, next_one, after_two)
    after_two = jnp.where(token == rows - 1, next_two, after_two)
    d_gated = taps[0:1, :] * d + taps[1:2, :] * after_one + taps[2:3, :] * after_two
    grads[:, :width] = (d_gated * value[...]).astype(BF16)
    grads[:, width : 2 * width] = d_cgate[...]
    grads[:, 2 * width :] = (d_gated * b_gate[...]).astype(BF16)
    total = jnp.zeros((rows, width), F32)
    for j, piece in enumerate((p0, p1, p2, p3)):
        copies[j].wait()
        block = slice(j * width, (j + 1) * width)
        term = dot_nt(grads[:, :width], held[0, block, :])
        for k in (1, 2):
            term = term + dot_nt(grads[:, k * width : (k + 1) * width], held[k, block, :])
        scale = gain[:, rel_rows(x, j, width)]
        total = total + scale * term * piece[...].astype(F32)
        if j == 0:
            d_own[...] = term
        else:
            (d1, d2, d3)[j - 1][:rows, :] = term.astype(BF16)
    ones = jnp.ones((16, width), F32)
    row = lax.dot_general(
        ones, total, (((1,), (1,)), ((), ())),
        precision=lax.Precision.HIGHEST, preferred_element_type=F32,
    )
    inner[...] = row
    high = row.astype(BF16)
    low = (row - high.astype(F32)).astype(BF16)
    for out in (d1, d2, d3):
        out[rows : rows + 16, :] = high[:, :width]
        out[rows + 16 : rows + 32, :] = high[:, width:]
        out[rows + 32 : rows + 48, :] = low[:, :width]
        out[rows + 48 : rows + 64, :] = low[:, width:]


def back_project(at, pieces, d_conv, following, taps, value, b_gate, d_cgate, gain, weight):
    rows, width = pieces[0].shape
    features = CH * width
    block = shape((rows + 64, width), BF16)
    return pl.pallas_call(
        back_kernel,
        out_shape=(
            shape((rows, 3 * width), BF16),
            shape((rows, width), F32),
            block,
            block,
            block,
            shape((16, rows), F32),
        ),
        in_specs=[smem()] + [vmem()] * 11 + [anywhere()],
        out_specs=(vmem(),) * 6,
        scratch_shapes=[
            pltpu.VMEM((3, features, width), BF16),
            pltpu.SemaphoreType.DMA((CH,)),
        ],
        compiler_params=params(56),
        cost_estimate=cost(rows * features * 3 * width, 6 * 2**20),
    )(at, *pieces, d_conv, following, taps, value, b_gate, d_cgate, gain[None], weight)


def scatter_groups(array, groups):
    return lax.psum_scatter(array, "seq", scatter_dimension=0, axis_index_groups=groups)


def shards(
    block_input,
    segment_ids,
    norm1_gain,
    in_weight,
    conv_weight,
    out_weight,
    norm2_gain,
    ffn_in_weight,
    ffn_out_weight,
    out_grad,
):
    x = lax.axis_index("ch")
    seq = lax.axis_index("seq")
    core, z, y = seq % 2, (seq // 2) % 4, seq // 8
    features = norm1_gain.shape[0]
    width = block_input.shape[1]
    hidden_units = ffn_out_weight.shape[1]

    def rolled(array):
        blocks = array.reshape((CH, width) + array.shape[1:])
        return jnp.concatenate([pick(blocks, (x + j) % CH, 0) for j in range(CH)], axis=0)

    count = first_count(segment_ids)
    at = jnp.stack([x, core, count, z, y]).astype(jnp.int32)
    own_one = pick(norm1_gain.reshape(CH, width), x, 0)
    own_two = pick(norm2_gain.reshape(CH, width), x, 0)
    in_planes = jnp.transpose(in_weight, (1, 0, 2))

    pieces = gather_ch(block_input)
    half_rows = out_weight.shape[0] // 2
    half = lax.dynamic_slice_in_dim(out_weight, core * half_rows, half_rows, 0)
    half_pieces = gather_ch(half)
    grad_full = lax.all_gather(out_grad, "ch", axis=1, tiled=True)

    normed_one, r_one, b_gate, c_gate, value_rows, gated_rows, edge = in_project(
        at, pieces, norm1_gain, in_planes
    )
    carried = from_behind(edge, "seq", 1)
    mixed_rows, conv_out, current, prior_one, prior_two = convolve(
        at, gated_rows, carried, c_gate, conv_weight
    )

    mixed_pieces = gather_ch(mixed_rows)
    *half_pieces, ffn_weight, _ = tie(*half_pieces, ffn_in_weight, mixed_rows)
    ffn_planes = jnp.transpose(ffn_weight, (1, 0, 2))
    half_full = join_columns(half_pieces, 2**20)
    gain_row = copy_row(tie(norm2_gain, mixed_rows)[0][None])
    ffn_planes, gain_row = tie(ffn_planes, gain_row)
    other_half = lax.ppermute(half_full, "seq", seq_pairs(0, 0, 1))
    (
        hidden,
        hidden_own,
        r_two,
        normed_two,
        act_rows,
        d_gate_up,
        d_own,
        d_one,
        d_two,
        d_three,
        *down_parts,
    ) = ffn(
        at,
        pieces,
        mixed_pieces,
        gain_row,
        half_full,
        other_half,
        ffn_planes,
        ffn_out_weight,
        grad_full,
    )
    received = [
        lax.ppermute(d, "ch", ch_pairs(j)) for j, d in ((2, d_two), (1, d_one), (3, d_three))
    ]
    *gives, keep = pair_products(at, normed_two, d_gate_up, grad_full, act_rows, True, False)
    got = swap_cores(gives)

    u_own, u_low, grad_gain_two = norm_back(
        d_own, received, hidden_own, r_two, own_two, out_grad
    )
    u_pieces = [u_own] + gather_ch(u_low)[1:]
    ffn_kept = add_cores(keep, got)
    ffn_kept, *down_parts = tie(ffn_kept, *down_parts)
    downs = [lax.ppermute(down_parts[j], "ch", ch_pairs(j)) for j in (2, 1, 3)]
    ffn_kept, *u_pieces = tie(ffn_kept, *u_pieces)
    groups = [[seq_index(i, k, c) for k in range(4)] for i in range(4) for c in range(2)]
    ffn_sum = scatter_groups(ffn_kept, groups)

    d_branch, d_hidden, d_conv, d_cgate, edge = mid(
        at, u_pieces, hidden, r_two, grad_full, out_weight, c_gate, conv_out
    )
    following = from_behind(edge, "seq", -1)
    following, *downs = tie(following, *downs)
    d_proj, d_own, d_one, d_two, d_three, inner = back_project(
        at, pieces, d_conv, following, conv_weight, value_rows, b_gate, d_cgate, norm1_gain,
        in_planes,
    )
    block_output = hidden_own + down_parts[0].astype(F32)
    for down in downs:
        block_output = block_output + down.astype(F32)
    block_output = block_output.astype(BF16)
    received = [lax.ppermute(d, "ch", ch_pairs(j)) for j, d in ((2, d_two), (1, d_one), (3, d_three))]

    *gives, keep = pair_products(at, normed_one, d_proj, d_branch, mixed_rows, True, True)
    got = swap_cores(gives)
    grad_conv = jnp.stack(
        [
            jnp.sum(d_conv * current.astype(F32), axis=0),
            jnp.sum(d_conv * prior_one.astype(F32), axis=0),
            jnp.sum(d_conv * prior_two.astype(F32), axis=0),
        ],
        axis=0,
    )
    input_grad, small = end(
        d_own, received, inner, d_hidden, block_input, r_one, own_one, grad_conv, grad_gain_two
    )
    small = small + lax.ppermute(small, "seq", seq_pairs(0, 0, 1))
    small, ffn_sum, *got = tie(small, ffn_sum, *got)
    own, *messages = send_z(at, keep, got, small)
    messages = [
        lax.ppermute(m, "seq", seq_pairs(0, j, 0)) for j, m in ((2, messages[1]), (1, messages[0]), (3, messages[2]))
    ]
    own, *messages, small = turn(at, own, messages, small)
    messages = [
        lax.ppermute(m, "seq", seq_pairs(j, 0, 0)) for j, m in ((2, messages[1]), (1, messages[0]), (3, messages[2]))
    ]
    groups = [[seq_index(k, i, c) for k in range(4)] for i in range(4) for c in range(2)]
    ffn_sum = scatter_groups(ffn_sum, groups).astype(F32)
    grad_ffn_in = ffn_sum[:, : 2 * hidden_units].reshape(-1, 2, hidden_units)
    grad_ffn_out = ffn_sum[:, 2 * hidden_units :]
    grad_ffn_in, grad_ffn_out, *messages = tie(grad_ffn_in, grad_ffn_out, *messages)
    grad_in, grad_out, grad_conv, grad_gain_one, grad_gain_two = last(own, messages, small)
    return (
        block_output,
        input_grad,
        grad_gain_one.reshape(-1),
        jnp.transpose(grad_in, (1, 0, 2)),
        grad_conv,
        grad_out,
        grad_gain_two.reshape(-1),
        grad_ffn_in,
        grad_ffn_out,
    )


def solution(mesh):
    return jax.shard_map(
        shards,
        mesh=mesh,
        in_specs=(
            P("seq", "ch"),
            P("seq"),
            P(),
            P(None, None, "ch"),
            P(None, "ch"),
            P(None, "ch"),
            P(),
            P(None, None, "ch"),
            P(None, "ch"),
            P("seq", "ch"),
        ),
        out_specs=(
            P("seq", "ch"),
            P("seq", "ch"),
            P("ch"),
            P("seq", None, "ch"),
            P(None, "ch"),
            P("seq", "ch"),
            P("ch"),
            P("seq", None, "ch"),
            P("seq", "ch"),
        ),
        check_vma=False,
    )
```

```python
import jax
import jax.numpy as jnp
from jax import lax
from jax.experimental import pallas as pl
from jax.experimental.pallas import tpu as pltpu
from jax.sharding import PartitionSpec as P

EPS = 1e-05
F32 = jnp.float32
BF16 = jnp.bfloat16
CH = 4
LONG = 2**36


def seq_index(y, z, core):
    return ((y % 4) * 4 + z % 4) * 2 + core


def seq_pairs(dy, dz, dcore):
    return [
        (seq_index(y, z, core), seq_index(y + dy, z + dz, core ^ dcore))
        for y in range(4)
        for z in range(4)
        for core in range(2)
    ]


def ch_pairs(step):
    return [(i, (i + step) % CH) for i in range(CH)]


def gather_ch(block):
    far = lax.ppermute(block, "ch", ch_pairs(2))
    near = [lax.ppermute(block, "ch", ch_pairs(-j)) for j in (1, 3)]
    return [block, near[0], far, near[1]]


def scatter_ch(chunks):
    total = chunks[0]
    for j in range(1, CH):
        total = total + lax.ppermute(chunks[j], "ch", ch_pairs(j)).astype(F32)
    return total


def sum_ch(vector):
    total = vector
    for j in range(1, CH):
        total = total + lax.ppermute(vector, "ch", ch_pairs(j))
    return total


def pick(array, index, axis):
    return lax.dynamic_index_in_dim(array, index, axis, keepdims=False)


def from_behind(array, axis, by):
    size = lax.axis_size(axis)
    pairs = [(i, i + by) for i in range(size) if 0 <= i + by < size]
    return lax.ppermute(array, axis, pairs)


def first_count(segment_ids):
    return jnp.sum((segment_ids == segment_ids[0]).astype(jnp.int32))


def tie(*arrays):
    return lax.optimization_barrier(arrays)


def reduce_axis(array, axis, me, along_y):
    total = pick(array, me, axis).astype(F32)
    for step in (1, 3, 2):
        pairs = seq_pairs(step, 0, 0) if along_y else seq_pairs(0, step, 0)
        total = total + lax.ppermute(pick(array, (me + step) % 4, axis), "seq", pairs).astype(F32)
    return total


def dot_nt(a, b):
    return lax.dot_general(a, b, (((1,), (1,)), ((), ())), preferred_element_type=F32)


def dot_tn(a, b):
    return lax.dot_general(a, b, (((0,), (0,)), ((), ())), preferred_element_type=F32)


def dot_nn(a, b):
    return lax.dot_general(a, b, (((1,), (0,)), ((), ())), preferred_element_type=F32)


def rel_rows(x, j, width):
    return pl.ds(pl.multiple_of(lax.rem(x + j, CH) * width, width), width)


def vmem():
    return pl.BlockSpec(memory_space=pltpu.VMEM)


def smem():
    return pl.BlockSpec(memory_space=pltpu.SMEM)


def anywhere():
    return pl.BlockSpec(memory_space=pl.ANY)


def shape(dims, dtype):
    return jax.ShapeDtypeStruct(dims, dtype)


def params(megabytes):
    return pltpu.CompilerParams(vmem_limit_bytes=megabytes * 1024 * 1024)


def cost(macs, nbytes):
    return pl.CostEstimate(flops=2 * macs, bytes_accessed=nbytes, transcendentals=0)


def in_kernel(at, p0, p1, p2, p3, gain, weight, normed, rms, b_out, c_out, v_out, gated, edge, held, sem):
    x = at[0]
    width = p0.shape[1]
    copies = [
        pltpu.make_async_copy(
            weight.at[:, rel_rows(x, j, width), :],
            held.at[:, pl.ds(j * width, width), :],
            sem.at[j],
        )
        for j in range(CH)
    ]
    for copy in copies:
        copy.start()
    pieces = [p0, p1, p2, p3]
    square = jnp.zeros((p0.shape[0], 1), F32)
    for piece in pieces:
        rows = piece[...].astype(F32)
        square = square + jnp.sum(rows * rows, axis=1, keepdims=True)
    r = lax.rsqrt(square / (CH * width) + EPS)
    rms[...] = r
    for j, piece in enumerate(pieces):
        scale = gain[:, rel_rows(x, j, width)]
        normed[:, j * width : (j + 1) * width] = (piece[...].astype(F32) * r * scale).astype(BF16)
    for copy in copies:
        copy.wait()
    b = dot_nn(normed[...], held[0])
    v = dot_nn(normed[...], held[2])
    b_out[...] = b
    v_out[...] = v
    product = (b * v).astype(BF16)
    gated[...] = product
    edge[...] = product[-16:]
    c_out[...] = dot_nn(normed[...], held[1])


def in_project(at, pieces, gain, weight):
    rows, width = pieces[0].shape
    features = CH * width
    out = shape((rows, width), F32)
    return pl.pallas_call(
        in_kernel,
        out_shape=(
            shape((rows, features), BF16),
            shape((rows, 1), F32),
            out,
            out,
            out,
            shape((rows, width), BF16),
            shape((16, width), BF16),
        ),
        in_specs=[smem()] + [vmem()] * 5 + [anywhere()],
        out_specs=(vmem(),) * 7,
        scratch_shapes=[
            pltpu.VMEM((3, features, width), BF16),
            pltpu.SemaphoreType.DMA((CH,)),
        ],
        compiler_params=params(56),
        cost_estimate=cost(rows * features * 3 * width, 6 * 2**20),
    )(at, *pieces, gain[None], weight)


def columns_kernel(p0, p1, p2, p3, out):
    width = p0.shape[1]
    for j, piece in enumerate((p0, p1, p2, p3)):
        out[:, j * width : (j + 1) * width] = piece[...]


def join_columns(pieces, weight):
    rows, width = pieces[0].shape
    return pl.pallas_call(
        columns_kernel,
        out_shape=shape((rows, CH * width), BF16),
        in_specs=[vmem()] * CH,
        out_specs=vmem(),
        compiler_params=params(56),
        cost_estimate=cost(weight, 2**21),
    )(*pieces)


def conv_kernel(at, gated, carried, c_gate, taps, mixed, conv_out, one_out, two_out):
    count = at[2]
    rows, width = gated.shape
    token = lax.broadcasted_iota(jnp.int32, (rows, width), 0)
    current = gated[...].astype(F32)
    before = carried[...].astype(F32)
    last, second = before[15:16], before[14:15]
    one = jnp.where(token == 0, last, pltpu.roll(current, 1, 0))
    one = jnp.where(token == count, 0.0, one)
    two = jnp.where(token == 0, second, pltpu.roll(current, 2, 0))
    two = jnp.where(token == 1, last, two)
    two = jnp.where((token == count) | (token == count + 1), 0.0, two)
    out = taps[0:1] * current + taps[1:2] * one + taps[2:3] * two
    mixed[...] = (c_gate[...] * out).astype(BF16)
    conv_out[...] = out
    one_out[...] = one.astype(BF16)
    two_out[...] = two.astype(BF16)


def convolve(at, gated, carried, c_gate, taps):
    rows, width = gated.shape
    low = shape((rows, width), BF16)
    mixed, out, one, two = pl.pallas_call(
        conv_kernel,
        out_shape=(low, shape((rows, width), F32), low, low),
        in_specs=[smem()] + [vmem()] * 4,
        out_specs=(vmem(),) * 4,
        compiler_params=params(56),
        cost_estimate=cost(2**22, 2**21),
    )(at, gated, carried, c_gate, taps)
    return mixed, out, gated, one, two


def copy_kernel(row, out):
    out[...] = row[...]


def copy_row(row):
    return pl.pallas_call(
        copy_kernel,
        out_shape=shape(row.shape, F32),
        in_specs=[vmem()],
        out_specs=vmem(),
        compiler_params=params(56),
        cost_estimate=cost(LONG, 2**13),
    )(row)


def ffn_kernel(
    at,
    x0, x1, x2, x3,
    m0, m1, m2, m3,
    gain,
    half,
    other,
    planes,
    down,
    cotangent,
    h_out, h_own, rms, normed_out, act_out, d_out, d_own, d1, d2, d3, f0, f1, f2, f3,
    w_out, w_in, w_down, g_rows, mixed, acc, down_acc, h, normed, act, d_gate_up, sem, out_sem,
):
    x, core = at[0], at[1]
    leaving = []

    def leave(source, target):
        copy = pltpu.make_async_copy(source, target, out_sem.at[len(leaving)])
        copy.start()
        leaving.append(copy)

    width = x0.shape[1]
    units = down.shape[1]
    step = units // 3
    halves = [
        pltpu.make_async_copy(half, w_out.at[0], sem.at[0]),
        pltpu.make_async_copy(other, w_out.at[1], sem.at[1]),
    ]
    planes_in = [
        pltpu.make_async_copy(
            planes.at[:, rel_rows(x, j, width), :],
            w_in.at[:, pl.ds(j * width, width), :],
            sem.at[2 + j],
        )
        for j in range(CH)
    ]
    rest = [
        pltpu.make_async_copy(cotangent, g_rows, sem.at[6]),
        pltpu.make_async_copy(down, w_down, sem.at[7]),
    ]
    for copy in halves + planes_in + rest:
        copy.start()
    for j, piece in enumerate((m0, m1, m2, m3)):
        mixed[:, j * width : (j + 1) * width] = piece[...]
    for copy in halves:
        copy.wait()
    square = jnp.zeros((x0.shape[0], 1), F32)
    for j, piece in enumerate((x0, x1, x2, x3)):
        block = lax.rem(x + j, CH)
        which = lax.rem(block // 2 + core, 2)
        rows = pl.ds(pl.multiple_of(lax.rem(block, 2) * width, width), width)
        hj = piece[...].astype(F32) + dot_nt(mixed[...], w_out[which, rows, :])
        h[:, j * width : (j + 1) * width] = hj
        square = square + jnp.sum(hj * hj, axis=1, keepdims=True)
    r = lax.rsqrt(square / (CH * width) + EPS)
    rms[...] = r
    h_own[...] = h[:, :width]
    for j in range(CH):
        columns = slice(j * width, (j + 1) * width)
        scale = gain[:, rel_rows(x, j, width)]
        normed[:, columns] = (h[:, columns] * r * scale).astype(BF16)
    leave(h, h_out)
    leave(normed, normed_out)
    for copy in planes_in + rest:
        copy.wait()

    for i in range(3):
        f = slice(i * step, (i + 1) * step)
        f_up = slice(units + i * step, units + (i + 1) * step)
        gate = dot_nn(normed[...], w_in[0, :, f])
        up = dot_nn(normed[...], w_in[1, :, f])
        d_act = dot_nn(g_rows[...], w_down[:, f])
        sigma = jax.nn.sigmoid(gate)
        swish = gate * sigma
        active = (swish * up).astype(BF16)
        act[:, f] = active
        for j in range(CH):
            rows = slice(j * width, (j + 1) * width)
            term = dot_nt(active, w_down[rows, f])
            down_acc[j] = term if i == 0 else down_acc[j] + term
        d_gate = (d_act * up * sigma * (1.0 + gate * (1.0 - sigma))).astype(BF16)
        d_up = (d_act * swish).astype(BF16)
        d_gate_up[:, f] = d_gate
        d_gate_up[:, f_up] = d_up
        leave(act.at[:, f], act_out.at[:, f])
        leave(d_gate_up.at[:, f], d_out.at[:, f])
        leave(d_gate_up.at[:, f_up], d_out.at[:, f_up])
        for j in range(CH):
            rows = slice(j * width, (j + 1) * width)
            term = dot_nt(d_gate, w_in[0, rows, f]) + dot_nt(d_up, w_in[1, rows, f])
            acc[j] = term if i == 0 else acc[j] + term
    d_own[...] = acc[0]
    d1[...] = acc[1].astype(BF16)
    d2[...] = acc[2].astype(BF16)
    d3[...] = acc[3].astype(BF16)
    for j, out in enumerate((f0, f1, f2, f3)):
        out[...] = down_acc[lax.rem(x + j, CH)].astype(BF16)
    for copy in leaving:
        copy.wait()


def ffn(at, pieces, mixed_pieces, gain, half, other, planes, down, cotangent):
    rows, width = pieces[0].shape
    features = CH * width
    units = down.shape[1]
    block = shape((rows, width), BF16)
    return pl.pallas_call(
        ffn_kernel,
        out_shape=(
            shape((rows, features), F32),
            shape((rows, width), F32),
            shape((rows, 1), F32),
            shape((rows, features), BF16),
            shape((rows, units), BF16),
            shape((rows, 2 * units), BF16),
            shape((rows, width), F32),
        )
        + (block,) * 7,
        in_specs=[smem()] + [vmem()] * 9 + [anywhere()] * 5,
        out_specs=(anywhere(), vmem(), vmem()) + (anywhere(),) * 3 + (vmem(),) * 8,
        scratch_shapes=[
            pltpu.VMEM((2, features // 2, features), BF16),
            pltpu.VMEM((2, features, units), BF16),
            pltpu.VMEM((features, units), BF16),
            pltpu.VMEM((rows, features), BF16),
            pltpu.VMEM((rows, features), BF16),
            pltpu.VMEM((CH, rows, width), F32),
            pltpu.VMEM((CH, rows, width), F32),
            pltpu.VMEM((rows, features), F32),
            pltpu.VMEM((rows, features), BF16),
            pltpu.VMEM((rows, units), BF16),
            pltpu.VMEM((rows, 2 * units), BF16),
            pltpu.SemaphoreType.DMA((8,)),
            pltpu.SemaphoreType.DMA((11,)),
        ],
        compiler_params=params(56),
        cost_estimate=cost(rows * features * (features + 6 * units), 20 * 2**20),
    )(at, *pieces, *mixed_pieces, gain, half, other, planes, down, cotangent)


def pair_kernel(
    at, a_left, a_right, b_left, b_right, give_a, give_b, keep, held, *, a_rolled, b_rolled
):
    x, core = at[0], at[1]
    y = pl.program_id(0)
    wide = keep.shape[2] * 8
    turned = lax.rem(y + CH - x, CH)
    cut = a_right.shape[1]
    for left, right, rolled, base in (
        (a_left, a_right, a_rolled, 0),
        (b_left, b_right, b_rolled, cut),
    ):
        where = turned if rolled else y
        block = left[:, pl.ds(pl.multiple_of(where * wide, wide), wide)]
        columns = right.shape[1]
        step = columns // 3 if columns % 384 == 0 else columns
        for first in range(0, columns, step):
            held[:, base + first : base + first + step] = dot_tn(
                block, right[:, first : first + step]
            )
    for z in range(4):
        mine = pl.multiple_of((2 * z + core) * 32, 32)
        theirs = pl.multiple_of((2 * z + 1 - core) * 32, 32)
        keep[z, 0] = held[pl.ds(mine, 32), :].astype(BF16)
        (give_a, give_b)[z // 2][z % 2, 0] = held[pl.ds(theirs, 32), :].astype(BF16)


def pair_products(at, a_left, a_right, b_left, b_right, a_rolled, b_rolled):
    columns = a_right.shape[1] + b_right.shape[1]
    tokens, features = a_left.shape
    out = shape((4, 4, features // 32, columns), BF16)
    spec = pl.BlockSpec((4, 1, features // 32, columns), lambda y: (0, y, 0, 0))
    half = shape((2, 4, features // 32, columns), BF16)
    half_spec = pl.BlockSpec((2, 1, features // 32, columns), lambda y: (0, y, 0, 0))

    def body(*refs):
        pair_kernel(*refs, a_rolled=a_rolled, b_rolled=b_rolled)

    return pl.pallas_call(
        body,
        grid=(4,),
        out_shape=(half, half, out),
        in_specs=[smem()] + [vmem()] * 4,
        out_specs=(half_spec, half_spec, spec),
        scratch_shapes=[pltpu.VMEM((features // 4, columns), F32)],
        compiler_params=params(56),
        cost_estimate=cost(tokens * features * columns, 4 * features * columns),
    )(at, a_left, a_right, b_left, b_right)


def swap_cores(halves):
    return [lax.ppermute(half, "seq", seq_pairs(0, 0, 1)) for half in halves]


def add_kernel(keep, got_a, got_b, out):
    out[:2] = (keep[:2].astype(F32) + got_a[...].astype(F32)).astype(BF16)
    out[2:] = (keep[2:].astype(F32) + got_b[...].astype(F32)).astype(BF16)


def add_cores(keep, got):
    spec = pl.BlockSpec((4, 1) + keep.shape[2:], lambda y: (0, y, 0, 0))
    half = pl.BlockSpec((2, 1) + keep.shape[2:], lambda y: (0, y, 0, 0))
    return pl.pallas_call(
        add_kernel,
        grid=(4,),
        out_shape=shape(keep.shape, BF16),
        in_specs=[spec, half, half],
        out_specs=spec,
        compiler_params=params(56),
        cost_estimate=cost(2**20, 6 * keep.size),
    )(keep, *got)


def spread(small):
    high = small.astype(BF16)
    low = (small - high.astype(F32)).astype(BF16)
    return high, low


def join(message, width):
    return message[:8, :width].astype(F32) + message[:8, width : 2 * width].astype(F32)


def send_kernel(at, keep, got_a, got_b, small_own, small_got, own, m1, m2, m3, small):
    z = at[3]
    rows = own.shape[0]
    width = small.shape[1]
    for j, out in enumerate((own, m1, m2, m3)):
        block = lax.rem(z + j, 4)
        inside = lax.rem(block, 2)
        got = jnp.where(block < 2, got_a[inside].astype(F32), got_b[inside].astype(F32))
        total = keep[block].astype(F32) + got
        out[:rows] = total.reshape(own.shape).astype(out.dtype)
    sums = small_own[...] + small_got[...]
    small[...] = sums
    high, low = spread(jnp.concatenate([sums, jnp.zeros_like(sums)], axis=0))
    for out in (m1, m2, m3):
        out[rows:, :width] = high
        out[rows:, width : 2 * width] = low


def send_z(at, keep, got, small, small_got):
    rows, columns = keep.shape[1] * keep.shape[2], keep.shape[3]
    message = shape((rows + 16, columns), BF16)
    return pl.pallas_call(
        send_kernel,
        out_shape=(
            shape((rows, columns), F32),
            message,
            message,
            message,
            shape(small.shape, F32),
        ),
        in_specs=[smem()] + [vmem()] * 5,
        out_specs=(vmem(),) * 5,
        compiler_params=params(56),
        cost_estimate=cost(2**20, 2**22),
    )(at, keep, *got, small, small_got)


def turn_kernel(at, own, m1, m2, m3, small, left, n1, n2, n3, small_out, total):
    y = at[4]
    rows = own.shape[0]
    width = small.shape[1]
    total[...] = own[...]
    small_sum = small[...]
    for m in (m1, m2, m3):
        total[...] += m[:rows].astype(F32)
        small_sum = small_sum + join(m[rows:], width)
    small_out[...] = small_sum
    part = rows // 4
    for j, out in enumerate((left, n1, n2, n3)):
        block = pl.multiple_of(lax.rem(y + j, 4) * part, part)
        out[:part] = total[pl.ds(block, part)].astype(out.dtype)
    high, low = spread(jnp.concatenate([small_sum, jnp.zeros_like(small_sum)], axis=0))
    for out in (n1, n2, n3):
        out[part:, :width] = high
        out[part:, width : 2 * width] = low


def turn(at, own, messages, small):
    rows, columns = own.shape
    message = shape((rows // 4 + 16, columns), BF16)
    return pl.pallas_call(
        turn_kernel,
        out_shape=(
            shape((rows // 4, columns), F32),
            message,
            message,
            message,
            shape(small.shape, F32),
        ),
        in_specs=[smem()] + [vmem()] * 5,
        out_specs=(vmem(),) * 5,
        scratch_shapes=[pltpu.VMEM((rows, columns), F32)],
        compiler_params=params(56),
        cost_estimate=cost(2**20, 2**21),
    )(at, own, *messages, small)


def last_kernel(own, m1, m2, m3, small, in_out, out_out, conv_out, gain_one, gain_two):
    rows = own.shape[0]
    width = small.shape[1]
    total = own[...]
    small_sum = small[...]
    for m in (m1, m2, m3):
        total = total + m[:rows].astype(F32)
        small_sum = small_sum + join(m[rows:], width)
    for k in range(3):
        in_out[k] = total[:, k * width : (k + 1) * width]
    out_out[...] = total[:, 3 * width :]
    conv_out[...] = small_sum[:3]
    gain_one[...] = small_sum[3:4]
    gain_two[...] = small_sum[4:5]


def last(own, messages, small):
    rows, columns = own.shape
    width = small.shape[1]
    return pl.pallas_call(
        last_kernel,
        out_shape=(
            shape((3, rows, width), F32),
            shape((rows, columns - 3 * width), F32),
            shape((3, width), F32),
            shape((1, width), F32),
            shape((1, width), F32),
        ),
        in_specs=[vmem()] * 5,
        out_specs=(vmem(),) * 5,
        compiler_params=params(56),
        cost_estimate=cost(2**20, 2**20),
    )(own, *messages, small)


def end_kernel(
    d_own, d1, d2, d3, inner, d_hidden, rows_in, rms, gain, conv_grad, gain_two, grad, small
):
    rows, width = d_own.shape
    total = d_own[...]
    line = inner[...]
    for d in (d1, d2, d3):
        total = total + d[:rows].astype(F32)
        high = [d[rows + 16 * i : rows + 16 * (i + 1)].astype(F32) for i in range(4)]
        line = line + jnp.concatenate(
            [high[0] + high[2], high[1] + high[3]], axis=1
        )
    column = lax.dot_general(
        line, jnp.full((16, width), 1.0 / 16, F32), (((0,), (0,)), ((), ())),
        precision=lax.Precision.HIGHEST, preferred_element_type=F32,
    )
    r = rms[...]
    xs = rows_in[...].astype(F32)
    small[0:3] = conv_grad[...]
    small[3:4] = jnp.sum(total * xs * r, axis=0, keepdims=True)
    small[4:5] = gain_two[...]
    small[5:8] = jnp.zeros((3, width), F32)
    grad[...] = (
        d_hidden[...] + r * gain[...] * total - xs * (r * r * r / (CH * width)) * column
    ).astype(BF16)


def end(d_own, received, inner, d_hidden, rows_in, rms, gain, conv_grad, gain_two):
    rows, width = d_own.shape
    return pl.pallas_call(
        end_kernel,
        out_shape=(shape((rows, width), BF16), shape((8, width), F32)),
        in_specs=[vmem()] * 11,
        out_specs=(vmem(),) * 2,
        compiler_params=params(56),
        cost_estimate=cost(2**32, 2**21),
    )(d_own, *received, inner, d_hidden, rows_in, rms, gain[None], conv_grad, gain_two)


def norm_kernel(d_own, d1, d2, d3, h, rms, gain, cotangent, u, u_low, gain_grad):
    total = d_own[...]
    for d in (d1, d2, d3):
        total = total + d[...].astype(F32)
    r = rms[...]
    gain_grad[...] = jnp.sum(total * h[...] * r, axis=0, keepdims=True)
    full = cotangent[...].astype(F32) + r * gain[...] * total
    u[...] = full
    u_low[...] = full.astype(BF16)


def norm_back(d_own, received, h, rms, gain, cotangent):
    rows, width = d_own.shape
    return pl.pallas_call(
        norm_kernel,
        out_shape=(
            shape((rows, width), F32),
            shape((rows, width), BF16),
            shape((1, width), F32),
        ),
        in_specs=[vmem()] * 8,
        out_specs=(vmem(),) * 3,
        compiler_params=params(56),
        cost_estimate=cost(LONG, 2**21),
    )(d_own, *received, h, rms, gain[None], cotangent)


def mid_kernel(
    at, u_own, u1, u2, u3, h, rms, cotangent, weight, c_gate, conv_out,
    d_branch, d_hidden, d_conv, d_cgate, edge,
):
    x = at[0]
    width = u_own.shape[1]
    dot = jnp.zeros((u_own.shape[0], 1), F32)
    us = (u_own, u1, u2, u3)
    for j, u in enumerate(us):
        g = cotangent[:, rel_rows(x, j, width)].astype(F32)
        hj = h[:, j * width : (j + 1) * width]
        dot = dot + jnp.sum((u[...].astype(F32) - g) * hj, axis=1, keepdims=True)
    r = rms[...]
    scale = dot * (r * r / (CH * width))
    d_mixed = jnp.zeros(u_own.shape, F32)
    for j, u in enumerate(us):
        columns = slice(j * width, (j + 1) * width)
        full = u[...].astype(F32) - h[:, columns] * scale
        if j == 0:
            d_hidden[...] = full
        rounded = full.astype(BF16)
        d_branch[:, columns] = rounded
        d_mixed = d_mixed + dot_nn(rounded, weight[rel_rows(x, j, width), :])
    product = d_mixed * c_gate[...]
    d_conv[...] = product
    edge[...] = product[:8]
    d_cgate[...] = (d_mixed * conv_out[...]).astype(BF16)


def mid(at, pieces, h, rms, cotangent, weight, c_gate, conv_out):
    rows, width = c_gate.shape
    wide = shape((rows, width), F32)
    return pl.pallas_call(
        mid_kernel,
        out_shape=(
            shape((rows, CH * width), BF16),
            wide,
            wide,
            shape((rows, width), BF16),
            shape((8, width), F32),
        ),
        in_specs=[smem()] + [vmem()] * 10,
        out_specs=(vmem(),) * 5,
        compiler_params=params(56),
        cost_estimate=cost(rows * CH * width * width, 6 * 2**20),
    )(at, *pieces, h, rms, cotangent, weight, c_gate, conv_out)


def back_kernel(
    at, p0, p1, p2, p3, d_conv, following, taps, value, b_gate, d_cgate, gain, weight,
    grads, d_own, d1, d2, d3, inner, held, sem,
):
    x, count = at[0], at[2]
    rows, width = p0.shape
    copies = [
        pltpu.make_async_copy(
            weight.at[:, rel_rows(x, j, width), :],
            held.at[:, pl.ds(j * width, width), :],
            sem.at[j],
        )
        for j in range(CH)
    ]
    for copy in copies:
        copy.start()
    token = lax.broadcasted_iota(jnp.int32, (rows, width), 0)
    d = d_conv[...]
    next_one, next_two = following[0:1, :], following[1:2, :]
    after_one = jnp.where(token + 1 == count, 0.0, pltpu.roll(d, rows - 1, 0))
    after_one = jnp.where(token == rows - 1, next_one, after_one)
    after_two = pltpu.roll(d, rows - 2, 0)
    after_two = jnp.where((token + 2 == count) | (token + 1 == count), 0.0, after_two)
    after_two = jnp.where(token == rows - 2, next_one, after_two)
    after_two = jnp.where(token == rows - 1, next_two, after_two)
    d_gated = taps[0:1, :] * d + taps[1:2, :] * after_one + taps[2:3, :] * after_two
    grads[:, :width] = (d_gated * value[...]).astype(BF16)
    grads[:, width : 2 * width] = d_cgate[...]
    grads[:, 2 * width :] = (d_gated * b_gate[...]).astype(BF16)
    total = jnp.zeros((rows, width), F32)
    for j, piece in enumerate((p0, p1, p2, p3)):
        copies[j].wait()
        block = slice(j * width, (j + 1) * width)
        term = dot_nt(grads[:, :width], held[0, block, :])
        for k in (1, 2):
            term = term + dot_nt(grads[:, k * width : (k + 1) * width], held[k, block, :])
        scale = gain[:, rel_rows(x, j, width)]
        total = total + scale * term * piece[...].astype(F32)
        if j == 0:
            d_own[...] = term
        else:
            (d1, d2, d3)[j - 1][:rows, :] = term.astype(BF16)
    ones = jnp.ones((16, width), F32)
    row = lax.dot_general(
        ones, total, (((1,), (1,)), ((), ())),
        precision=lax.Precision.HIGHEST, preferred_element_type=F32,
    )
    inner[...] = row
    high = row.astype(BF16)
    low = (row - high.astype(F32)).astype(BF16)
    for out in (d1, d2, d3):
        out[rows : rows + 16, :] = high[:, :width]
        out[rows + 16 : rows + 32, :] = high[:, width:]
        out[rows + 32 : rows + 48, :] = low[:, :width]
        out[rows + 48 : rows + 64, :] = low[:, width:]


def back_project(at, pieces, d_conv, following, taps, value, b_gate, d_cgate, gain, weight):
    rows, width = pieces[0].shape
    features = CH * width
    block = shape((rows + 64, width), BF16)
    return pl.pallas_call(
        back_kernel,
        out_shape=(
            shape((rows, 3 * width), BF16),
            shape((rows, width), F32),
            block,
            block,
            block,
            shape((16, rows), F32),
        ),
        in_specs=[smem()] + [vmem()] * 11 + [anywhere()],
        out_specs=(vmem(),) * 6,
        scratch_shapes=[
            pltpu.VMEM((3, features, width), BF16),
            pltpu.SemaphoreType.DMA((CH,)),
        ],
        compiler_params=params(56),
        cost_estimate=cost(rows * features * 3 * width, 6 * 2**20),
    )(at, *pieces, d_conv, following, taps, value, b_gate, d_cgate, gain[None], weight)


def scatter_groups(array, groups):
    return lax.psum_scatter(array, "seq", scatter_dimension=0, axis_index_groups=groups)


def shards(
    block_input,
    segment_ids,
    norm1_gain,
    in_weight,
    conv_weight,
    out_weight,
    norm2_gain,
    ffn_in_weight,
    ffn_out_weight,
    out_grad,
):
    x = lax.axis_index("ch")
    seq = lax.axis_index("seq")
    core, z, y = seq % 2, (seq // 2) % 4, seq // 8
    features = norm1_gain.shape[0]
    width = block_input.shape[1]
    hidden_units = ffn_out_weight.shape[1]

    def rolled(array):
        blocks = array.reshape((CH, width) + array.shape[1:])
        return jnp.concatenate([pick(blocks, (x + j) % CH, 0) for j in range(CH)], axis=0)

    count = first_count(segment_ids)
    at = jnp.stack([x, core, count, z, y]).astype(jnp.int32)
    own_one = pick(norm1_gain.reshape(CH, width), x, 0)
    own_two = pick(norm2_gain.reshape(CH, width), x, 0)
    in_planes = jnp.transpose(in_weight, (1, 0, 2))

    pieces = gather_ch(block_input)
    half_rows = out_weight.shape[0] // 2
    half = lax.dynamic_slice_in_dim(out_weight, core * half_rows, half_rows, 0)
    half_pieces = gather_ch(half)
    grad_full = lax.all_gather(out_grad, "ch", axis=1, tiled=True)

    normed_one, r_one, b_gate, c_gate, value_rows, gated_rows, edge = in_project(
        at, pieces, norm1_gain, in_planes
    )
    carried = from_behind(edge, "seq", 1)
    mixed_rows, conv_out, current, prior_one, prior_two = convolve(
        at, gated_rows, carried, c_gate, conv_weight
    )

    mixed_pieces = gather_ch(mixed_rows)
    *half_pieces, ffn_weight, _ = tie(*half_pieces, ffn_in_weight, mixed_rows)
    ffn_planes = jnp.transpose(ffn_weight, (1, 0, 2))
    half_full = join_columns(half_pieces, 2**20)
    gain_row = copy_row(tie(norm2_gain, mixed_rows)[0][None])
    ffn_planes, gain_row = tie(ffn_planes, gain_row)
    other_half = lax.ppermute(half_full, "seq", seq_pairs(0, 0, 1))
    (
        hidden,
        hidden_own,
        r_two,
        normed_two,
        act_rows,
        d_gate_up,
        d_own,
        d_one,
        d_two,
        d_three,
        *down_parts,
    ) = ffn(
        at,
        pieces,
        mixed_pieces,
        gain_row,
        half_full,
        other_half,
        ffn_planes,
        ffn_out_weight,
        grad_full,
    )
    received = [
        lax.ppermute(d, "ch", ch_pairs(j)) for j, d in ((2, d_two), (1, d_one), (3, d_three))
    ]
    *gives, keep = pair_products(at, normed_two, d_gate_up, grad_full, act_rows, True, False)
    got = swap_cores(gives)

    u_own, u_low, grad_gain_two = norm_back(
        d_own, received, hidden_own, r_two, own_two, out_grad
    )
    u_pieces = [u_own] + gather_ch(u_low)[1:]
    ffn_kept = add_cores(keep, got)
    ffn_kept, *u_pieces = tie(ffn_kept, *u_pieces)
    groups = [[seq_index(i, k, c) for k in range(4)] for i in range(4) for c in range(2)]
    ffn_sum = scatter_groups(ffn_kept, groups)

    d_branch, d_hidden, d_conv, d_cgate, edge = mid(
        at, u_pieces, hidden, r_two, grad_full, out_weight, c_gate, conv_out
    )
    following = from_behind(edge, "seq", -1)
    d_proj, d_own, d_one, d_two, d_three, inner = back_project(
        at, pieces, d_conv, following, conv_weight, value_rows, b_gate, d_cgate, norm1_gain,
        in_planes,
    )
    received = [lax.ppermute(d, "ch", ch_pairs(j)) for j, d in ((2, d_two), (1, d_one), (3, d_three))]

    *gives, keep = pair_products(at, normed_one, d_proj, d_branch, mixed_rows, True, True)
    got = swap_cores(gives)
    grad_conv = jnp.stack(
        [
            jnp.sum(d_conv * current.astype(F32), axis=0),
            jnp.sum(d_conv * prior_one.astype(F32), axis=0),
            jnp.sum(d_conv * prior_two.astype(F32), axis=0),
        ],
        axis=0,
    )
    input_grad, small = end(
        d_own, received, inner, d_hidden, block_input, r_one, own_one, grad_conv, grad_gain_two
    )
    small_got = lax.ppermute(small, "seq", seq_pairs(0, 0, 1))
    own, *messages, small = send_z(at, keep, got, small, small_got)
    own, ffn_sum, *down_parts = tie(own, ffn_sum, *down_parts)
    messages = [
        lax.ppermute(m, "seq", seq_pairs(0, j, 0)) for j, m in ((2, messages[1]), (1, messages[0]), (3, messages[2]))
    ]
    downs = [lax.ppermute(down_parts[j], "ch", ch_pairs(j)) for j in (2, 1, 3)]
    own, *messages, small = turn(at, own, messages, small)
    downs, messages = lax.optimization_barrier((downs, messages))
    block_output = hidden_own + down_parts[0].astype(F32)
    for down in downs:
        block_output = block_output + down.astype(F32)
    block_output = block_output.astype(BF16)
    messages = [
        lax.ppermute(m, "seq", seq_pairs(j, 0, 0)) for j, m in ((2, messages[1]), (1, messages[0]), (3, messages[2]))
    ]
    groups = [[seq_index(k, i, c) for k in range(4)] for i in range(4) for c in range(2)]
    ffn_sum = scatter_groups(ffn_sum, groups).astype(F32)
    grad_ffn_in = ffn_sum[:, : 2 * hidden_units].reshape(-1, 2, hidden_units)
    grad_ffn_out = ffn_sum[:, 2 * hidden_units :]
    grad_ffn_in, grad_ffn_out, *messages = tie(grad_ffn_in, grad_ffn_out, *messages)
    grad_in, grad_out, grad_conv, grad_gain_one, grad_gain_two = last(own, messages, small)
    return (
        block_output,
        input_grad,
        grad_gain_one.reshape(-1),
        jnp.transpose(grad_in, (1, 0, 2)),
        grad_conv,
        grad_out,
        grad_gain_two.reshape(-1),
        grad_ffn_in,
        grad_ffn_out,
    )


def solution(mesh):
    return jax.shard_map(
        shards,
        mesh=mesh,
        in_specs=(
            P("seq", "ch"),
            P("seq"),
            P(),
            P(None, None, "ch"),
            P(None, "ch"),
            P(None, "ch"),
            P(),
            P(None, None, "ch"),
            P(None, "ch"),
            P("seq", "ch"),
        ),
        out_specs=(
            P("seq", "ch"),
            P("seq", "ch"),
            P("ch"),
            P("seq", None, "ch"),
            P(None, "ch"),
            P("seq", "ch"),
            P("ch"),
            P("seq", None, "ch"),
            P("seq", "ch"),
        ),
        check_vma=False,
    )
```

```python
import jax
import jax.numpy as jnp
from jax import lax
from jax.experimental import pallas as pl
from jax.experimental.pallas import tpu as pltpu
from jax.sharding import PartitionSpec as P

EPS = 1e-05
F32 = jnp.float32
BF16 = jnp.bfloat16
CH = 4
LONG = 2**36


def seq_index(y, z, core):
    return ((y % 4) * 4 + z % 4) * 2 + core


def seq_pairs(dy, dz, dcore):
    return [
        (seq_index(y, z, core), seq_index(y + dy, z + dz, core ^ dcore))
        for y in range(4)
        for z in range(4)
        for core in range(2)
    ]


def ch_pairs(step):
    return [(i, (i + step) % CH) for i in range(CH)]


def gather_ch(block):
    far = lax.ppermute(block, "ch", ch_pairs(2))
    near = [lax.ppermute(block, "ch", ch_pairs(-j)) for j in (1, 3)]
    return [block, near[0], far, near[1]]


def scatter_ch(chunks):
    total = chunks[0]
    for j in range(1, CH):
        total = total + lax.ppermute(chunks[j], "ch", ch_pairs(j)).astype(F32)
    return total


def sum_ch(vector):
    total = vector
    for j in range(1, CH):
        total = total + lax.ppermute(vector, "ch", ch_pairs(j))
    return total


def pick(array, index, axis):
    return lax.dynamic_index_in_dim(array, index, axis, keepdims=False)


def from_behind(array, axis, by):
    size = lax.axis_size(axis)
    pairs = [(i, i + by) for i in range(size) if 0 <= i + by < size]
    return lax.ppermute(array, axis, pairs)


def first_count(segment_ids):
    return jnp.sum((segment_ids == segment_ids[0]).astype(jnp.int32))


def tie(*arrays):
    return lax.optimization_barrier(arrays)


def reduce_axis(array, axis, me, along_y):
    total = pick(array, me, axis).astype(F32)
    for step in (1, 3, 2):
        pairs = seq_pairs(step, 0, 0) if along_y else seq_pairs(0, step, 0)
        total = total + lax.ppermute(pick(array, (me + step) % 4, axis), "seq", pairs).astype(F32)
    return total


def dot_nt(a, b):
    return lax.dot_general(a, b, (((1,), (1,)), ((), ())), preferred_element_type=F32)


def dot_tn(a, b):
    return lax.dot_general(a, b, (((0,), (0,)), ((), ())), preferred_element_type=F32)


def dot_nn(a, b):
    return lax.dot_general(a, b, (((1,), (0,)), ((), ())), preferred_element_type=F32)


def rel_rows(x, j, width):
    return pl.ds(pl.multiple_of(lax.rem(x + j, CH) * width, width), width)


def vmem():
    return pl.BlockSpec(memory_space=pltpu.VMEM)


def smem():
    return pl.BlockSpec(memory_space=pltpu.SMEM)


def anywhere():
    return pl.BlockSpec(memory_space=pl.ANY)


def shape(dims, dtype):
    return jax.ShapeDtypeStruct(dims, dtype)


def params(megabytes):
    return pltpu.CompilerParams(vmem_limit_bytes=megabytes * 1024 * 1024)


def cost(macs, nbytes):
    return pl.CostEstimate(flops=2 * macs, bytes_accessed=nbytes, transcendentals=0)


def in_kernel(at, p0, p1, p2, p3, gain, weight, normed, rms, b_out, c_out, v_out, gated, edge, held, sem):
    x = at[0]
    width = p0.shape[1]
    copies = [
        pltpu.make_async_copy(
            weight.at[:, rel_rows(x, j, width), :],
            held.at[:, pl.ds(j * width, width), :],
            sem.at[j],
        )
        for j in range(CH)
    ]
    for copy in copies:
        copy.start()
    pieces = [p0, p1, p2, p3]
    square = jnp.zeros((p0.shape[0], 1), F32)
    for piece in pieces:
        rows = piece[...].astype(F32)
        square = square + jnp.sum(rows * rows, axis=1, keepdims=True)
    r = lax.rsqrt(square / (CH * width) + EPS)
    rms[...] = r
    for j, piece in enumerate(pieces):
        scale = gain[:, rel_rows(x, j, width)]
        normed[:, j * width : (j + 1) * width] = (piece[...].astype(F32) * r * scale).astype(BF16)
    for copy in copies:
        copy.wait()
    b = dot_nn(normed[...], held[0])
    v = dot_nn(normed[...], held[2])
    b_out[...] = b
    v_out[...] = v
    product = (b * v).astype(BF16)
    gated[...] = product
    rows = product.shape[0]
    token = lax.broadcasted_iota(jnp.int32, (16, width), 0)
    crosses = (token == 14) & (at[2] == rows - 1)
    edge[...] = jnp.where(crosses, 0.0, product[-16:].astype(F32)).astype(BF16)
    c_out[...] = dot_nn(normed[...], held[1])


def in_project(at, pieces, gain, weight):
    rows, width = pieces[0].shape
    features = CH * width
    out = shape((rows, width), F32)
    return pl.pallas_call(
        in_kernel,
        out_shape=(
            shape((rows, features), BF16),
            shape((rows, 1), F32),
            out,
            out,
            out,
            shape((rows, width), BF16),
            shape((16, width), BF16),
        ),
        in_specs=[smem()] + [vmem()] * 5 + [anywhere()],
        out_specs=(vmem(),) * 7,
        scratch_shapes=[
            pltpu.VMEM((3, features, width), BF16),
            pltpu.SemaphoreType.DMA((CH,)),
        ],
        compiler_params=params(56),
        cost_estimate=cost(rows * features * 3 * width, 6 * 2**20),
    )(at, *pieces, gain[None], weight)


def columns_kernel(p0, p1, p2, p3, out):
    width = p0.shape[1]
    for j, piece in enumerate((p0, p1, p2, p3)):
        out[:, j * width : (j + 1) * width] = piece[...]


def join_columns(pieces, weight):
    rows, width = pieces[0].shape
    return pl.pallas_call(
        columns_kernel,
        out_shape=shape((rows, CH * width), BF16),
        in_specs=[vmem()] * CH,
        out_specs=vmem(),
        compiler_params=params(56),
        cost_estimate=cost(weight, 2**21),
    )(*pieces)


def conv_kernel(at, gated, carried, c_gate, taps, mixed, conv_out, one_out, two_out):
    count = at[2]
    rows, width = gated.shape
    token = lax.broadcasted_iota(jnp.int32, (rows, width), 0)
    current = gated[...].astype(F32)
    before = carried[...].astype(F32)
    last, second = before[15:16], before[14:15]
    one = jnp.where(token == 0, last, pltpu.roll(current, 1, 0))
    one = jnp.where(token == count, 0.0, one)
    two = jnp.where(token == 0, second, pltpu.roll(current, 2, 0))
    two = jnp.where(token == 1, last, two)
    two = jnp.where((token == count) | (token == count + 1), 0.0, two)
    out = taps[0:1] * current + taps[1:2] * one + taps[2:3] * two
    mixed[...] = (c_gate[...] * out).astype(BF16)
    conv_out[...] = out
    one_out[...] = one.astype(BF16)
    two_out[...] = two.astype(BF16)


def convolve(at, gated, carried, c_gate, taps):
    rows, width = gated.shape
    low = shape((rows, width), BF16)
    mixed, out, one, two = pl.pallas_call(
        conv_kernel,
        out_shape=(low, shape((rows, width), F32), low, low),
        in_specs=[smem()] + [vmem()] * 4,
        out_specs=(vmem(),) * 4,
        compiler_params=params(56),
        cost_estimate=cost(2**22, 2**21),
    )(at, gated, carried, c_gate, taps)
    return mixed, out, gated, one, two


def copy_kernel(row, out):
    out[...] = row[...]


def copy_row(row):
    return pl.pallas_call(
        copy_kernel,
        out_shape=shape(row.shape, F32),
        in_specs=[vmem()],
        out_specs=vmem(),
        compiler_params=params(56),
        cost_estimate=cost(LONG, 2**13),
    )(row)


def ffn_kernel(
    at,
    x0, x1, x2, x3,
    m0, m1, m2, m3,
    gain,
    half,
    other,
    planes,
    down,
    cotangent,
    h_out, h_own, rms, normed_out, act_out, d_out, d_own, d1, d2, d3, f0, f1, f2, f3,
    w_out, w_in, w_down, g_rows, mixed, acc, down_acc, h, normed, act, d_gate_up, sem, out_sem,
):
    x, core = at[0], at[1]
    leaving = []

    def leave(source, target):
        copy = pltpu.make_async_copy(source, target, out_sem.at[len(leaving)])
        copy.start()
        leaving.append(copy)

    width = x0.shape[1]
    units = down.shape[1]
    step = units // 3
    halves = [
        pltpu.make_async_copy(half, w_out.at[0], sem.at[0]),
        pltpu.make_async_copy(other, w_out.at[1], sem.at[1]),
    ]
    planes_in = [
        pltpu.make_async_copy(
            planes.at[:, rel_rows(x, j, width), :],
            w_in.at[:, pl.ds(j * width, width), :],
            sem.at[2 + j],
        )
        for j in range(CH)
    ]
    rest = [
        pltpu.make_async_copy(cotangent, g_rows, sem.at[6]),
        pltpu.make_async_copy(down, w_down, sem.at[7]),
    ]
    for copy in halves + planes_in + rest:
        copy.start()
    for j, piece in enumerate((m0, m1, m2, m3)):
        mixed[:, j * width : (j + 1) * width] = piece[...]
    for copy in halves:
        copy.wait()
    square = jnp.zeros((x0.shape[0], 1), F32)
    for j, piece in enumerate((x0, x1, x2, x3)):
        block = lax.rem(x + j, CH)
        which = lax.rem(block // 2 + core, 2)
        rows = pl.ds(pl.multiple_of(lax.rem(block, 2) * width, width), width)
        hj = piece[...].astype(F32) + dot_nt(mixed[...], w_out[which, rows, :])
        h[:, j * width : (j + 1) * width] = hj
        square = square + jnp.sum(hj * hj, axis=1, keepdims=True)
    r = lax.rsqrt(square / (CH * width) + EPS)
    rms[...] = r
    h_own[...] = h[:, :width]
    for j in range(CH):
        columns = slice(j * width, (j + 1) * width)
        scale = gain[:, rel_rows(x, j, width)]
        normed[:, columns] = (h[:, columns] * r * scale).astype(BF16)
    leave(h, h_out)
    leave(normed, normed_out)
    for copy in planes_in + rest:
        copy.wait()

    for i in range(3):
        f = slice(i * step, (i + 1) * step)
        f_up = slice(units + i * step, units + (i + 1) * step)
        gate = dot_nn(normed[...], w_in[0, :, f])
        up = dot_nn(normed[...], w_in[1, :, f])
        d_act = dot_nn(g_rows[...], w_down[:, f])
        sigma = jax.nn.sigmoid(gate)
        swish = gate * sigma
        active = (swish * up).astype(BF16)
        act[:, f] = active
        for j in range(CH):
            rows = slice(j * width, (j + 1) * width)
            term = dot_nt(active, w_down[rows, f])
            down_acc[j] = term if i == 0 else down_acc[j] + term
        d_gate = (d_act * up * sigma * (1.0 + gate * (1.0 - sigma))).astype(BF16)
        d_up = (d_act * swish).astype(BF16)
        d_gate_up[:, f] = d_gate
        d_gate_up[:, f_up] = d_up
        leave(act.at[:, f], act_out.at[:, f])
        leave(d_gate_up.at[:, f], d_out.at[:, f])
        leave(d_gate_up.at[:, f_up], d_out.at[:, f_up])
        for j in range(CH):
            rows = slice(j * width, (j + 1) * width)
            term = dot_nt(d_gate, w_in[0, rows, f]) + dot_nt(d_up, w_in[1, rows, f])
            acc[j] = term if i == 0 else acc[j] + term
    d_own[...] = acc[0]
    d1[...] = acc[1].astype(BF16)
    d2[...] = acc[2].astype(BF16)
    d3[...] = acc[3].astype(BF16)
    for j, out in enumerate((f0, f1, f2, f3)):
        out[...] = down_acc[lax.rem(x + j, CH)].astype(BF16)
    for copy in leaving:
        copy.wait()


def ffn(at, pieces, mixed_pieces, gain, half, other, planes, down, cotangent):
    rows, width = pieces[0].shape
    features = CH * width
    units = down.shape[1]
    block = shape((rows, width), BF16)
    return pl.pallas_call(
        ffn_kernel,
        out_shape=(
            shape((rows, features), F32),
            shape((rows, width), F32),
            shape((rows, 1), F32),
            shape((rows, features), BF16),
            shape((rows, units), BF16),
            shape((rows, 2 * units), BF16),
            shape((rows, width), F32),
        )
        + (block,) * 7,
        in_specs=[smem()] + [vmem()] * 9 + [anywhere()] * 5,
        out_specs=(anywhere(), vmem(), vmem()) + (anywhere(),) * 3 + (vmem(),) * 8,
        scratch_shapes=[
            pltpu.VMEM((2, features // 2, features), BF16),
            pltpu.VMEM((2, features, units), BF16),
            pltpu.VMEM((features, units), BF16),
            pltpu.VMEM((rows, features), BF16),
            pltpu.VMEM((rows, features), BF16),
            pltpu.VMEM((CH, rows, width), F32),
            pltpu.VMEM((CH, rows, width), F32),
            pltpu.VMEM((rows, features), F32),
            pltpu.VMEM((rows, features), BF16),
            pltpu.VMEM((rows, units), BF16),
            pltpu.VMEM((rows, 2 * units), BF16),
            pltpu.SemaphoreType.DMA((8,)),
            pltpu.SemaphoreType.DMA((11,)),
        ],
        compiler_params=params(56),
        cost_estimate=cost(rows * features * (features + 6 * units), 20 * 2**20),
    )(at, *pieces, *mixed_pieces, gain, half, other, planes, down, cotangent)


def pair_kernel(
    at, a_left, a_right, b_left, b_right, give_a, give_b, keep, held, *, a_rolled, b_rolled
):
    x, core = at[0], at[1]
    y = pl.program_id(0)
    wide = keep.shape[2] * 8
    turned = lax.rem(y + CH - x, CH)
    cut = a_right.shape[1]
    for left, right, rolled, base in (
        (a_left, a_right, a_rolled, 0),
        (b_left, b_right, b_rolled, cut),
    ):
        where = turned if rolled else y
        block = left[:, pl.ds(pl.multiple_of(where * wide, wide), wide)]
        columns = right.shape[1]
        step = columns // 3 if columns % 384 == 0 else columns
        for first in range(0, columns, step):
            held[:, base + first : base + first + step] = dot_tn(
                block, right[:, first : first + step]
            )
    for z in range(4):
        mine = pl.multiple_of((2 * z + core) * 32, 32)
        theirs = pl.multiple_of((2 * z + 1 - core) * 32, 32)
        keep[z, 0] = held[pl.ds(mine, 32), :].astype(BF16)
        (give_a, give_b)[z // 2][z % 2, 0] = held[pl.ds(theirs, 32), :].astype(BF16)


def pair_products(at, a_left, a_right, b_left, b_right, a_rolled, b_rolled):
    columns = a_right.shape[1] + b_right.shape[1]
    tokens, features = a_left.shape
    out = shape((4, 4, features // 32, columns), BF16)
    spec = pl.BlockSpec((4, 1, features // 32, columns), lambda y: (0, y, 0, 0))
    half = shape((2, 4, features // 32, columns), BF16)
    half_spec = pl.BlockSpec((2, 1, features // 32, columns), lambda y: (0, y, 0, 0))

    def body(*refs):
        pair_kernel(*refs, a_rolled=a_rolled, b_rolled=b_rolled)

    return pl.pallas_call(
        body,
        grid=(4,),
        out_shape=(half, half, out),
        in_specs=[smem()] + [vmem()] * 4,
        out_specs=(half_spec, half_spec, spec),
        scratch_shapes=[pltpu.VMEM((features // 4, columns), F32)],
        compiler_params=params(56),
        cost_estimate=cost(tokens * features * columns, 4 * features * columns),
    )(at, a_left, a_right, b_left, b_right)


def swap_cores(halves):
    return [lax.ppermute(half, "seq", seq_pairs(0, 0, 1)) for half in halves]


def add_kernel(keep, got_a, got_b, out):
    out[:2] = (keep[:2].astype(F32) + got_a[...].astype(F32)).astype(BF16)
    out[2:] = (keep[2:].astype(F32) + got_b[...].astype(F32)).astype(BF16)


def add_cores(keep, got):
    spec = pl.BlockSpec((4, 1) + keep.shape[2:], lambda y: (0, y, 0, 0))
    half = pl.BlockSpec((2, 1) + keep.shape[2:], lambda y: (0, y, 0, 0))
    return pl.pallas_call(
        add_kernel,
        grid=(4,),
        out_shape=shape(keep.shape, BF16),
        in_specs=[spec, half, half],
        out_specs=spec,
        compiler_params=params(56),
        cost_estimate=cost(2**20, 6 * keep.size),
    )(keep, *got)


def spread(small):
    high = small.astype(BF16)
    low = (small - high.astype(F32)).astype(BF16)
    return high, low


def join(message, width):
    return message[:8, :width].astype(F32) + message[:8, width : 2 * width].astype(F32)


def send_kernel(at, keep, got_a, got_b, small_own, small_got, own, m1, m2, m3, small):
    z = at[3]
    rows = own.shape[0]
    width = small.shape[1]
    for j, out in enumerate((own, m1, m2, m3)):
        block = lax.rem(z + j, 4)
        inside = lax.rem(block, 2)
        got = jnp.where(block < 2, got_a[inside].astype(F32), got_b[inside].astype(F32))
        total = keep[block].astype(F32) + got
        out[:rows] = total.reshape(own.shape).astype(out.dtype)
    sums = small_own[...] + small_got[...]
    small[...] = sums
    high, low = spread(jnp.concatenate([sums, jnp.zeros_like(sums)], axis=0))
    for out in (m1, m2, m3):
        out[rows:, :width] = high
        out[rows:, width : 2 * width] = low


def send_z(at, keep, got, small, small_got):
    rows, columns = keep.shape[1] * keep.shape[2], keep.shape[3]
    message = shape((rows + 16, columns), BF16)
    return pl.pallas_call(
        send_kernel,
        out_shape=(
            shape((rows, columns), F32),
            message,
            message,
            message,
            shape(small.shape, F32),
        ),
        in_specs=[smem()] + [vmem()] * 5,
        out_specs=(vmem(),) * 5,
        compiler_params=params(56),
        cost_estimate=cost(2**20, 2**22),
    )(at, keep, *got, small, small_got)


def turn_kernel(at, own, m1, m2, m3, small, left, n1, n2, n3, small_out, total):
    y = at[4]
    rows = own.shape[0]
    width = small.shape[1]
    total[...] = own[...]
    small_sum = small[...]
    for m in (m1, m2, m3):
        total[...] += m[:rows].astype(F32)
        small_sum = small_sum + join(m[rows:], width)
    small_out[...] = small_sum
    part = rows // 4
    for j, out in enumerate((left, n1, n2, n3)):
        block = pl.multiple_of(lax.rem(y + j, 4) * part, part)
        out[:part] = total[pl.ds(block, part)].astype(out.dtype)
    high, low = spread(jnp.concatenate([small_sum, jnp.zeros_like(small_sum)], axis=0))
    for out in (n1, n2, n3):
        out[part:, :width] = high
        out[part:, width : 2 * width] = low


def turn(at, own, messages, small):
    rows, columns = own.shape
    message = shape((rows // 4 + 16, columns), BF16)
    return pl.pallas_call(
        turn_kernel,
        out_shape=(
            shape((rows // 4, columns), F32),
            message,
            message,
            message,
            shape(small.shape, F32),
        ),
        in_specs=[smem()] + [vmem()] * 5,
        out_specs=(vmem(),) * 5,
        scratch_shapes=[pltpu.VMEM((rows, columns), F32)],
        compiler_params=params(56),
        cost_estimate=cost(2**20, 2**21),
    )(at, own, *messages, small)


def last_kernel(own, m1, m2, m3, small, in_out, out_out, conv_out, gain_one, gain_two):
    rows = own.shape[0]
    width = small.shape[1]
    total = own[...]
    small_sum = small[...]
    for m in (m1, m2, m3):
        total = total + m[:rows].astype(F32)
        small_sum = small_sum + join(m[rows:], width)
    for k in range(3):
        in_out[k] = total[:, k * width : (k + 1) * width]
    out_out[...] = total[:, 3 * width :]
    conv_out[...] = small_sum[:3]
    gain_one[...] = small_sum[3:4]
    gain_two[...] = small_sum[4:5]


def last(own, messages, small):
    rows, columns = own.shape
    width = small.shape[1]
    return pl.pallas_call(
        last_kernel,
        out_shape=(
            shape((3, rows, width), F32),
            shape((rows, columns - 3 * width), F32),
            shape((3, width), F32),
            shape((1, width), F32),
            shape((1, width), F32),
        ),
        in_specs=[vmem()] * 5,
        out_specs=(vmem(),) * 5,
        compiler_params=params(56),
        cost_estimate=cost(2**20, 2**20),
    )(own, *messages, small)


def end_kernel(
    d_own, d1, d2, d3, inner, d_hidden, rows_in, rms, gain, conv_grad, gain_two, grad, small
):
    rows, width = d_own.shape
    total = d_own[...]
    line = inner[...]
    for d in (d1, d2, d3):
        total = total + d[:rows].astype(F32)
        high = [d[rows + 16 * i : rows + 16 * (i + 1)].astype(F32) for i in range(4)]
        line = line + jnp.concatenate(
            [high[0] + high[2], high[1] + high[3]], axis=1
        )
    column = lax.dot_general(
        line, jnp.full((16, width), 1.0 / 16, F32), (((0,), (0,)), ((), ())),
        precision=lax.Precision.HIGHEST, preferred_element_type=F32,
    )
    r = rms[...]
    xs = rows_in[...].astype(F32)
    small[0:3] = conv_grad[...]
    small[3:4] = jnp.sum(total * xs * r, axis=0, keepdims=True)
    small[4:5] = gain_two[...]
    small[5:8] = jnp.zeros((3, width), F32)
    grad[...] = (
        d_hidden[...] + r * gain[...] * total - xs * (r * r * r / (CH * width)) * column
    ).astype(BF16)


def end(d_own, received, inner, d_hidden, rows_in, rms, gain, conv_grad, gain_two):
    rows, width = d_own.shape
    return pl.pallas_call(
        end_kernel,
        out_shape=(shape((rows, width), BF16), shape((8, width), F32)),
        in_specs=[vmem()] * 11,
        out_specs=(vmem(),) * 2,
        compiler_params=params(56),
        cost_estimate=cost(2**32, 2**21),
    )(d_own, *received, inner, d_hidden, rows_in, rms, gain[None], conv_grad, gain_two)


def norm_kernel(d_own, d1, d2, d3, h, rms, gain, cotangent, u, u_low, gain_grad):
    total = d_own[...]
    for d in (d1, d2, d3):
        total = total + d[...].astype(F32)
    r = rms[...]
    gain_grad[...] = jnp.sum(total * h[...] * r, axis=0, keepdims=True)
    full = cotangent[...].astype(F32) + r * gain[...] * total
    u[...] = full
    u_low[...] = full.astype(BF16)


def norm_back(d_own, received, h, rms, gain, cotangent):
    rows, width = d_own.shape
    return pl.pallas_call(
        norm_kernel,
        out_shape=(
            shape((rows, width), F32),
            shape((rows, width), BF16),
            shape((1, width), F32),
        ),
        in_specs=[vmem()] * 8,
        out_specs=(vmem(),) * 3,
        compiler_params=params(56),
        cost_estimate=cost(LONG, 2**21),
    )(d_own, *received, h, rms, gain[None], cotangent)


def mid_kernel(
    at, u_own, u1, u2, u3, h, rms, cotangent, weight, c_gate, conv_out,
    d_branch, d_hidden, d_conv, d_cgate, edge,
):
    x = at[0]
    width = u_own.shape[1]
    dot = jnp.zeros((u_own.shape[0], 1), F32)
    us = (u_own, u1, u2, u3)
    for j, u in enumerate(us):
        g = cotangent[:, rel_rows(x, j, width)].astype(F32)
        hj = h[:, j * width : (j + 1) * width]
        dot = dot + jnp.sum((u[...].astype(F32) - g) * hj, axis=1, keepdims=True)
    r = rms[...]
    scale = dot * (r * r / (CH * width))
    d_mixed = jnp.zeros(u_own.shape, F32)
    for j, u in enumerate(us):
        columns = slice(j * width, (j + 1) * width)
        full = u[...].astype(F32) - h[:, columns] * scale
        if j == 0:
            d_hidden[...] = full
        rounded = full.astype(BF16)
        d_branch[:, columns] = rounded
        d_mixed = d_mixed + dot_nn(rounded, weight[rel_rows(x, j, width), :])
    product = d_mixed * c_gate[...]
    d_conv[...] = product
    edge[...] = product[:8]
    d_cgate[...] = (d_mixed * conv_out[...]).astype(BF16)


def mid(at, pieces, h, rms, cotangent, weight, c_gate, conv_out):
    rows, width = c_gate.shape
    wide = shape((rows, width), F32)
    return pl.pallas_call(
        mid_kernel,
        out_shape=(
            shape((rows, CH * width), BF16),
            wide,
            wide,
            shape((rows, width), BF16),
            shape((8, width), F32),
        ),
        in_specs=[smem()] + [vmem()] * 10,
        out_specs=(vmem(),) * 5,
        compiler_params=params(56),
        cost_estimate=cost(rows * CH * width * width, 6 * 2**20),
    )(at, *pieces, h, rms, cotangent, weight, c_gate, conv_out)


def back_kernel(
    at, p0, p1, p2, p3, d_conv, following, taps, value, b_gate, d_cgate, gain, weight,
    grads, d_own, d1, d2, d3, inner, held, sem,
):
    x, count = at[0], at[2]
    rows, width = p0.shape
    copies = [
        pltpu.make_async_copy(
            weight.at[:, rel_rows(x, j, width), :],
            held.at[:, pl.ds(j * width, width), :],
            sem.at[j],
        )
        for j in range(CH)
    ]
    for copy in copies:
        copy.start()
    token = lax.broadcasted_iota(jnp.int32, (rows, width), 0)
    d = d_conv[...]
    next_one, next_two = following[0:1, :], following[1:2, :]
    after_one = jnp.where(token + 1 == count, 0.0, pltpu.roll(d, rows - 1, 0))
    after_one = jnp.where(token == rows - 1, next_one, after_one)
    after_two = pltpu.roll(d, rows - 2, 0)
    after_two = jnp.where((token + 2 == count) | (token + 1 == count), 0.0, after_two)
    after_two = jnp.where(token == rows - 2, jnp.where(count == rows - 1, 0.0, next_one), after_two)
    after_two = jnp.where(token == rows - 1, next_two, after_two)
    d_gated = taps[0:1, :] * d + taps[1:2, :] * after_one + taps[2:3, :] * after_two
    grads[:, :width] = (d_gated * value[...]).astype(BF16)
    grads[:, width : 2 * width] = d_cgate[...]
    grads[:, 2 * width :] = (d_gated * b_gate[...]).astype(BF16)
    total = jnp.zeros((rows, width), F32)
    for j, piece in enumerate((p0, p1, p2, p3)):
        copies[j].wait()
        block = slice(j * width, (j + 1) * width)
        term = dot_nt(grads[:, :width], held[0, block, :])
        for k in (1, 2):
            term = term + dot_nt(grads[:, k * width : (k + 1) * width], held[k, block, :])
        scale = gain[:, rel_rows(x, j, width)]
        total = total + scale * term * piece[...].astype(F32)
        if j == 0:
            d_own[...] = term
        else:
            (d1, d2, d3)[j - 1][:rows, :] = term.astype(BF16)
    ones = jnp.ones((16, width), F32)
    row = lax.dot_general(
        ones, total, (((1,), (1,)), ((), ())),
        precision=lax.Precision.HIGHEST, preferred_element_type=F32,
    )
    inner[...] = row
    high = row.astype(BF16)
    low = (row - high.astype(F32)).astype(BF16)
    for out in (d1, d2, d3):
        out[rows : rows + 16, :] = high[:, :width]
        out[rows + 16 : rows + 32, :] = high[:, width:]
        out[rows + 32 : rows + 48, :] = low[:, :width]
        out[rows + 48 : rows + 64, :] = low[:, width:]


def back_project(at, pieces, d_conv, following, taps, value, b_gate, d_cgate, gain, weight):
    rows, width = pieces[0].shape
    features = CH * width
    block = shape((rows + 64, width), BF16)
    return pl.pallas_call(
        back_kernel,
        out_shape=(
            shape((rows, 3 * width), BF16),
            shape((rows, width), F32),
            block,
            block,
            block,
            shape((16, rows), F32),
        ),
        in_specs=[smem()] + [vmem()] * 11 + [anywhere()],
        out_specs=(vmem(),) * 6,
        scratch_shapes=[
            pltpu.VMEM((3, features, width), BF16),
            pltpu.SemaphoreType.DMA((CH,)),
        ],
        compiler_params=params(56),
        cost_estimate=cost(rows * features * 3 * width, 6 * 2**20),
    )(at, *pieces, d_conv, following, taps, value, b_gate, d_cgate, gain[None], weight)


def scatter_groups(array, groups):
    return lax.psum_scatter(array, "seq", scatter_dimension=0, axis_index_groups=groups)


def shards(
    block_input,
    segment_ids,
    norm1_gain,
    in_weight,
    conv_weight,
    out_weight,
    norm2_gain,
    ffn_in_weight,
    ffn_out_weight,
    out_grad,
):
    x = lax.axis_index("ch")
    seq = lax.axis_index("seq")
    core, z, y = seq % 2, (seq // 2) % 4, seq // 8
    features = norm1_gain.shape[0]
    width = block_input.shape[1]
    hidden_units = ffn_out_weight.shape[1]

    def rolled(array):
        blocks = array.reshape((CH, width) + array.shape[1:])
        return jnp.concatenate([pick(blocks, (x + j) % CH, 0) for j in range(CH)], axis=0)

    count = first_count(segment_ids)
    at = jnp.stack([x, core, count, z, y]).astype(jnp.int32)
    own_one = pick(norm1_gain.reshape(CH, width), x, 0)
    own_two = pick(norm2_gain.reshape(CH, width), x, 0)
    in_planes = jnp.transpose(in_weight, (1, 0, 2))

    pieces = gather_ch(block_input)
    half_rows = out_weight.shape[0] // 2
    half = lax.dynamic_slice_in_dim(out_weight, core * half_rows, half_rows, 0)
    half_pieces = gather_ch(half)
    grad_full = lax.all_gather(out_grad, "ch", axis=1, tiled=True)

    normed_one, r_one, b_gate, c_gate, value_rows, gated_rows, edge = in_project(
        at, pieces, norm1_gain, in_planes
    )
    carried = from_behind(edge, "seq", 1)
    mixed_rows, conv_out, current, prior_one, prior_two = convolve(
        at, gated_rows, carried, c_gate, conv_weight
    )

    mixed_pieces = gather_ch(mixed_rows)
    *half_pieces, ffn_weight, _ = tie(*half_pieces, ffn_in_weight, mixed_rows)
    ffn_planes = jnp.transpose(ffn_weight, (1, 0, 2))
    half_full = join_columns(half_pieces, 2**20)
    gain_row = copy_row(tie(norm2_gain, mixed_rows)[0][None])
    ffn_planes, gain_row = tie(ffn_planes, gain_row)
    other_half = lax.ppermute(half_full, "seq", seq_pairs(0, 0, 1))
    (
        hidden,
        hidden_own,
        r_two,
        normed_two,
        act_rows,
        d_gate_up,
        d_own,
        d_one,
        d_two,
        d_three,
        *down_parts,
    ) = ffn(
        at,
        pieces,
        mixed_pieces,
        gain_row,
        half_full,
        other_half,
        ffn_planes,
        ffn_out_weight,
        grad_full,
    )
    received = [
        lax.ppermute(d, "ch", ch_pairs(j)) for j, d in ((2, d_two), (1, d_one), (3, d_three))
    ]
    *gives, keep = pair_products(at, normed_two, d_gate_up, grad_full, act_rows, True, False)
    got = swap_cores(gives)

    u_own, u_low, grad_gain_two = norm_back(
        d_own, received, hidden_own, r_two, own_two, out_grad
    )
    u_pieces = [u_own] + gather_ch(u_low)[1:]
    ffn_kept = add_cores(keep, got)
    ffn_kept, *u_pieces = tie(ffn_kept, *u_pieces)
    groups = [[seq_index(i, k, c) for k in range(4)] for i in range(4) for c in range(2)]
    ffn_sum = scatter_groups(ffn_kept, groups)

    d_branch, d_hidden, d_conv, d_cgate, edge = mid(
        at, u_pieces, hidden, r_two, grad_full, out_weight, c_gate, conv_out
    )
    following = from_behind(edge, "seq", -1)
    d_proj, d_own, d_one, d_two, d_three, inner = back_project(
        at, pieces, d_conv, following, conv_weight, value_rows, b_gate, d_cgate, norm1_gain,
        in_planes,
    )
    received = [lax.ppermute(d, "ch", ch_pairs(j)) for j, d in ((2, d_two), (1, d_one), (3, d_three))]

    *gives, keep = pair_products(at, normed_one, d_proj, d_branch, mixed_rows, True, True)
    got = swap_cores(gives)
    grad_conv = jnp.stack(
        [
            jnp.sum(d_conv * current.astype(F32), axis=0),
            jnp.sum(d_conv * prior_one.astype(F32), axis=0),
            jnp.sum(d_conv * prior_two.astype(F32), axis=0),
        ],
        axis=0,
    )
    input_grad, small = end(
        d_own, received, inner, d_hidden, block_input, r_one, own_one, grad_conv, grad_gain_two
    )
    small_got = lax.ppermute(small, "seq", seq_pairs(0, 0, 1))
    own, *messages, small = send_z(at, keep, got, small, small_got)
    own, ffn_sum, *down_parts = tie(own, ffn_sum, *down_parts)
    messages = [
        lax.ppermute(m, "seq", seq_pairs(0, j, 0)) for j, m in ((2, messages[1]), (1, messages[0]), (3, messages[2]))
    ]
    downs = [lax.ppermute(down_parts[j], "ch", ch_pairs(j)) for j in (2, 1, 3)]
    own, *messages, small = turn(at, own, messages, small)
    downs, messages = lax.optimization_barrier((downs, messages))
    block_output = hidden_own + down_parts[0].astype(F32)
    for down in downs:
        block_output = block_output + down.astype(F32)
    block_output = block_output.astype(BF16)
    messages = [
        lax.ppermute(m, "seq", seq_pairs(j, 0, 0)) for j, m in ((2, messages[1]), (1, messages[0]), (3, messages[2]))
    ]
    groups = [[seq_index(k, i, c) for k in range(4)] for i in range(4) for c in range(2)]
    ffn_sum = scatter_groups(ffn_sum, groups).astype(F32)
    grad_ffn_in = ffn_sum[:, : 2 * hidden_units].reshape(-1, 2, hidden_units)
    grad_ffn_out = ffn_sum[:, 2 * hidden_units :]
    grad_ffn_in, grad_ffn_out, *messages = tie(grad_ffn_in, grad_ffn_out, *messages)
    grad_in, grad_out, grad_conv, grad_gain_one, grad_gain_two = last(own, messages, small)
    return (
        block_output,
        input_grad,
        grad_gain_one.reshape(-1),
        jnp.transpose(grad_in, (1, 0, 2)),
        grad_conv,
        grad_out,
        grad_gain_two.reshape(-1),
        grad_ffn_in,
        grad_ffn_out,
    )


def solution(mesh):
    return jax.shard_map(
        shards,
        mesh=mesh,
        in_specs=(
            P("seq", "ch"),
            P("seq"),
            P(),
            P(None, None, "ch"),
            P(None, "ch"),
            P(None, "ch"),
            P(),
            P(None, None, "ch"),
            P(None, "ch"),
            P("seq", "ch"),
        ),
        out_specs=(
            P("seq", "ch"),
            P("seq", "ch"),
            P("ch"),
            P("seq", None, "ch"),
            P(None, "ch"),
            P("seq", "ch"),
            P("ch"),
            P("seq", None, "ch"),
            P("seq", "ch"),
        ),
        check_vma=False,
    )
```
